128 devices in a mesh: rounds: 16 (over z_lo, x, core), stab: 8 (over y, z_hi).
Axes of the slice: x: 4, y: 4, z: 4 (z_hi: 2, z_lo: 2; z = z_hi * 2 + z_lo), core: 2. Of those that a mesh axis runs over, the one named last changes fastest.
Arguments:
- syndrome: int32 [128, 1024], P('rounds', 'stab'), may hold values from 0 to 1
- basis_ids: int32 [1024], P('stab'), may hold values from 0 to 1
- coordinates: int32 [2, 1024], P(None, 'stab'), may hold values from 0 to 41
- syndrome_table: bfloat16 [2, 256], replicated, may hold values from -3 to 3
- basis_table: bfloat16 [2, 256], replicated, may hold values from -3 to 3
- coord_table: bfloat16 [2, 42, 256], replicated, may hold values from -3 to 3
- round_table: bfloat16 [128, 256], P('rounds'), may hold values from -3 to 3
- gain_space: float32 [256], replicated, may hold values from 0.1 to 1.9
- w_qkv_space: bfloat16 [256, 768], replicated, may hold values from -20 to 20
- w_out_space: bfloat16 [256, 256], replicated, may hold values from -0.375 to 0.375
- gain_time: float32 [256], replicated, may hold values from 0.1 to 1.9
- w_qkv_time: bfloat16 [256, 768], replicated, may hold values from -20 to 20
- w_out_time: bfloat16 [256, 256], replicated, may hold values from -0.375 to 0.375
- grad_hidden: bfloat16 [128, 1024, 256], P('rounds', 'stab'), may hold values from -6 to 6
Outputs:
- hidden: bfloat16 [128, 1024, 256], P('rounds', 'stab')
- grad_embedded: bfloat16 [128, 1024, 256], P('rounds', 'stab')
- grad_w_qkv_space: float32 [256, 768], replicated
- grad_w_out_space: float32 [256, 256], replicated
- grad_w_qkv_time: float32 [256, 768], replicated
- grad_w_out_time: float32 [256, 256], replicated
The draws below stay inside these ranges and needn't reach their ends.
All inputs are finite; a program needn't handle non-finite values.
Results may differ from the reference program's by a relative error of at most 0.029.
The reference program's roundings to bfloat16 on the way (of `embedded`, `normed`, `packed`, `weights`, `attended`, `grad_attended`, `grad_scores` and `grad_packed`) count: a program that leaves them out, or rounds other values in their place, can miss the bound.
Values may be sent and summed in bfloat16 or wider, within the bound.
No kernel may reach another device: no remote copies, remote signals or barrier semaphores. Data moves between devices by JAX's collectives and lax.ppermute only.
A program may use at most 128 MiB of HBM per device.

```python
import math
import jax
import jax.numpy as jnp
from jax import lax

D = 256
HEADS = 4
COORDS = 42
STABS = 1024
ROUNDS = 128
TOKENS = 131072


def draw_w_qkv_space(key, part):
    key = jax.random.fold_in(key, 11)
    query_key, other_key, value_key = jax.random.split(key, 3)
    spread = 1.5 / math.sqrt(D)
    query_part = jnp.clip(jax.random.normal(query_key, (D, D), jnp.float32), -6.0, 6.0) * spread
    value_part = jnp.clip(jax.random.normal(value_key, (D, D), jnp.float32), -6.0, 6.0) * (1.0 / math.sqrt(D))
    key_part = jnp.clip(jax.random.normal(other_key, (D, D), jnp.float32), -6.0, 6.0) * spread
    return jnp.concatenate([query_part, key_part, value_part], axis=1).astype(jnp.bfloat16)


def draw_w_qkv_time(key, part):
    key = jax.random.fold_in(key, 12)
    query_key, other_key, value_key = jax.random.split(key, 3)
    spread = 1.5 / math.sqrt(D)
    query_part = jnp.clip(jax.random.normal(query_key, (D, D), jnp.float32), -6.0, 6.0) * spread
    value_part = jnp.clip(jax.random.normal(value_key, (D, D), jnp.float32), -6.0, 6.0) * (1.0 / math.sqrt(D))
    key_part = jnp.clip(jax.random.normal(other_key, (D, D), jnp.float32), -6.0, 6.0) * spread
    return jnp.concatenate([query_part, key_part, value_part], axis=1).astype(jnp.bfloat16)


def place_ends(array, key, low, high):
    dims = array.shape
    place = [jax.random.randint(jax.random.fold_in(key, axis), (), 0, dims[axis]) for axis in range(len(dims))]
    array = array.at[tuple(place)].set(low)
    longest = dims.index(max(dims))
    place[longest] = (place[longest] + 1) % dims[longest]
    return array.at[tuple(place)].set(high)


def shard_levels(key, extent, cuts, smallest, largest):
    loudness, own = 1.0, jax.random.fold_in(key, 6)
    for axis_at, shards_of in cuts:
        heights = jnp.exp(jax.random.uniform(jax.random.fold_in(own, axis_at), (shards_of,), jnp.float32, smallest / len(cuts), largest / len(cuts)))
        loudness = loudness * jnp.repeat(heights, extent[axis_at] // shards_of).reshape([-1 if axis == axis_at else 1 for axis in range(len(extent))])
    return loudness


def normal_values(own_key, shape, scale, limit, cuts=(), kind=jnp.bfloat16):
    loudness = shard_levels(own_key, shape, cuts, -0.22, 0.18) if cuts else 1.0
    array = jax.random.normal(own_key, shape, jnp.float32) * scale * loudness
    return jnp.minimum(jnp.maximum(array, -limit), limit).astype(kind)


def setup_inputs(seed: int = 0) -> dict:
    splits = jax.random.split(jax.random.key(seed), 15)
    syndrome = place_ends(jax.random.randint(splits[0], (ROUNDS, STABS), 0, 2), jax.random.fold_in(splits[0], 1), 0, 1).astype(jnp.int32)
    basis_ids = place_ends(jax.random.randint(splits[1], (STABS,), 0, 2), jax.random.fold_in(splits[1], 1), 0, 1).astype(jnp.int32)
    coordinates = place_ends(jax.random.randint(splits[2], (2, STABS), 0, COORDS), jax.random.fold_in(splits[2], 1), 0, COORDS - 1).astype(jnp.int32)
    syndrome_table = normal_values(splits[3], (2, D), 0.5, 3.0)
    basis_table = normal_values(splits[4], (2, D), 0.5, 3.0)
    coord_table = normal_values(splits[5], (2, COORDS, D), 0.5, 3.0)
    round_table = normal_values(splits[6], (ROUNDS, D), 0.5, 3.0, ((0, 16),))
    gain_space = jnp.clip(1.0 + 0.18 * jax.random.normal(splits[7], (D,), jnp.float32), 0.1, 1.9)
    w_qkv_space = draw_w_qkv_space(jax.random.fold_in(splits[14], 71), 0)
    w_out_space = normal_values(splits[9], (D, D), D ** -0.5, 0.375)
    gain_time = jnp.clip(1.0 + 0.18 * jax.random.normal(splits[10], (D,), jnp.float32), 0.1, 1.9)
    w_qkv_time = draw_w_qkv_time(jax.random.fold_in(splits[14], 71), 0)
    w_out_time = normal_values(splits[12], (D, D), D ** -0.5, 0.375)
    grad_hidden = normal_values(splits[13], (ROUNDS, STABS, D), 1.0, 6.0, ((0, 16), (1, 8)))
    return {"syndrome": syndrome, "basis_ids": basis_ids, "coordinates": coordinates, "syndrome_table": syndrome_table, "basis_table": basis_table, "coord_table": coord_table, "round_table": round_table, "gain_space": gain_space, "w_qkv_space": w_qkv_space, "w_out_space": w_out_space, "gain_time": gain_time, "w_qkv_time": w_qkv_time, "w_out_time": w_out_time, "grad_hidden": grad_hidden}


EPSILON = 1e-06
SPACE_FORMS = ('bqhe,bkhe->bhqk', 'bhqk,bkhe->bqhe', 'bhqk,bqhe->bkhe')
TIME_FORMS = ('qbhe,kbhe->bhqk', 'bhqk,kbhe->qbhe', 'bhqk,qbhe->kbhe')

def contract(form, left, right):
    return jnp.einsum(form, left.astype(jnp.float32), right.astype(jnp.float32))

def split_heads(values, head_count):
    return values.reshape(values.shape[:-1] + (head_count, values.shape[-1] // head_count))

def merge_heads(values):
    return values.reshape(values.shape[:-2] + (values.shape[-2] * values.shape[-1],))

def embed_tokens(syndrome, basis_ids, coordinates, syndrome_table, basis_table, coord_table, round_table):
    levels = jnp.arange(coord_table.shape[1], dtype=jnp.int32)
    row_onehot = (coordinates[0][:, None] == levels[None, :]).astype(jnp.bfloat16)
    col_onehot = (coordinates[1][:, None] == levels[None, :]).astype(jnp.bfloat16)
    stab_part = jnp.dot(row_onehot, coord_table[0], preferred_element_type=jnp.float32)
    stab_part = stab_part + jnp.dot(col_onehot, coord_table[1], preferred_element_type=jnp.float32)
    basis_part = jnp.where(basis_ids[:, None] == 1, basis_table[1][None, :], basis_table[0][None, :]).astype(jnp.float32)
    syndrome_part = jnp.where(syndrome[:, :, None] == 1, syndrome_table[1][None, None, :], syndrome_table[0][None, None, :]).astype(jnp.float32)
    summed = syndrome_part + (stab_part + basis_part)[None, :, :] + round_table.astype(jnp.float32)[:, None, :]
    return summed.astype(jnp.bfloat16)

def rms_forward(stream, gain):
    values = stream.astype(jnp.float32)
    inverse = lax.rsqrt(lax.optimization_barrier(jnp.mean(values * values, axis=-1, keepdims=True)) + EPSILON)
    return ((values * inverse * gain).astype(jnp.bfloat16), inverse)

def rms_backward(stream, gain, inverse, grad_normed):
    values = stream.astype(jnp.float32)
    gained = grad_normed * gain
    inner = lax.optimization_barrier(jnp.mean(gained * values, axis=-1, keepdims=True))
    return inverse * gained - values * (inverse * inverse * inverse) * inner

def project(stream, gain, w_qkv):
    normed, inverse = rms_forward(stream, gain)
    packed = jnp.dot(normed, w_qkv, preferred_element_type=jnp.float32).astype(jnp.bfloat16)
    width = stream.shape[-1]
    return (normed, inverse, packed[..., :width], packed[..., width:2 * width], packed[..., 2 * width:])

def add_branch(stream, attended, w_out):
    branch = jnp.dot(attended, w_out, preferred_element_type=jnp.float32)
    return (stream.astype(jnp.float32) + branch).astype(jnp.bfloat16)

def stream_grad(stream, gain, inverse, w_qkv, grad_packed, grad_new):
    grad_normed = jnp.dot(grad_packed, w_qkv.T, preferred_element_type=jnp.float32)
    return (grad_new.astype(jnp.float32) + rms_backward(stream, gain, inverse, grad_normed)).astype(jnp.bfloat16)

def token_product(left, right):
    left_rows = left.reshape(-1, left.shape[-1])
    right_rows = right.reshape(-1, right.shape[-1])
    return jnp.dot(left_rows.T, right_rows, preferred_element_type=jnp.float32)

def attend_forward(query, keys, values, head_count, forms):
    query_heads = split_heads(query, head_count)
    scaling = query_heads.shape[-1] ** (-0.5)
    scores = contract(forms[0], query_heads, split_heads(keys, head_count)) * scaling
    row_peak = lax.optimization_barrier(jnp.max(scores, axis=-1, keepdims=True))
    shifted = jnp.exp(scores - row_peak)
    row_total = lax.optimization_barrier(jnp.sum(shifted, axis=-1, keepdims=True))
    weights = (shifted / row_total).astype(jnp.bfloat16)
    attended = contract(forms[1], weights, split_heads(values, head_count))
    return (merge_heads(attended).astype(jnp.bfloat16), row_peak, row_total)

def attend_backward(query, keys, values, row_peak, row_total, grad_attended, head_count, forms):
    query_heads = split_heads(query, head_count)
    key_heads = split_heads(keys, head_count)
    value_heads = split_heads(values, head_count)
    grad_heads = split_heads(grad_attended, head_count)
    scaling = query_heads.shape[-1] ** (-0.5)
    scores = contract(forms[0], query_heads, key_heads) * scaling
    probabilities = jnp.exp(scores - row_peak) / row_total
    weights = probabilities.astype(jnp.bfloat16)
    grad_weights = contract(forms[0], grad_heads, value_heads)
    grad_values = contract(forms[2], weights, grad_heads)
    inner = lax.optimization_barrier(jnp.sum(probabilities * grad_weights, axis=-1, keepdims=True))
    grad_scores = (probabilities * (grad_weights - inner) * scaling).astype(jnp.bfloat16)
    grad_query = contract(forms[1], grad_scores, key_heads)
    grad_keys = contract(forms[2], grad_scores, query_heads)
    return (merge_heads(grad_query), merge_heads(grad_keys), merge_heads(grad_values))

def space_layout(batch_count, count_query):
    block_rows = count_query
    if count_query > 512:
        block_rows = 1
        for candidate in range(1, 513):
            if count_query % candidate == 0:
                block_rows = candidate
    group_size = 1
    for candidate in range(1, batch_count + 1):
        if batch_count % candidate == 0 and candidate * block_rows <= max(512, block_rows):
            group_size = candidate
    return (group_size, block_rows)

def space_blocks(values, group_size, block_rows):
    batch_count, count_query, width = values.shape
    shaped = values.reshape(batch_count // group_size, group_size, count_query // block_rows, block_rows, width)
    return jnp.moveaxis(shaped, 2, 1)

def space_unblock(values):
    moved = jnp.moveaxis(values, 2, 1)
    return moved.reshape(moved.shape[0] * moved.shape[1], moved.shape[2] * moved.shape[3], moved.shape[4])

def space_forward(query, keys, values, head_count):
    batch_count, count_query, width = query.shape
    group_size, block_rows = space_layout(batch_count, count_query)
    key_groups = keys.reshape(batch_count // group_size, group_size, keys.shape[1], width)
    value_groups = values.reshape(batch_count // group_size, group_size, keys.shape[1], width)

    def per_group(items):
        query_group, key_group, value_group = items

        def per_block(query_block):
            return attend_forward(query_block, key_group, value_group, head_count, SPACE_FORMS)
        return lax.map(per_block, query_group)
    attended, peaks, totals = lax.map(per_group, (space_blocks(query, group_size, block_rows), key_groups, value_groups))
    return (space_unblock(attended), peaks, totals)

def space_backward(query, keys, values, peaks, totals, grad_attended, head_count):
    batch_count, count_query, width = query.shape
    group_size, block_rows = space_layout(batch_count, count_query)
    key_groups = keys.reshape(batch_count // group_size, group_size, keys.shape[1], width)
    value_groups = values.reshape(batch_count // group_size, group_size, keys.shape[1], width)

    def per_group(items):
        query_group, grad_group, key_group, value_group, peak_group, total_group = items

        def per_block(carry, block_items):
            query_block, grad_block, peak_block, total_block = block_items
            grad_query, grad_keys, grad_values = attend_backward(query_block, key_group, value_group, peak_block, total_block, grad_block, head_count, SPACE_FORMS)
            return ((carry[0] + grad_keys, carry[1] + grad_values), grad_query)
        zeros = jnp.zeros(key_group.shape, jnp.float32)
        sums, grad_query = lax.scan(per_block, (zeros, zeros), (query_group, grad_group, peak_group, total_group))
        return (grad_query, sums[0], sums[1])
    grad_query, grad_keys, grad_values = lax.map(per_group, (space_blocks(query, group_size, block_rows), space_blocks(grad_attended, group_size, block_rows), key_groups, value_groups, peaks, totals))
    return (space_unblock(grad_query), grad_keys.reshape(keys.shape), grad_values.reshape(keys.shape))

def stab_blocks(values):
    cut = math.gcd(values.shape[1], 64)
    return jnp.moveaxis(values.reshape(values.shape[0], values.shape[1] // cut, cut, values.shape[2]), 1, 0)

def stab_unblock(values):
    moved = jnp.moveaxis(values, 0, 1)
    return moved.reshape(moved.shape[0], moved.shape[1] * moved.shape[2], moved.shape[3])

def time_forward(query, keys, values):

    def one_block(items):
        return attend_forward(items[0], items[1], items[2], HEADS, TIME_FORMS)
    attended, peaks, totals = lax.map(one_block, (stab_blocks(query), stab_blocks(keys), stab_blocks(values)))
    return (stab_unblock(attended), peaks, totals)

def time_backward(query, keys, values, peaks, totals, grad_attended):

    def one_block(items):
        return attend_backward(items[0], items[1], items[2], items[3], items[4], items[5], HEADS, TIME_FORMS)
    grad_query, grad_keys, grad_values = lax.map(one_block, (stab_blocks(query), stab_blocks(keys), stab_blocks(values), peaks, totals, stab_blocks(grad_attended)))
    return (stab_unblock(grad_query), stab_unblock(grad_keys), stab_unblock(grad_values))

def pack_grads(grad_query, grad_keys, grad_values):
    return jnp.concatenate([grad_query.astype(jnp.bfloat16), grad_keys.astype(jnp.bfloat16), grad_values.astype(jnp.bfloat16)], axis=-1)

def reference(syndrome, basis_ids, coordinates, syndrome_table, basis_table, coord_table, round_table, gain_space, w_qkv_space, w_out_space, gain_time, w_qkv_time, w_out_time, grad_hidden):
    embedded = embed_tokens(syndrome, basis_ids, coordinates, syndrome_table, basis_table, coord_table, round_table)
    normed_space, inverse_space, query_space, keys_space, values_space = project(embedded, gain_space, w_qkv_space)
    attended_space, peaks_space, totals_space = space_forward(query_space, keys_space, values_space, HEADS)
    middle = add_branch(embedded, attended_space, w_out_space)
    normed_time, inverse_time, query_time, keys_time, values_time = project(middle, gain_time, w_qkv_time)
    attended_time, peaks_time, totals_time = time_forward(query_time, keys_time, values_time)
    hidden = add_branch(middle, attended_time, w_out_time)
    grad_attended_time = jnp.dot(grad_hidden, w_out_time.T, preferred_element_type=jnp.float32).astype(jnp.bfloat16)
    grads_time = time_backward(query_time, keys_time, values_time, peaks_time, totals_time, grad_attended_time)
    grad_packed_time = pack_grads(grads_time[0], grads_time[1], grads_time[2])
    grad_middle = stream_grad(middle, gain_time, inverse_time, w_qkv_time, grad_packed_time, grad_hidden)
    grad_attended_space = jnp.dot(grad_middle, w_out_space.T, preferred_element_type=jnp.float32).astype(jnp.bfloat16)
    grads_space = space_backward(query_space, keys_space, values_space, peaks_space, totals_space, grad_attended_space, HEADS)
    grad_packed_space = pack_grads(grads_space[0], grads_space[1], grads_space[2])
    grad_embedded = stream_grad(embedded, gain_space, inverse_space, w_qkv_space, grad_packed_space, grad_middle)
    scaling = 1.0 / math.sqrt(TOKENS)
    grad_w_qkv_space = token_product(normed_space, grad_packed_space) * scaling
    grad_w_out_space = token_product(attended_space, grad_middle) * scaling
    grad_w_qkv_time = token_product(normed_time, grad_packed_time) * scaling
    grad_w_out_time = token_product(attended_time, grad_hidden) * scaling
    return (hidden, grad_embedded, grad_w_qkv_space, grad_w_out_space, grad_w_qkv_time, grad_w_out_time)
```

```python
import math

import jax
import jax.numpy as jnp
from jax import lax
from jax.experimental import pallas as pl
from jax.experimental.pallas import tpu as pltpu
from jax.sharding import PartitionSpec as P

HEADS = 4
EPSILON = 1e-06
BOTH = ("stab", "rounds")
LEVELS = 128
VMEM_BYTES = 56 * 2**20
F32 = jnp.float32
BF16 = jnp.bfloat16


def dot(left, right, left_dim, right_dim):
    return lax.dot_general(
        left, right, (((left_dim,), (right_dim,)), ((), ())), preferred_element_type=F32
    )


def kernel_params(cost):
    return dict(
        compiler_params=pltpu.CompilerParams(vmem_limit_bytes=VMEM_BYTES),
        cost_estimate=pl.CostEstimate(flops=cost, bytes_accessed=cost // 400, transcendentals=0),
    )


def whole(shape):
    return pl.BlockSpec(shape, lambda *_: (0,) * len(shape))


def norm_columns(values, gain):
    inverse = lax.rsqrt(jnp.mean(values * values, axis=0, keepdims=True) + EPSILON)
    return (values * inverse * gain).astype(BF16), inverse


def norm_columns_backward(values, gain, inverse, grad_normed):
    gained = grad_normed * gain
    inner = jnp.mean(gained * values, axis=0, keepdims=True)
    return inverse * gained - values * (inverse * inverse * inverse) * inner


def space_forward_kernel(
    index_ref, table_ref, gain_ref, w_qkv_ref, w_out_ref,
    middle_ref, x_ref, normed_ref, inverse_ref, packed_ref, attended_ref, exps_ref, total_ref,
    row_ref, onehot_ref,
):
    head = pl.program_id(0)
    features, tokens = x_ref.shape
    depth = features // HEADS
    scale = depth**-0.5

    @pl.when(head == 0)
    def _():
        width = index_ref.shape[2]
        for block in range(index_ref.shape[0]):
            levels = lax.broadcasted_iota(jnp.int32, (LEVELS, width), 0)
            hit = levels == LEVELS - 1
            for kind in range(index_ref.shape[1]):
                hit = hit | (levels == index_ref[block, kind : kind + 1, :])
            onehot_ref[:, block * width : (block + 1) * width] = hit.astype(F32).astype(BF16)
        onehot = onehot_ref[...]
        table = table_ref[...]
        row_ref[...] = dot(onehot, table, 0, 0).astype(BF16)
        x = dot(table, onehot, 0, 0).astype(BF16)
        x_ref[...] = x
        normed, inverse = norm_columns(x.astype(F32), gain_ref[...])
        normed_ref[...] = normed
        inverse_ref[...] = inverse
        packed_ref[...] = dot(w_qkv_ref[...], normed, 0, 0).astype(BF16)

    at = pl.multiple_of(head * depth, depth)
    query = packed_ref[pl.ds(at, depth), :]
    keys = packed_ref[pl.ds(features + at, depth), :]
    values = packed_ref[pl.ds(2 * features + at, depth), :]
    block = 256
    for start in range(0, tokens, block):
        cols = slice(start, start + block)
        scores = dot(keys, query[:, cols], 0, 0) * scale
        shifted = jnp.exp(scores - jnp.max(scores, axis=0, keepdims=True))
        total = jnp.sum(shifted, axis=0, keepdims=True)
        exps = shifted.astype(BF16)
        exps_ref[0, :, cols] = exps
        inverse_total = 1.0 / total
        total_ref[0, :, cols] = inverse_total
        attended = dot(values, exps, 1, 0) * inverse_total
        attended_ref[pl.ds(at, depth), cols] = attended.astype(BF16)

    @pl.when(head == HEADS - 1)
    def _():
        branch = dot(attended_ref[...], w_out_ref[...], 0, 0)
        middle = (row_ref[...].astype(F32) + branch).astype(BF16)
        middle_ref[...] = middle.reshape(middle_ref.shape)


def space_forward(index, table, gain, w_qkv, w_out, chunks):
    tokens = index.shape[0] * index.shape[2]
    features = table.shape[1]
    shapes = [
        ((chunks, tokens // chunks, features), BF16),
        ((features, tokens), BF16),
        ((features, tokens), BF16),
        ((1, tokens), F32),
        ((3 * features, tokens), BF16),
        ((features, tokens), BF16),
        ((HEADS, tokens, tokens), BF16),
        ((HEADS, 1, tokens), F32),
    ]
    per_head = lambda shape: pl.BlockSpec((1,) + shape[1:], lambda head: (head, 0, 0))
    return pl.pallas_call(
        space_forward_kernel,
        grid=(HEADS,),
        out_shape=[jax.ShapeDtypeStruct(*item) for item in shapes],
        in_specs=[whole(a.shape) for a in (index, table, gain, w_qkv, w_out)],
        out_specs=[whole(shape) for shape, _ in shapes[:6]]
        + [per_head(shape) for shape, _ in shapes[6:]],
        scratch_shapes=[
            pltpu.VMEM((tokens, features), BF16),
            pltpu.VMEM((LEVELS, tokens), BF16),
        ],
        **kernel_params(4_000_000_000),
        name="space_forward",
    )(index, table, gain, w_qkv, w_out)


def time_kernel(
    middle_ref, grad_ref, gain_ref, w_qkv_ref, w_out_ref,
    grad_middle_ref, hidden_ref, normed_ref, grad_packed_ref, attended_ref, grad_row_ref,
    x_ref, inverse_ref, packed_ref, grad_attended_ref, rows_ref, grads_ref,
):
    stab_parts, round_parts, stabs, features = middle_ref.shape
    rounds = stab_parts * round_parts
    tokens = rounds * stabs
    depth = features // HEADS
    scale = depth**-0.5

    middle = jnp.swapaxes(middle_ref[...].astype(F32), 0, 1).reshape(tokens, features)
    grad = grad_ref[...].astype(F32).reshape(tokens, features)
    lanes = rows_ref.shape[2]
    halves = [slice(part * lanes, (part + 1) * lanes) for part in range(features // lanes)]
    for part, half in enumerate(halves):
        rows_ref[part] = middle[:, half]
        grads_ref[part] = grad[:, half]
    for stab in range(stabs):
        cols = slice(stab * rounds, (stab + 1) * rounds)
        at = pl.ds(stab, rounds, stride=stabs)
        for part, half in enumerate(halves):
            x_ref[half, cols] = rows_ref[part, at, :].T
            grad_row_ref[cols, half] = grads_ref[part, at, :].astype(BF16)
    x = x_ref[...]
    normed, inverse = norm_columns(x, gain_ref[...])
    normed_ref[...] = normed
    inverse_ref[...] = inverse
    packed_ref[...] = dot(w_qkv_ref[...], normed, 0, 0).astype(BF16)
    grad_attended_ref[...] = dot(w_out_ref[...], grad_row_ref[...], 1, 1).astype(BF16)

    def one_stab(stab, carry):
        cols = pl.ds(pl.multiple_of(stab * rounds, rounds), rounds)
        for head in range(HEADS):
            at = head * depth
            query = packed_ref[at : at + depth, cols]
            keys = packed_ref[features + at : features + at + depth, cols]
            values = packed_ref[2 * features + at : 2 * features + at + depth, cols]
            grad = grad_attended_ref[at : at + depth, cols]
            scores = dot(keys, query, 0, 0) * scale
            shifted = jnp.exp(scores - jnp.max(scores, axis=0, keepdims=True))
            probabilities = shifted * (1.0 / jnp.sum(shifted, axis=0, keepdims=True))
            weights = probabilities.astype(BF16)
            attended_ref[at : at + depth, cols] = dot(values, weights, 1, 0).astype(BF16)
            grad_weights = dot(values, grad, 0, 0)
            inner = jnp.sum(probabilities * grad_weights, axis=0, keepdims=True)
            grad_scores = (probabilities * (grad_weights - inner) * scale).astype(BF16)
            grad_packed_ref[at : at + depth, cols] = dot(keys, grad_scores, 1, 0).astype(BF16)
            grad_packed_ref[features + at : features + at + depth, cols] = dot(
                query, grad_scores, 1, 1
            ).astype(BF16)
            grad_packed_ref[2 * features + at : 2 * features + at + depth, cols] = dot(
                grad, weights, 1, 1
            ).astype(BF16)
        return carry

    lax.fori_loop(0, stabs, one_stab, 0)

    grad_normed = dot(w_qkv_ref[...], grad_packed_ref[...], 1, 0)
    grad_stream = norm_columns_backward(x_ref[...], gain_ref[...], inverse_ref[...], grad_normed)
    for stab in range(stabs):
        cols = slice(stab * rounds, (stab + 1) * rounds)
        at = pl.ds(stab, rounds, stride=stabs)
        for part, half in enumerate(halves):
            grads_ref[part, at, :] = grads_ref[part, at, :] + grad_stream[half, cols].T
    for part, half in enumerate(halves):
        grad_middle = grads_ref[part].reshape(round_parts, stab_parts, stabs, lanes)
        grad_middle_ref[:, :, :, half] = jnp.swapaxes(grad_middle, 0, 1).astype(BF16)
    branch = dot(attended_ref[...], w_out_ref[...], 0, 0)
    for stab in range(stabs):
        cols = slice(stab * rounds, (stab + 1) * rounds)
        at = pl.ds(stab, rounds, stride=stabs)
        for part, half in enumerate(halves):
            rows_ref[part, at, :] = rows_ref[part, at, :] + branch[cols, half]
    for part, half in enumerate(halves):
        hidden = rows_ref[part].reshape(hidden_ref.shape[:3] + (lanes,))
        hidden_ref[:, :, :, half] = hidden.astype(BF16)


def time_block(middle, grad, gain, w_qkv, w_out):
    stab_parts, round_parts, stabs, features = middle.shape
    tokens = stab_parts * round_parts * stabs
    shapes = [
        (middle.shape, BF16),
        (grad.shape, BF16),
        ((features, tokens), BF16),
        ((3 * features, tokens), BF16),
        ((features, tokens), BF16),
        ((tokens, features), BF16),
    ]
    return pl.pallas_call(
        time_kernel,
        out_shape=[jax.ShapeDtypeStruct(*item) for item in shapes],
        scratch_shapes=[
            pltpu.VMEM((features, tokens), F32),
            pltpu.VMEM((1, tokens), F32),
            pltpu.VMEM((3 * features, tokens), BF16),
            pltpu.VMEM((features, tokens), BF16),
            pltpu.VMEM((features // 128, tokens, 128), F32),
            pltpu.VMEM((features // 128, tokens, 128), F32),
        ],
        **kernel_params(3_000_000_000),
        name="time_block",
    )(middle, grad, gain, w_qkv, w_out)


def space_backward_kernel(
    grad_ref, x_ref, normed_ref, inverse_ref, packed_ref, attended_ref, exps_ref, total_ref,
    gain_ref, w_qkv_ref, w_out_ref,
    grad_stream_ref, grad_w_qkv_ref, grad_w_out_ref,
    grad_attended_ref, grad_packed_ref,
):
    head = pl.program_id(0)
    features, tokens = x_ref.shape
    depth = features // HEADS
    scale = depth**-0.5

    @pl.when(head == 0)
    def _():
        grad = grad_ref[...].reshape(tokens, features)
        grad_attended_ref[...] = dot(w_out_ref[...], grad, 1, 1).astype(BF16)
        grad_w_out_ref[...] = dot(attended_ref[...], grad, 1, 0).astype(grad_w_out_ref.dtype)

    at = pl.multiple_of(head * depth, depth)
    query = packed_ref[pl.ds(at, depth), :]
    keys = packed_ref[pl.ds(features + at, depth), :]
    values = packed_ref[pl.ds(2 * features + at, depth), :]
    grad = grad_attended_ref[pl.ds(at, depth), :].astype(F32) * total_ref[0]
    inner = jnp.sum(
        grad * attended_ref[pl.ds(at, depth), :].astype(F32), axis=0, keepdims=True
    )
    grad = grad.astype(BF16)
    block = 256
    grad_keys = jnp.zeros((depth, tokens), F32)
    grad_values = jnp.zeros((depth, tokens), F32)
    for start in range(0, tokens, block):
        cols = slice(start, start + block)
        exps = exps_ref[0, :, cols]
        grad_weights = dot(values, grad[:, cols], 0, 0)
        grad_scores = (exps.astype(F32) * (grad_weights - inner[:, cols])).astype(BF16)
        grad_query = dot(keys, grad_scores, 1, 0) * scale
        grad_packed_ref[pl.ds(at, depth), cols] = grad_query.astype(BF16)
        grad_keys = grad_keys + dot(query[:, cols], grad_scores, 1, 1)
        grad_values = grad_values + dot(grad[:, cols], exps, 1, 1)
    grad_packed_ref[pl.ds(features + at, depth), :] = (grad_keys * scale).astype(BF16)
    grad_packed_ref[pl.ds(2 * features + at, depth), :] = grad_values.astype(BF16)

    @pl.when(head == HEADS - 1)
    def _():
        grad_packed = grad_packed_ref[...]
        grad_w_qkv_ref[...] = dot(normed_ref[...], grad_packed, 1, 1).astype(grad_w_qkv_ref.dtype)
        grad_normed = dot(w_qkv_ref[...], grad_packed, 1, 0)
        grad_stream = norm_columns_backward(
            x_ref[...].astype(F32), gain_ref[...], inverse_ref[...], grad_normed
        )
        grad_new = grad_ref[...].reshape(tokens, features).astype(F32)
        grad_stream_ref[...] = (grad_new + grad_stream.T).astype(BF16)


def space_backward(grad, saved, gain, w_qkv, w_out):
    x, normed, inverse, packed, attended, exps, totals = saved
    features, tokens = x.shape
    arguments = (grad, x, normed, inverse, packed, attended, exps, totals, gain, w_qkv, w_out)
    per_head = lambda shape: pl.BlockSpec((1,) + shape[1:], lambda head: (head, 0, 0))
    in_specs = [whole(a.shape) for a in arguments]
    in_specs[5 + 1] = per_head(exps.shape)
    in_specs[5 + 2] = per_head(totals.shape)
    shapes = [
        ((tokens, features), BF16),
        ((features, 3 * features), BF16),
        ((features, features), BF16),
    ]
    return pl.pallas_call(
        space_backward_kernel,
        grid=(HEADS,),
        out_shape=[jax.ShapeDtypeStruct(*item) for item in shapes],
        in_specs=in_specs,
        out_specs=[whole(shape) for shape, _ in shapes],
        scratch_shapes=[
            pltpu.VMEM((features, tokens), BF16),
            pltpu.VMEM((3 * features, tokens), BF16),
        ],
        **kernel_params(8_000_000_000),
        name="space_backward",
    )(*arguments)


def weight_grad_kernel(normed_ref, grad_packed_ref, attended_ref, grad_ref, qkv_ref, out_ref):
    qkv_ref[...] = dot(normed_ref[...], grad_packed_ref[...], 1, 1).astype(qkv_ref.dtype)
    out_ref[...] = dot(attended_ref[...], grad_ref[...], 1, 0).astype(out_ref.dtype)


def weight_grads(normed, grad_packed, attended, grad):
    features = normed.shape[0]
    return pl.pallas_call(
        weight_grad_kernel,
        out_shape=[
            jax.ShapeDtypeStruct((features, 3 * features), BF16),
            jax.ShapeDtypeStruct((features, features), BF16),
        ],
        **kernel_params(600_000_000),
        name="weight_grads",
    )(normed, grad_packed, attended, grad)


def exchange(values, axes):
    return lax.all_to_all(values, axes, split_axis=0, concat_axis=0, tiled=True)


def reduce_to_all(flat, parts, scaling):
    pieces = exchange(flat.reshape(parts, flat.shape[0] // parts, flat.shape[1]), BOTH)
    mine = jnp.sum(pieces.astype(F32), axis=0) * scaling
    spread = jnp.broadcast_to(mine.astype(BF16)[None], pieces.shape)
    return exchange(spread, BOTH).reshape(flat.shape).astype(F32)


def on_device(
    syndrome,
    basis_ids,
    coordinates,
    syndrome_table,
    basis_table,
    coord_table,
    round_table,
    gain_space,
    w_qkv_space,
    w_out_space,
    gain_time,
    w_qkv_time,
    w_out_time,
    grad_hidden,
):
    stab_parts = lax.axis_size("stab")
    round_parts = lax.axis_size("rounds")
    parts = stab_parts * round_parts
    rounds_here, stabs_here, features = grad_hidden.shape
    stabs_time = stabs_here // round_parts
    coords = coord_table.shape[1]

    own = jnp.stack([basis_ids + 2 * coords, coordinates[0], coordinates[1] + coords])
    own = jnp.broadcast_to(own[None], (rounds_here,) + own.shape)
    index = exchange(
        jnp.concatenate([syndrome[:, None, :] + 2 * coords + 2, own], axis=1), "stab"
    )
    my_round = lax.dynamic_slice_in_dim(round_table, lax.axis_index("stab"), 1, axis=0)
    used = 2 * coords + 4
    table = jnp.concatenate(
        [
            coord_table.reshape(2 * coords, features),
            basis_table,
            syndrome_table,
            jnp.zeros((LEVELS - 1 - used, features), BF16),
            my_round,
        ]
    )
    grad_chunks = grad_hidden.reshape(rounds_here, round_parts, stabs_time, features)
    grad_time = exchange(jnp.swapaxes(grad_chunks, 0, 1), "rounds")

    gain_s = gain_space.reshape(features, 1)
    gain_t = gain_time.reshape(features, 1)
    middle, *saved = space_forward(index, table, gain_s, w_qkv_space, w_out_space, parts)
    middle_time = exchange(middle, BOTH)
    middle_time = middle_time.reshape(stab_parts, round_parts, stabs_time, features)
    grad_middle, hidden, normed, grad_packed, attended, grad_rows = time_block(
        middle_time, grad_time, gain_t, w_qkv_time, w_out_time
    )
    grad_space = exchange(grad_middle.reshape(parts, stabs_time, features), BOTH)
    hidden_home = exchange(hidden, "rounds")
    hidden_home = jnp.swapaxes(hidden_home, 0, 1).reshape(grad_hidden.shape)
    time_qkv, time_out = weight_grads(normed, grad_packed, attended, grad_rows)
    scaling = 1.0 / math.sqrt(parts * rounds_here * stabs_here)
    time_grads = reduce_to_all(
        jnp.concatenate([time_qkv.reshape(-1, features), time_out]), parts, scaling
    )
    grad_stream, space_qkv, space_out = space_backward(
        grad_space, saved, gain_s, w_qkv_space, w_out_space
    )
    grad_embedded = exchange(grad_stream.reshape(rounds_here, stabs_here, features), "stab")
    space_grads = reduce_to_all(
        jnp.concatenate([space_qkv.reshape(-1, features), space_out]), parts, scaling
    )

    def unpack(grads):
        return grads[: 3 * features].reshape(features, 3 * features), grads[3 * features :]

    return (hidden_home, grad_embedded) + unpack(space_grads) + unpack(time_grads)


def solution(mesh):
    in_specs = (
        P("rounds", "stab"),
        P("stab"),
        P(None, "stab"),
        P(),
        P(),
        P(),
        P("rounds", None),
        P(),
        P(),
        P(),
        P(),
        P(),
        P(),
        P("rounds", "stab", None),
    )
    out_specs = (P("rounds", "stab", None), P("rounds", "stab", None), P(), P(), P(), P())
    return jax.shard_map(
        on_device, mesh=mesh, in_specs=in_specs, out_specs=out_specs, check_vma=False
    )
```

```python
import math

import jax
import jax.numpy as jnp
from jax import lax
from jax.experimental import pallas as pl
from jax.experimental.pallas import tpu as pltpu
from jax.sharding import PartitionSpec as P

HEADS = 4
EPSILON = 1e-06
F32 = jnp.float32
BF16 = jnp.bfloat16

LEVELS = 128
ROW_AT, COLUMN_AT, BASIS_AT, SYNDROME_AT, ROUND_AT = 0, 48, 96, 104, 112


def dot(left, right, left_dim, right_dim):
    return lax.dot_general(
        left, right, (((left_dim,), (right_dim,)), ((), ())), preferred_element_type=F32
    )


def call(kernel, shapes, arguments, megabytes, microseconds, scratch=(), **grid):
    return pl.pallas_call(
        kernel,
        out_shape=[jax.ShapeDtypeStruct(*item) for item in shapes],
        scratch_shapes=[pltpu.VMEM(*item) for item in scratch],
        compiler_params=pltpu.CompilerParams(vmem_limit_bytes=megabytes * 2**20),
        cost_estimate=pl.CostEstimate(
            flops=microseconds * 500_000_000,
            bytes_accessed=microseconds * 2_000_000,
            transcendentals=0,
        ),
        name=kernel.__name__,
        **grid,
    )(*arguments)


def whole(shape):
    return pl.BlockSpec(shape, lambda *_: (0,) * len(shape))


def per_head(shape):
    return pl.BlockSpec((1,) + shape[1:], lambda head: (head,) + (0,) * (len(shape) - 1))


def as_column(gain):
    return jnp.broadcast_to(gain, (8, gain.shape[1])).T[:, :1]


def norm_columns(values, gain):
    inverse = lax.rsqrt(jnp.mean(values * values, axis=0, keepdims=True) + EPSILON)
    return (values * inverse * gain).astype(BF16), inverse


def norm_columns_backward(values, gain, inverse, grad_normed):
    gained = grad_normed * gain
    inner = jnp.mean(gained * values, axis=0, keepdims=True)
    return inverse * gained - values * (inverse * inverse * inverse) * inner


def store_blocks(ref, kind, grad_qkv, grad_out):
    features = grad_out.shape[0]
    blocks = [grad_qkv[:, j * features : (j + 1) * features] for j in range(3)] + [grad_out]
    count = ref.shape[0] // len(blocks)
    for j, block in enumerate(blocks):
        ref[j * count : (j + 1) * count, kind] = block.astype(BF16).reshape(
            count, ref.shape[2], features
        )


def index_kernel(syndrome_ref, basis_ref, coordinates_ref, index_ref):
    width = index_ref.shape[2]
    for block in range(index_ref.shape[0]):
        index_ref[block, 0:1, :] = syndrome_ref[block : block + 1, :] + SYNDROME_AT
        index_ref[block, 1:2, :] = basis_ref[...] + BASIS_AT
        index_ref[block, 2:3, :] = coordinates_ref[0:1, :] + ROW_AT
        index_ref[block, 3:4, :] = coordinates_ref[1:2, :] + COLUMN_AT
        index_ref[block, 4:5, :] = jnp.full((1, width), ROUND_AT + block, jnp.int32)


def space_forward(
    index_ref, syndrome_table_ref, basis_table_ref, coord_table_ref, round_table_ref,
    gain_ref, w_qkv_ref, w_out_ref,
    middle_ref, x_ref, normed_ref, inverse_ref, packed_ref, attended_ref, exps_ref, total_ref,
    table_ref, row_ref, onehot_ref,
):
    head = pl.program_id(0)
    features, tokens = x_ref.shape
    depth = features // HEADS

    @pl.when(head == 0)
    def _():
        coords = coord_table_ref.shape[1]
        table_ref[...] = jnp.zeros(table_ref.shape, F32)
        table_ref[ROW_AT : ROW_AT + coords, :] = coord_table_ref[0].astype(F32)
        table_ref[COLUMN_AT : COLUMN_AT + coords, :] = coord_table_ref[1].astype(F32)
        table_ref[BASIS_AT : BASIS_AT + 2, :] = basis_table_ref[...].astype(F32)
        table_ref[SYNDROME_AT : SYNDROME_AT + 2, :] = syndrome_table_ref[...].astype(F32)
        rounds = round_table_ref.shape[0]
        table_ref[ROUND_AT : ROUND_AT + rounds, :] = round_table_ref[...].astype(F32)
        width = index_ref.shape[2]
        levels = lax.broadcasted_iota(jnp.int32, (LEVELS, width), 0)
        for block in range(index_ref.shape[0]):
            hit = levels == index_ref[block, 0:1, :]
            for kind in range(1, index_ref.shape[1]):
                hit = hit | (levels == index_ref[block, kind : kind + 1, :])
            onehot_ref[:, block * width : (block + 1) * width] = hit.astype(F32).astype(BF16)
        onehot = onehot_ref[...]
        table = table_ref[...].astype(BF16)
        row_ref[...] = dot(onehot, table, 0, 0).astype(BF16)
        x = dot(table, onehot, 0, 0).astype(BF16)
        x_ref[...] = x
        normed, inverse = norm_columns(x.astype(F32), as_column(gain_ref[...]))
        normed_ref[...] = normed
        inverse_ref[...] = inverse
        packed = dot(w_qkv_ref[...], normed, 0, 0)
        packed_ref[:features, :] = (packed[:features] * (math.log2(math.e) * depth**-0.5)).astype(
            BF16
        )
        packed_ref[features:, :] = packed[features:].astype(BF16)

    at = pl.multiple_of(head * depth, depth)
    query = packed_ref[pl.ds(at, depth), :]
    keys = packed_ref[pl.ds(features + at, depth), :].T
    values = packed_ref[pl.ds(2 * features + at, depth), :]
    values = jnp.concatenate([values, jnp.ones((16, tokens), BF16)])
    block = SPACE_BLOCK
    starts = list(range(0, tokens, block))
    scores = dot(keys, query[:, :block], 1, 0)
    for start in starts:
        cols = slice(start, start + block)
        if start + block < tokens:
            later = dot(keys, query[:, start + block : start + 2 * block], 1, 0)
        exps = jnp.exp2(scores - jnp.max(scores, axis=0, keepdims=True)).astype(BF16)
        exps_ref[0, :, cols] = exps
        product = dot(values, exps, 1, 0)
        inverse_total = 1.0 / product[depth : depth + 1]
        total_ref[0, :, cols] = inverse_total
        attended_ref[pl.ds(at, depth), cols] = (product[:depth] * inverse_total).astype(BF16)
        scores = later

    @pl.when(head == HEADS - 1)
    def _():
        branch = dot(attended_ref[...], w_out_ref[...], 0, 0)
        middle = (row_ref[...].astype(F32) + branch).astype(BF16)
        middle_ref[...] = middle.reshape(middle_ref.shape)


SPACE_BLOCK = 256


def run_space_forward(index, tables, gain, w_qkv, w_out, chunks):
    tokens = index.shape[0] * index.shape[2]
    features = w_out.shape[0]
    shapes = [
        ((chunks, tokens // chunks, features), BF16),
        ((features, tokens), BF16),
        ((features, tokens), BF16),
        ((1, tokens), F32),
        ((3 * features, tokens), BF16),
        ((features, tokens), BF16),
        ((HEADS, tokens, tokens), BF16),
        ((HEADS, 1, tokens), F32),
    ]
    arguments = (index,) + tables + (gain, w_qkv, w_out)
    return call(
        space_forward,
        shapes,
        arguments,
        32,
        10,
        scratch=[
            ((LEVELS, features), F32),
            ((tokens, features), BF16),
            ((LEVELS, tokens), BF16),
        ],
        grid=(HEADS,),
        in_specs=[whole(a.shape) for a in arguments],
        out_specs=[whole(shape) for shape, _ in shapes[:6]]
        + [per_head(shape) for shape, _ in shapes[6:]],
    )


def time_block(
    middle_ref, grad_ref, gain_ref, w_qkv_ref, w_out_ref,
    grad_middle_ref, normed_ref, grad_packed_ref, attended_ref, grad_row_ref,
    x_ref, inverse_ref, packed_ref, grad_attended_ref, rows_ref, grads_ref,
):
    stab_parts, round_parts, stabs, features = middle_ref.shape
    rounds = stab_parts * round_parts
    tokens = rounds * stabs
    depth = features // HEADS
    scale = depth**-0.5

    middle = jnp.swapaxes(middle_ref[...].astype(F32), 0, 1).reshape(tokens, features)
    grad = grad_ref[...].astype(F32).reshape(tokens, features)
    lanes = rows_ref.shape[2]
    halves = [slice(part * lanes, (part + 1) * lanes) for part in range(features // lanes)]
    for part, half in enumerate(halves):
        rows_ref[part] = middle[:, half]
        grads_ref[part] = grad[:, half]
    for stab in range(stabs):
        cols = slice(stab * rounds, (stab + 1) * rounds)
        at = pl.ds(stab, rounds, stride=stabs)
        for part, half in enumerate(halves):
            x_ref[half, cols] = rows_ref[part, at, :].T
            grad_row_ref[cols, half] = grads_ref[part, at, :].astype(BF16)
    x = x_ref[...]
    gain = as_column(gain_ref[...])
    normed, inverse = norm_columns(x, gain)
    normed_ref[...] = normed
    inverse_ref[...] = inverse
    packed = dot(w_qkv_ref[...], normed, 0, 0)
    to_base_two = math.log2(math.e) * scale
    packed_ref[:features, :] = (packed[:features] * to_base_two).astype(BF16)
    packed_ref[features:, :] = packed[features:].astype(BF16)
    grad_attended_ref[...] = dot(w_out_ref[...], grad_row_ref[...], 1, 1).astype(BF16)

    def one_stab(stab, carry):
        cols = pl.ds(pl.multiple_of(stab * rounds, rounds), rounds)
        for head in range(HEADS):
            at = head * depth
            query = packed_ref[at : at + depth, cols]
            keys = packed_ref[features + at : features + at + depth, cols]
            values = packed_ref[2 * features + at : 2 * features + at + depth, cols]
            grad = grad_attended_ref[at : at + depth, cols]
            scores = dot(keys, query, 0, 0)
            shifted = jnp.exp2(scores - jnp.max(scores, axis=0, keepdims=True))
            probabilities = shifted * (1.0 / jnp.sum(shifted, axis=0, keepdims=True))
            weights = probabilities.astype(BF16)
            attended_ref[at : at + depth, cols] = dot(values, weights, 1, 0).astype(BF16)
            grad_weights = dot(values, grad, 0, 0)
            inner = jnp.sum(probabilities * grad_weights, axis=0, keepdims=True)
            grad_scores = (probabilities * (grad_weights - inner)).astype(BF16)
            grad_packed_ref[at : at + depth, cols] = (dot(keys, grad_scores, 1, 0) * scale).astype(
                BF16
            )
            grad_packed_ref[features + at : features + at + depth, cols] = (
                dot(query, grad_scores, 1, 1) * math.log(2.0)
            ).astype(BF16)
            grad_packed_ref[2 * features + at : 2 * features + at + depth, cols] = dot(
                grad, weights, 1, 1
            ).astype(BF16)
        return carry

    lax.fori_loop(0, stabs, one_stab, 0, unroll=TIME_UNROLL)

    grad_normed = dot(w_qkv_ref[...], grad_packed_ref[...], 1, 0)
    grad_stream = norm_columns_backward(x_ref[...], gain, inverse_ref[...], grad_normed)
    for stab in range(stabs):
        cols = slice(stab * rounds, (stab + 1) * rounds)
        at = pl.ds(stab, rounds, stride=stabs)
        for part, half in enumerate(halves):
            grads_ref[part, at, :] = grads_ref[part, at, :] + grad_stream[half, cols].T
    for part, half in enumerate(halves):
        grad_middle = grads_ref[part].reshape(round_parts, stab_parts, stabs, lanes)
        grad_middle_ref[:, :, :, half] = jnp.swapaxes(grad_middle, 0, 1).astype(BF16)


TIME_UNROLL = 2


def run_time_block(middle, grad, gain, w_qkv, w_out):
    stab_parts, round_parts, stabs, features = middle.shape
    tokens = stab_parts * round_parts * stabs
    shapes = [
        (middle.shape, BF16),
        ((features, tokens), BF16),
        ((3 * features, tokens), BF16),
        ((features, tokens), BF16),
        ((tokens, features), BF16),
    ]
    return call(
        time_block,
        shapes,
        (middle, grad, gain, w_qkv, w_out),
        24,
        10,
        scratch=[
            ((features, tokens), F32),
            ((1, tokens), F32),
            ((3 * features, tokens), BF16),
            ((features, tokens), BF16),
            ((features // 128, tokens, 128), F32),
            ((features // 128, tokens, 128), F32),
        ],
    )


def time_rest(
    middle_ref, normed_ref, grad_packed_ref, attended_ref, grad_row_ref, w_out_ref,
    hidden_ref, pieces_ref,
    rows_ref,
):
    stab_parts, round_parts, stabs, features = middle_ref.shape
    rounds = stab_parts * round_parts
    tokens = rounds * stabs
    lanes = rows_ref.shape[2]
    halves = [slice(part * lanes, (part + 1) * lanes) for part in range(features // lanes)]
    attended = attended_ref[...]
    branch = dot(attended, w_out_ref[...], 0, 0)
    middle = jnp.swapaxes(middle_ref[...].astype(F32), 0, 1).reshape(tokens, features)
    for part, half in enumerate(halves):
        rows_ref[part] = middle[:, half]
    for stab in range(stabs):
        cols = slice(stab * rounds, (stab + 1) * rounds)
        at = pl.ds(stab, rounds, stride=stabs)
        for part, half in enumerate(halves):
            rows_ref[part, at, :] = rows_ref[part, at, :] + branch[cols, half]
    for part, half in enumerate(halves):
        hidden = rows_ref[part].reshape(hidden_ref.shape[:3] + (lanes,))
        hidden_ref[:, :, :, half] = hidden.astype(BF16)
    store_blocks(
        pieces_ref,
        0,
        dot(normed_ref[...], grad_packed_ref[...], 1, 1),
        dot(attended, grad_row_ref[...], 1, 0),
    )


def run_time_rest(middle, grad_shape, normed, grad_packed, attended, grad_rows, w_out):
    features, tokens = normed.shape
    parts = middle.shape[0] * middle.shape[1]
    return call(
        time_rest,
        [(grad_shape, BF16), ((parts, 1, 4 * features // parts, features), BF16)],
        (middle, normed, grad_packed, attended, grad_rows, w_out),
        24,
        5,
        scratch=[((features // 128, tokens, 128), F32)],
    )


def space_backward(
    grad_ref, normed_ref, packed_ref, attended_ref, exps_ref, total_ref, w_out_ref, time_ref,
    grad_packed_ref, pieces_ref,
    grad_attended_ref, grad_scores_ref,
):
    head = pl.program_id(0)
    features, tokens = attended_ref.shape
    depth = features // HEADS

    @pl.when(head == 0)
    def _():
        grad = grad_ref[...].reshape(tokens, features)
        grad_attended_ref[...] = dot(w_out_ref[...], grad, 1, 1).astype(BF16)

    at = pl.multiple_of(head * depth, depth)
    query = packed_ref[pl.ds(at, depth), :]
    keys = packed_ref[pl.ds(features + at, depth), :]
    values = packed_ref[pl.ds(2 * features + at, depth), :].T
    grad = grad_attended_ref[pl.ds(at, depth), :].astype(F32) * total_ref[0]
    inner = jnp.sum(
        grad * attended_ref[pl.ds(at, depth), :].astype(F32), axis=0, keepdims=True
    )
    grad = grad.astype(BF16)
    block = SPACE_BLOCK
    grad_weights = dot(values, grad[:, :block], 1, 0)
    for start in range(0, tokens, block):
        cols = slice(start, start + block)
        if start + block < tokens:
            later = dot(values, grad[:, start + block : start + 2 * block], 1, 0)
        exps = exps_ref[0, :, cols].astype(F32)
        grad_scores = (exps * (grad_weights - inner[:, cols])).astype(BF16)
        grad_scores_ref[:, cols] = grad_scores
        grad_query = dot(keys, grad_scores, 1, 0) * depth**-0.5
        grad_packed_ref[pl.ds(at, depth), cols] = grad_query.astype(BF16)
        grad_weights = later
    grad_packed_ref[pl.ds(2 * features + at, depth), :] = dot(grad, exps_ref[0], 1, 1).astype(BF16)
    grad_packed_ref[pl.ds(features + at, depth), :] = (
        dot(query, grad_scores_ref[...], 1, 1) * math.log(2.0)
    ).astype(BF16)

    @pl.when(head == HEADS - 1)
    def _():
        grad = grad_ref[...].reshape(tokens, features)
        pieces_ref[:, 0:1] = time_ref[...]
        store_blocks(
            pieces_ref,
            1,
            dot(normed_ref[...], grad_packed_ref[...], 1, 1),
            dot(attended_ref[...], grad, 1, 0),
        )


def run_space_backward(grad, normed, packed, attended, exps, totals, w_out, time_pieces):
    features, tokens = attended.shape
    arguments = (grad, normed, packed, attended, exps, totals, w_out, time_pieces)
    in_specs = [whole(a.shape) for a in arguments]
    in_specs[4] = per_head(exps.shape)
    in_specs[5] = per_head(totals.shape)
    parts, _, rows, _ = time_pieces.shape
    shapes = [((3 * features, tokens), BF16), ((parts, 2, rows, features), BF16)]
    return call(
        space_backward,
        shapes,
        arguments,
        32,
        14,
        scratch=[((features, tokens), BF16), ((tokens, tokens), BF16)],
        grid=(HEADS,),
        in_specs=in_specs,
        out_specs=[whole(shape) for shape, _ in shapes],
    )


def space_stream(
    grad_ref, x_ref, inverse_ref, grad_packed_ref, gain_ref, w_qkv_ref, out_ref
):
    features, tokens = x_ref.shape
    grad_normed = dot(w_qkv_ref[...], grad_packed_ref[...], 1, 0)
    grad_stream = norm_columns_backward(
        x_ref[...].astype(F32), as_column(gain_ref[...]), inverse_ref[...], grad_normed
    )
    parts, groups, rows, _ = out_ref.shape
    grad_new = grad_ref[...].reshape(tokens, features).astype(F32)
    result = (grad_new + grad_stream.T).astype(BF16)
    here = tokens // (parts * rows)
    out_ref[:, :here] = result.reshape(parts, here, rows, features)
    out_ref[:, here:] = jnp.zeros((parts, groups - here, rows, features), BF16)


def run_space_stream(grad, x, inverse, grad_packed, gain, w_qkv, parts):
    features, tokens = x.shape
    rows = grad.shape[1]
    return call(
        space_stream,
        [((parts, tokens // (parts * rows) + 2, rows, features), BF16)],
        (grad, x, inverse, grad_packed, gain, w_qkv),
        24,
        4,
    )[0]


def unpack_weights(pieces_ref, space_qkv_ref, space_out_ref, time_qkv_ref, time_out_ref):
    features = space_out_ref.shape[0]
    count = pieces_ref.shape[0] // 4
    for kind, qkv_ref, out_ref in (
        (0, time_qkv_ref, time_out_ref),
        (1, space_qkv_ref, space_out_ref),
    ):
        for j in range(4):
            block = pieces_ref[j * count : (j + 1) * count, kind].reshape(features, features)
            if j < 3:
                qkv_ref[:, j * features : (j + 1) * features] = block.astype(F32)
            else:
                out_ref[...] = block.astype(F32)


def exchange(values, axes):
    return lax.all_to_all(values, axes, split_axis=0, concat_axis=0, tiled=True)


def on_device(
    syndrome,
    basis_ids,
    coordinates,
    syndrome_table,
    basis_table,
    coord_table,
    round_table,
    gain_space,
    w_qkv_space,
    w_out_space,
    gain_time,
    w_qkv_time,
    w_out_time,
    grad_hidden,
):
    stab_parts = lax.axis_size("stab")
    round_parts = lax.axis_size("rounds")
    parts = stab_parts * round_parts
    rounds_here, stabs_here, features = grad_hidden.shape
    stabs_time = stabs_here // round_parts

    own_index = call(
        index_kernel,
        [((stab_parts, 5, stabs_here), jnp.int32)],
        (syndrome, basis_ids.reshape(1, stabs_here), coordinates),
        4,
        1,
    )[0]
    index = exchange(own_index, "stab")
    grad_chunks = grad_hidden.reshape(rounds_here, round_parts, stabs_time, features)
    grad_chunks, index = lax.optimization_barrier((jnp.swapaxes(grad_chunks, 0, 1), index))
    grad_time = exchange(grad_chunks, "rounds")

    gain_s = gain_space.reshape(1, features)
    gain_t = gain_time.reshape(1, features)
    tables = (syndrome_table, basis_table, coord_table, round_table)
    middle, x, normed, inverse, packed, attended, exps, totals = run_space_forward(
        index, tables, gain_s, w_qkv_space, w_out_space, parts
    )
    middle_time = exchange(middle, ("stab", "rounds"))
    middle_time = middle_time.reshape(stab_parts, round_parts, stabs_time, features)
    grad_middle, normed_t, grad_packed_t, attended_t, grad_rows = run_time_block(
        middle_time, grad_time, gain_t, w_qkv_time, w_out_time
    )
    grad_space = exchange(grad_middle.reshape(parts, stabs_time, features), ("stab", "rounds"))
    hidden, time_pieces = run_time_rest(
        middle_time, grad_time.shape, normed_t, grad_packed_t, attended_t, grad_rows, w_out_time
    )
    hidden, grad_space = lax.optimization_barrier((hidden, grad_space))
    hidden_home = exchange(hidden, "rounds")
    hidden_home = jnp.swapaxes(hidden_home, 0, 1).reshape(grad_hidden.shape)
    grad_packed, pieces = run_space_backward(
        grad_space, normed, packed, attended, exps, totals, w_out_space, time_pieces
    )
    sources = exchange(pieces, ("rounds", "stab"))
    outgoing = run_space_stream(
        grad_space, x, inverse, grad_packed, gain_s, w_qkv_space, stab_parts
    )
    scaling = 1.0 / math.sqrt(parts * rounds_here * stabs_here)
    summed = (jnp.sum(sources.astype(F32), axis=0) * scaling).astype(BF16)
    here = outgoing.shape[1] - summed.shape[0]
    spread = jnp.broadcast_to(summed[None], (stab_parts,) + summed.shape)
    incoming = exchange(lax.dynamic_update_slice(outgoing, spread, (0, here, 0, 0)), "stab")
    grad_embedded = incoming[:, :here].reshape(grad_hidden.shape)
    gathered = incoming[:, here:]
    gathered = exchange(
        jnp.broadcast_to(gathered[None], (round_parts,) + gathered.shape), "rounds"
    )
    weights = call(
        unpack_weights,
        [((features, 3 * features), F32), ((features, features), F32)] * 2,
        (gathered.reshape((parts,) + summed.shape),),
        24,
        3,
    )
    return (hidden_home, grad_embedded) + tuple(weights)


def solution(mesh):
    in_specs = (
        P("rounds", "stab"),
        P("stab"),
        P(None, "stab"),
        P(),
        P(),
        P(),
        P("rounds", None),
        P(),
        P(),
        P(),
        P(),
        P(),
        P(),
        P("rounds", "stab", None),
    )
    out_specs = (P("rounds", "stab", None), P("rounds", "stab", None), P(), P(), P(), P())
    return jax.shard_map(
        on_device, mesh=mesh, in_specs=in_specs, out_specs=out_specs, check_vma=False
    )
```

```python
import math

import jax
import jax.numpy as jnp
from jax import lax
from jax.experimental import pallas as pl
from jax.experimental.pallas import tpu as pltpu
from jax.sharding import PartitionSpec as P

HEADS = 4
EPSILON = 1e-06
VMEM_BYTES = 60 * 2**20
F32 = jnp.float32
BF16 = jnp.bfloat16

LEVELS = 128
ROW_AT, COLUMN_AT, BASIS_AT, SYNDROME_AT, ROUND_AT = 0, 48, 96, 104, 112


def dot(left, right, left_dim, right_dim):
    return lax.dot_general(
        left, right, (((left_dim,), (right_dim,)), ((), ())), preferred_element_type=F32
    )


def call(kernel, shapes, arguments, microseconds, scratch=(), **grid):
    return pl.pallas_call(
        kernel,
        out_shape=[jax.ShapeDtypeStruct(*item) for item in shapes],
        scratch_shapes=[pltpu.VMEM(*item) for item in scratch],
        compiler_params=pltpu.CompilerParams(vmem_limit_bytes=VMEM_BYTES),
        cost_estimate=pl.CostEstimate(
            flops=microseconds * 500_000_000,
            bytes_accessed=microseconds * 2_000_000,
            transcendentals=0,
        ),
        name=kernel.__name__,
        **grid,
    )(*arguments)


def whole(shape):
    return pl.BlockSpec(shape, lambda *_: (0,) * len(shape))


def per_head(shape):
    return pl.BlockSpec((1,) + shape[1:], lambda head: (head,) + (0,) * (len(shape) - 1))


def as_column(gain):
    return jnp.broadcast_to(gain, (8, gain.shape[1])).T[:, :1]


def norm_columns(values, gain):
    inverse = lax.rsqrt(jnp.mean(values * values, axis=0, keepdims=True) + EPSILON)
    return (values * inverse * gain).astype(BF16), inverse


def norm_columns_backward(values, gain, inverse, grad_normed):
    gained = grad_normed * gain
    inner = jnp.mean(gained * values, axis=0, keepdims=True)
    return inverse * gained - values * (inverse * inverse * inverse) * inner


def store_blocks(ref, kind, grad_qkv, grad_out):
    features = grad_out.shape[0]
    blocks = [grad_qkv[:, j * features : (j + 1) * features] for j in range(3)] + [grad_out]
    count = ref.shape[0] // len(blocks)
    for j, block in enumerate(blocks):
        ref[j * count : (j + 1) * count, kind] = block.astype(BF16).reshape(
            count, ref.shape[2], features
        )


def index_kernel(syndrome_ref, basis_ref, coordinates_ref, index_ref):
    width = index_ref.shape[2]
    for block in range(index_ref.shape[0]):
        index_ref[block, 0:1, :] = syndrome_ref[block : block + 1, :] + SYNDROME_AT
        index_ref[block, 1:2, :] = basis_ref[...] + BASIS_AT
        index_ref[block, 2:3, :] = coordinates_ref[0:1, :] + ROW_AT
        index_ref[block, 3:4, :] = coordinates_ref[1:2, :] + COLUMN_AT
        index_ref[block, 4:5, :] = jnp.full((1, width), ROUND_AT + block, jnp.int32)


def space_forward(
    index_ref, syndrome_table_ref, basis_table_ref, coord_table_ref, round_table_ref,
    gain_ref, w_qkv_ref, w_out_ref,
    middle_ref, x_ref, normed_ref, inverse_ref, packed_ref, attended_ref, exps_ref, total_ref,
    table_ref, row_ref, onehot_ref,
):
    head = pl.program_id(0)
    features, tokens = x_ref.shape
    depth = features // HEADS

    @pl.when(head == 0)
    def _():
        coords = coord_table_ref.shape[1]
        table_ref[...] = jnp.zeros(table_ref.shape, F32)
        table_ref[ROW_AT : ROW_AT + coords, :] = coord_table_ref[0].astype(F32)
        table_ref[COLUMN_AT : COLUMN_AT + coords, :] = coord_table_ref[1].astype(F32)
        table_ref[BASIS_AT : BASIS_AT + 2, :] = basis_table_ref[...].astype(F32)
        table_ref[SYNDROME_AT : SYNDROME_AT + 2, :] = syndrome_table_ref[...].astype(F32)
        rounds = round_table_ref.shape[0]
        table_ref[ROUND_AT : ROUND_AT + rounds, :] = round_table_ref[...].astype(F32)
        width = index_ref.shape[2]
        levels = lax.broadcasted_iota(jnp.int32, (LEVELS, width), 0)
        for block in range(index_ref.shape[0]):
            hit = levels == index_ref[block, 0:1, :]
            for kind in range(1, index_ref.shape[1]):
                hit = hit | (levels == index_ref[block, kind : kind + 1, :])
            onehot_ref[:, block * width : (block + 1) * width] = hit.astype(F32).astype(BF16)
        onehot = onehot_ref[...]
        table = table_ref[...].astype(BF16)
        row_ref[...] = dot(onehot, table, 0, 0).astype(BF16)
        x = dot(table, onehot, 0, 0).astype(BF16)
        x_ref[...] = x
        normed, inverse = norm_columns(x.astype(F32), as_column(gain_ref[...]))
        normed_ref[...] = normed
        inverse_ref[...] = inverse
        packed = dot(w_qkv_ref[...], normed, 0, 0)
        packed_ref[:features, :] = (packed[:features] * (math.log2(math.e) * depth**-0.5)).astype(
            BF16
        )
        packed_ref[features:, :] = packed[features:].astype(BF16)

    at = pl.multiple_of(head * depth, depth)
    query = packed_ref[pl.ds(at, depth), :]
    keys = packed_ref[pl.ds(features + at, depth), :].T
    values = packed_ref[pl.ds(2 * features + at, depth), :]
    values = jnp.concatenate([values, jnp.ones((16, tokens), BF16)])
    block = SPACE_BLOCK
    starts = list(range(0, tokens, block))
    scores = dot(keys, query[:, :block], 1, 0)
    for start in starts:
        cols = slice(start, start + block)
        if start + block < tokens:
            later = dot(keys, query[:, start + block : start + 2 * block], 1, 0)
        exps = jnp.exp2(scores - jnp.max(scores, axis=0, keepdims=True)).astype(BF16)
        exps_ref[0, :, cols] = exps
        product = dot(values, exps, 1, 0)
        inverse_total = 1.0 / product[depth : depth + 1]
        total_ref[0, :, cols] = inverse_total
        attended_ref[pl.ds(at, depth), cols] = (product[:depth] * inverse_total).astype(BF16)
        scores = later

    @pl.when(head == HEADS - 1)
    def _():
        branch = dot(attended_ref[...], w_out_ref[...], 0, 0)
        middle = (row_ref[...].astype(F32) + branch).astype(BF16)
        middle_ref[...] = middle.reshape(middle_ref.shape)


SPACE_BLOCK = 256


def run_space_forward(index, tables, gain, w_qkv, w_out, chunks):
    tokens = index.shape[0] * index.shape[2]
    features = w_out.shape[0]
    shapes = [
        ((chunks, tokens // chunks, features), BF16),
        ((features, tokens), BF16),
        ((features, tokens), BF16),
        ((1, tokens), F32),
        ((3 * features, tokens), BF16),
        ((features, tokens), BF16),
        ((HEADS, tokens, tokens), BF16),
        ((HEADS, 1, tokens), F32),
    ]
    arguments = (index,) + tables + (gain, w_qkv, w_out)
    return call(
        space_forward,
        shapes,
        arguments,
        10,
        scratch=[
            ((LEVELS, features), F32),
            ((tokens, features), BF16),
            ((LEVELS, tokens), BF16),
        ],
        grid=(HEADS,),
        in_specs=[whole(a.shape) for a in arguments],
        out_specs=[whole(shape) for shape, _ in shapes[:6]]
        + [per_head(shape) for shape, _ in shapes[6:]],
    )


def time_grad(grad_ref, w_out_ref, grad_row_ref, grad_attended_ref, grads_ref):
    round_parts, stab_parts, stabs, features = grad_ref.shape
    rounds = stab_parts * round_parts
    grad = grad_ref[...].astype(F32).reshape(rounds * stabs, features)
    lanes = grads_ref.shape[2]
    for part in range(features // lanes):
        half = slice(part * lanes, (part + 1) * lanes)
        grads_ref[part] = grad[:, half]
        for stab in range(stabs):
            cols = slice(stab * rounds, (stab + 1) * rounds)
            at = pl.ds(stab, rounds, stride=stabs)
            grad_row_ref[cols, half] = grads_ref[part, at, :].astype(BF16)
    grad_attended_ref[...] = dot(w_out_ref[...], grad_row_ref[...], 1, 1).astype(BF16)


def run_time_grad(grad, w_out):
    round_parts, stab_parts, stabs, features = grad.shape
    tokens = stab_parts * round_parts * stabs
    return call(
        time_grad,
        [((tokens, features), BF16), ((features, tokens), BF16)],
        (grad, w_out),
        3,
        scratch=[((features // 128, tokens, 128), F32)],
    )


def time_block(
    middle_ref, grad_ref, grad_attended_ref, gain_ref, w_qkv_ref,
    grad_middle_ref, normed_ref, grad_packed_ref, attended_ref,
    x_ref, inverse_ref, packed_ref, rows_ref,
):
    stab_parts, round_parts, stabs, features = middle_ref.shape
    rounds = stab_parts * round_parts
    tokens = rounds * stabs
    depth = features // HEADS
    scale = depth**-0.5

    middle = jnp.swapaxes(middle_ref[...].astype(F32), 0, 1).reshape(tokens, features)
    lanes = rows_ref.shape[2]
    halves = [slice(part * lanes, (part + 1) * lanes) for part in range(features // lanes)]
    for part, half in enumerate(halves):
        rows_ref[part] = middle[:, half]
    for stab in range(stabs):
        cols = slice(stab * rounds, (stab + 1) * rounds)
        at = pl.ds(stab, rounds, stride=stabs)
        for part, half in enumerate(halves):
            x_ref[half, cols] = rows_ref[part, at, :].T
    x = x_ref[...]
    gain = as_column(gain_ref[...])
    normed, inverse = norm_columns(x, gain)
    normed_ref[...] = normed
    inverse_ref[...] = inverse
    packed = dot(w_qkv_ref[...], normed, 0, 0)
    to_base_two = math.log2(math.e) * scale
    packed_ref[:features, :] = (packed[:features] * to_base_two).astype(BF16)
    packed_ref[features:, :] = packed[features:].astype(BF16)

    def one_stab(stab, carry):
        cols = pl.ds(pl.multiple_of(stab * rounds, rounds), rounds)
        for head in range(HEADS):
            at = head * depth
            query = packed_ref[at : at + depth, cols]
            keys = packed_ref[features + at : features + at + depth, cols]
            values = packed_ref[2 * features + at : 2 * features + at + depth, cols]
            grad = grad_attended_ref[at : at + depth, cols]
            scores = dot(keys, query, 0, 0)
            shifted = jnp.exp2(scores - jnp.max(scores, axis=0, keepdims=True))
            probabilities = shifted * (1.0 / jnp.sum(shifted, axis=0, keepdims=True))
            weights = probabilities.astype(BF16)
            attended_ref[at : at + depth, cols] = dot(values, weights, 1, 0).astype(BF16)
            grad_weights = dot(values, grad, 0, 0)
            inner = jnp.sum(probabilities * grad_weights, axis=0, keepdims=True)
            grad_scores = (probabilities * (grad_weights - inner)).astype(BF16)
            grad_packed_ref[at : at + depth, cols] = (dot(keys, grad_scores, 1, 0) * scale).astype(
                BF16
            )
            grad_packed_ref[features + at : features + at + depth, cols] = (
                dot(query, grad_scores, 1, 1) * math.log(2.0)
            ).astype(BF16)
            grad_packed_ref[2 * features + at : 2 * features + at + depth, cols] = dot(
                grad, weights, 1, 1
            ).astype(BF16)
        return carry

    lax.fori_loop(0, stabs, one_stab, 0, unroll=TIME_UNROLL)

    grad_normed = dot(w_qkv_ref[...], grad_packed_ref[...], 1, 0)
    grad_stream = norm_columns_backward(x_ref[...], gain, inverse_ref[...], grad_normed)
    for stab in range(stabs):
        cols = slice(stab * rounds, (stab + 1) * rounds)
        at = pl.ds(stab, rounds, stride=stabs)
        for part, half in enumerate(halves):
            rows_ref[part, at, :] = grad_stream[half, cols].T
    for part, half in enumerate(halves):
        grad_middle = rows_ref[part].reshape(round_parts, stab_parts, stabs, lanes)
        grad_middle = grad_middle + grad_ref[:, :, :, half].astype(F32)
        grad_middle_ref[:, :, :, half] = jnp.swapaxes(grad_middle, 0, 1).astype(BF16)


TIME_UNROLL = 2


def run_time_block(middle, grad, grad_attended, gain, w_qkv):
    stab_parts, round_parts, stabs, features = middle.shape
    tokens = stab_parts * round_parts * stabs
    shapes = [
        (middle.shape, BF16),
        ((features, tokens), BF16),
        ((3 * features, tokens), BF16),
        ((features, tokens), BF16),
    ]
    return call(
        time_block,
        shapes,
        (middle, grad, grad_attended, gain, w_qkv),
        10,
        scratch=[
            ((features, tokens), F32),
            ((1, tokens), F32),
            ((3 * features, tokens), BF16),
            ((features // 128, tokens, 128), F32),
        ],
    )


def time_rest(
    middle_ref, normed_ref, grad_packed_ref, attended_ref, grad_row_ref, w_out_ref,
    hidden_ref, pieces_ref,
    rows_ref,
):
    stab_parts, round_parts, stabs, features = middle_ref.shape
    rounds = stab_parts * round_parts
    tokens = rounds * stabs
    lanes = rows_ref.shape[2]
    halves = [slice(part * lanes, (part + 1) * lanes) for part in range(features // lanes)]
    attended = attended_ref[...]
    branch = dot(attended, w_out_ref[...], 0, 0)
    middle = jnp.swapaxes(middle_ref[...].astype(F32), 0, 1).reshape(tokens, features)
    for part, half in enumerate(halves):
        rows_ref[part] = middle[:, half]
    for stab in range(stabs):
        cols = slice(stab * rounds, (stab + 1) * rounds)
        at = pl.ds(stab, rounds, stride=stabs)
        for part, half in enumerate(halves):
            rows_ref[part, at, :] = rows_ref[part, at, :] + branch[cols, half]
    for part, half in enumerate(halves):
        hidden = rows_ref[part].reshape(round_parts, stab_parts, stabs, lanes)
        hidden_ref[:, :stab_parts, :, half] = hidden.astype(BF16)
    groups = hidden_ref.shape[1] - stab_parts
    hidden_ref[:, stab_parts:] = jnp.zeros((round_parts, groups, stabs, features), BF16)
    store_blocks(
        pieces_ref,
        0,
        dot(normed_ref[...], grad_packed_ref[...], 1, 1),
        dot(attended, grad_row_ref[...], 1, 0),
    )


def run_time_rest(middle, normed, grad_packed, attended, grad_rows, w_out):
    features, tokens = normed.shape
    stab_parts, round_parts, stabs, _ = middle.shape
    parts = stab_parts * round_parts
    return call(
        time_rest,
        [
            ((round_parts, 3 * stab_parts, stabs, features), BF16),
            ((parts, 1, 4 * features // parts, features), BF16),
        ],
        (middle, normed, grad_packed, attended, grad_rows, w_out),
        5,
        scratch=[((features // 128, tokens, 128), F32)],
    )


def space_backward(
    grad_ref, normed_ref, packed_ref, attended_ref, exps_ref, total_ref, w_out_ref, time_ref,
    grad_packed_ref, pieces_ref,
    grad_attended_ref, grad_scores_ref,
):
    head = pl.program_id(0)
    features, tokens = attended_ref.shape
    depth = features // HEADS

    @pl.when(head == 0)
    def _():
        grad = grad_ref[...].reshape(tokens, features)
        grad_attended_ref[...] = dot(w_out_ref[...], grad, 1, 1).astype(BF16)

    at = pl.multiple_of(head * depth, depth)
    query = packed_ref[pl.ds(at, depth), :]
    keys = packed_ref[pl.ds(features + at, depth), :]
    values = packed_ref[pl.ds(2 * features + at, depth), :].T
    grad = grad_attended_ref[pl.ds(at, depth), :].astype(F32) * total_ref[0]
    inner = jnp.sum(
        grad * attended_ref[pl.ds(at, depth), :].astype(F32), axis=0, keepdims=True
    )
    grad = grad.astype(BF16)
    block = SPACE_BLOCK
    grad_weights = dot(values, grad[:, :block], 1, 0)
    for start in range(0, tokens, block):
        cols = slice(start, start + block)
        if start + block < tokens:
            later = dot(values, grad[:, start + block : start + 2 * block], 1, 0)
        exps = exps_ref[0, :, cols].astype(F32)
        grad_scores = (exps * (grad_weights - inner[:, cols])).astype(BF16)
        grad_scores_ref[:, cols] = grad_scores
        grad_query = dot(keys, grad_scores, 1, 0) * depth**-0.5
        grad_packed_ref[pl.ds(at, depth), cols] = grad_query.astype(BF16)
        grad_weights = later
    grad_packed_ref[pl.ds(2 * features + at, depth), :] = dot(grad, exps_ref[0], 1, 1).astype(BF16)
    grad_packed_ref[pl.ds(features + at, depth), :] = (
        dot(query, grad_scores_ref[...], 1, 1) * math.log(2.0)
    ).astype(BF16)

    @pl.when(head == HEADS - 1)
    def _():
        grad = grad_ref[...].reshape(tokens, features)
        pieces_ref[:, 0:1] = time_ref[...]
        store_blocks(
            pieces_ref,
            1,
            dot(normed_ref[...], grad_packed_ref[...], 1, 1),
            dot(attended_ref[...], grad, 1, 0),
        )


def run_space_backward(grad, normed, packed, attended, exps, totals, w_out, time_pieces):
    features, tokens = attended.shape
    arguments = (grad, normed, packed, attended, exps, totals, w_out, time_pieces)
    in_specs = [whole(a.shape) for a in arguments]
    in_specs[4] = per_head(exps.shape)
    in_specs[5] = per_head(totals.shape)
    parts, _, rows, _ = time_pieces.shape
    shapes = [((3 * features, tokens), BF16), ((parts, 2, rows, features), BF16)]
    return call(
        space_backward,
        shapes,
        arguments,
        14,
        scratch=[((features, tokens), BF16), ((tokens, tokens), BF16)],
        grid=(HEADS,),
        in_specs=in_specs,
        out_specs=[whole(shape) for shape, _ in shapes],
    )


def space_stream(
    grad_ref, x_ref, inverse_ref, grad_packed_ref, gain_ref, w_qkv_ref, out_ref
):
    features, tokens = x_ref.shape
    grad_normed = dot(w_qkv_ref[...], grad_packed_ref[...], 1, 0)
    grad_stream = norm_columns_backward(
        x_ref[...].astype(F32), as_column(gain_ref[...]), inverse_ref[...], grad_normed
    )
    parts, groups, rows, _ = out_ref.shape
    grad_new = grad_ref[...].reshape(tokens, features).astype(F32)
    result = (grad_new + grad_stream.T).astype(BF16)
    here = tokens // (parts * rows)
    out_ref[:, :here] = result.reshape(parts, here, rows, features)
    out_ref[:, here:] = jnp.zeros((parts, groups - here, rows, features), BF16)


def run_space_stream(grad, x, inverse, grad_packed, gain, w_qkv, parts):
    features, tokens = x.shape
    rows = grad.shape[1]
    return call(
        space_stream,
        [((parts, tokens // (parts * rows) + 2, rows, features), BF16)],
        (grad, x, inverse, grad_packed, gain, w_qkv),
        4,
    )[0]


def unpack(
    incoming_ref, hidden_ref, space_qkv_ref, space_out_ref, time_qkv_ref, time_out_ref
):
    round_parts, _, stabs, features = incoming_ref.shape
    here = hidden_ref.shape[0]
    for block in range(round_parts):
        cols = slice(block * stabs, (block + 1) * stabs)
        hidden_ref[:, cols, :] = incoming_ref[block, :here]
    count = round_parts // 4
    for j in range(4):
        pieces = incoming_ref[j * count : (j + 1) * count, here:].astype(F32)
        pieces = pieces.reshape(count, here, 2, stabs, features)
        for kind, qkv_ref, out_ref in (
            (0, time_qkv_ref, time_out_ref),
            (1, space_qkv_ref, space_out_ref),
        ):
            block = pieces[:, :, kind].reshape(features, features)
            if j < 3:
                qkv_ref[:, j * features : (j + 1) * features] = block
            else:
                out_ref[...] = block


def exchange(values, axes):
    return lax.all_to_all(values, axes, split_axis=0, concat_axis=0, tiled=True)


def on_device(
    syndrome,
    basis_ids,
    coordinates,
    syndrome_table,
    basis_table,
    coord_table,
    round_table,
    gain_space,
    w_qkv_space,
    w_out_space,
    gain_time,
    w_qkv_time,
    w_out_time,
    grad_hidden,
):
    stab_parts = lax.axis_size("stab")
    round_parts = lax.axis_size("rounds")
    parts = stab_parts * round_parts
    rounds_here, stabs_here, features = grad_hidden.shape
    stabs_time = stabs_here // round_parts

    own_index = call(
        index_kernel,
        [((stab_parts, 5, stabs_here), jnp.int32)],
        (syndrome, basis_ids.reshape(1, stabs_here), coordinates),
        1,
    )[0]
    index = exchange(own_index, "stab")
    grad_chunks = grad_hidden.reshape(rounds_here, round_parts, stabs_time, features)
    grad_chunks, index = lax.optimization_barrier((jnp.swapaxes(grad_chunks, 0, 1), index))
    grad_time = exchange(grad_chunks, "rounds")

    gain_s = gain_space.reshape(1, features)
    gain_t = gain_time.reshape(1, features)
    tables = (syndrome_table, basis_table, coord_table, round_table)
    middle, x, normed, inverse, packed, attended, exps, totals = run_space_forward(
        index, tables, gain_s, w_qkv_space, w_out_space, parts
    )
    middle, grad_time = lax.optimization_barrier((middle, grad_time))
    middle_time = exchange(middle, ("stab", "rounds"))
    middle_time = middle_time.reshape(stab_parts, round_parts, stabs_time, features)
    grad_rows, grad_attended_t = run_time_grad(grad_time, w_out_time)
    grad_middle, normed_t, grad_packed_t, attended_t = run_time_block(
        middle_time, grad_time, grad_attended_t, gain_t, w_qkv_time
    )
    grad_space = exchange(grad_middle.reshape(parts, stabs_time, features), ("stab", "rounds"))
    hidden, time_pieces = run_time_rest(
        middle_time, normed_t, grad_packed_t, attended_t, grad_rows, w_out_time
    )
    grad_packed, pieces = run_space_backward(
        grad_space, normed, packed, attended, exps, totals, w_out_space, time_pieces
    )
    sources = exchange(pieces, ("rounds", "stab"))
    outgoing = run_space_stream(
        grad_space, x, inverse, grad_packed, gain_s, w_qkv_space, stab_parts
    )
    scaling = 1.0 / math.sqrt(parts * rounds_here * stabs_here)
    summed = (jnp.sum(sources.astype(F32), axis=0) * scaling).astype(BF16)
    here = outgoing.shape[1] - summed.shape[0]
    spread = jnp.broadcast_to(summed[None], (stab_parts,) + summed.shape)
    incoming = exchange(lax.dynamic_update_slice(outgoing, spread, (0, here, 0, 0)), "stab")
    grad_embedded = incoming[:, :here].reshape(grad_hidden.shape)
    gathered = incoming[:, here:].reshape(1, 2 * stab_parts, stabs_time, features)
    spread = jnp.broadcast_to(gathered, (round_parts,) + gathered.shape[1:])
    incoming = exchange(lax.dynamic_update_slice(hidden, spread, (0, stab_parts, 0, 0)), "rounds")
    hidden_home, *weights = call(
        unpack,
        [(grad_hidden.shape, BF16)]
        + [((features, 3 * features), F32), ((features, features), F32)] * 2,
        (incoming,),
        3,
    )
    return (hidden_home, grad_embedded) + tuple(weights)


def solution(mesh):
    in_specs = (
        P("rounds", "stab"),
        P("stab"),
        P(None, "stab"),
        P(),
        P(),
        P(),
        P("rounds", None),
        P(),
        P(),
        P(),
        P(),
        P(),
        P(),
        P("rounds", "stab", None),
    )
    out_specs = (P("rounds", "stab", None), P("rounds", "stab", None), P(), P(), P(), P())
    return jax.shard_map(
        on_device, mesh=mesh, in_specs=in_specs, out_specs=out_specs, check_vma=False
    )
```

```python
import math

import jax
import jax.numpy as jnp
from jax import lax
from jax.experimental import pallas as pl
from jax.experimental.pallas import tpu as pltpu
from jax.sharding import PartitionSpec as P

HEADS = 4
EPSILON = 1e-06
VMEM_BYTES = 20 * 2**20
F32 = jnp.float32
BF16 = jnp.bfloat16

LEVELS = 128
ROW_AT, COLUMN_AT, BASIS_AT, SYNDROME_AT, ROUND_AT = 0, 48, 96, 104, 112


def dot(left, right, left_dim, right_dim):
    return lax.dot_general(
        left, right, (((left_dim,), (right_dim,)), ((), ())), preferred_element_type=F32
    )


def call(kernel, shapes, arguments, microseconds, scratch=(), **grid):
    return pl.pallas_call(
        kernel,
        out_shape=[
            jax.ShapeDtypeStruct(*item) if isinstance(item, tuple) else item for item in shapes
        ],
        scratch_shapes=[pltpu.VMEM(*item) if isinstance(item, tuple) else item for item in scratch],
        compiler_params=pltpu.CompilerParams(vmem_limit_bytes=VMEM_BYTES),
        cost_estimate=pl.CostEstimate(
            flops=microseconds * 500_000_000,
            bytes_accessed=microseconds * 2_000_000,
            transcendentals=0,
        ),
        name=kernel.__name__,
        **grid,
    )(*arguments)


def in_vmem(*arrays):
    return [pltpu.with_memory_space_constraint(array, pltpu.VMEM) for array in arrays]


def in_range(inverse_totals):
    least, most = jnp.min(inverse_totals), jnp.max(inverse_totals)
    return jnp.logical_and(least > 2.0**-30, most < 2.0**30)


def split_rows(row):
    terms = []
    for _ in range(3):
        terms.append(row.astype(BF16))
        row = row - terms[-1].astype(F32)
    zeros = jnp.zeros((16 - len(terms), row.shape[1]), BF16)
    return jnp.concatenate(terms + [zeros])


def as_column(gain):
    return jnp.broadcast_to(gain, (8, gain.shape[1])).T[:, :1]


def norm_columns(values, gain):
    inverse = lax.rsqrt(jnp.mean(values * values, axis=0, keepdims=True) + EPSILON)
    return (values * inverse * gain).astype(BF16), inverse


def norm_columns_backward(values, gain, inverse, grad_normed):
    gained = grad_normed * gain
    inner = jnp.mean(gained * values, axis=0, keepdims=True)
    return inverse * gained - values * (inverse * inverse * inverse) * inner


def store_blocks(ref, kind, grad_qkv, grad_out):
    features = grad_out.shape[0]
    blocks = [grad_qkv[:, j * features : (j + 1) * features] for j in range(3)] + [grad_out]
    count = ref.shape[0] // len(blocks)
    for j, block in enumerate(blocks):
        ref[j * count : (j + 1) * count, kind] = block.astype(BF16).reshape(
            count, ref.shape[2], features
        )


def index_kernel(syndrome_ref, basis_ref, coordinates_ref, index_ref):
    width = index_ref.shape[2]
    for block in range(index_ref.shape[0]):
        index_ref[block, 0:1, :] = syndrome_ref[block : block + 1, :] + SYNDROME_AT
        index_ref[block, 1:2, :] = basis_ref[...] + BASIS_AT
        index_ref[block, 2:3, :] = coordinates_ref[0:1, :] + ROW_AT
        index_ref[block, 3:4, :] = coordinates_ref[1:2, :] + COLUMN_AT
        index_ref[block, 4:5, :] = jnp.full((1, width), ROUND_AT + block, jnp.int32)


def space_forward(
    index_ref, syndrome_table_ref, basis_table_ref, coord_table_ref, round_table_ref,
    gain_ref, w_qkv_ref, w_out_ref,
    middle_ref, inverse_ref, attended_ref, total_ref, x_ref, normed_ref, packed_ref, exps_ref,
    table_ref, row_ref, onehot_ref,
):
    features, tokens = x_ref.shape
    depth = features // HEADS
    coords = coord_table_ref.shape[1]
    table_ref[...] = jnp.zeros(table_ref.shape, F32)
    table_ref[ROW_AT : ROW_AT + coords, :] = coord_table_ref[0].astype(F32)
    table_ref[COLUMN_AT : COLUMN_AT + coords, :] = coord_table_ref[1].astype(F32)
    table_ref[BASIS_AT : BASIS_AT + 2, :] = basis_table_ref[...].astype(F32)
    table_ref[SYNDROME_AT : SYNDROME_AT + 2, :] = syndrome_table_ref[...].astype(F32)
    rounds = round_table_ref.shape[0]
    table_ref[ROUND_AT : ROUND_AT + rounds, :] = round_table_ref[...].astype(F32)
    width = index_ref.shape[2]
    levels = lax.broadcasted_iota(jnp.int32, (LEVELS, width), 0)
    for block in range(index_ref.shape[0]):
        hit = levels == index_ref[block, 0:1, :]
        for kind in range(1, index_ref.shape[1]):
            hit = hit | (levels == index_ref[block, kind : kind + 1, :])
        onehot_ref[:, block * width : (block + 1) * width] = hit.astype(F32).astype(BF16)
    table = table_ref[...].astype(BF16)
    x = dot(table, onehot_ref[...], 0, 0).astype(BF16)
    x_ref[...] = x
    normed, inverse = norm_columns(x.astype(F32), as_column(gain_ref[...]))
    normed_ref[...] = normed
    inverse_ref[...] = inverse
    packed = dot(w_qkv_ref[...], normed, 0, 0)
    packed_ref[:features, :] = (packed[:features] * (math.log2(math.e) * depth**-0.5)).astype(BF16)
    packed_ref[features:, :] = packed[features:].astype(BF16)
    row_ref[...] = dot(onehot_ref[...], table, 0, 0).astype(BF16)

    def operands(head):
        at = head * depth
        query = packed_ref[at : at + depth, :]
        keys = packed_ref[features + at : features + at + depth, :].T
        values = packed_ref[2 * features + at : 2 * features + at + depth, :]
        return query, keys, jnp.concatenate([values, jnp.ones((16, tokens), BF16)])

    def attend(head, values, cols):
        product = dot(values, exps_ref[head, :, cols], 1, 0)
        inverse_total = 1.0 / product[depth : depth + 1]
        total_ref[head, :, cols] = inverse_total
        attended_ref[head * depth : (head + 1) * depth, cols] = (
            product[:depth] * inverse_total
        ).astype(BF16)

    blocks = [slice(start, start + SPACE_BLOCK) for start in range(0, tokens, SPACE_BLOCK)]
    before = None
    for head in range(HEADS):
        query, keys, values = operands(head)
        for cols in blocks:
            for low in range(0, tokens, KEY_TILE):
                rows = slice(low, low + KEY_TILE)
                exps_ref[head, rows, cols] = jnp.exp2(
                    dot(keys[rows], query[:, cols], 1, 0)
                ).astype(BF16)
            if before is not None:
                attend(*before)
            before = head, values, cols
    attend(*before)

    @pl.when(jnp.logical_not(in_range(total_ref[...])))
    def _():
        for head in range(HEADS):
            query, keys, values = operands(head)
            for cols in blocks:
                scores = dot(keys, query[:, cols], 1, 0)
                peak = jnp.max(scores, axis=0, keepdims=True)
                exps_ref[head, :, cols] = jnp.exp2(scores - peak).astype(BF16)
                attend(head, values, cols)

    branch = dot(attended_ref[...], w_out_ref[...], 0, 0)
    middle = (row_ref[...].astype(F32) + branch).astype(BF16)
    middle_ref[...] = middle.reshape(middle_ref.shape)


SPACE_BLOCK = 256
KEY_TILE = 128
VMEM = pl.BlockSpec(memory_space=pltpu.VMEM)
ANY = pl.BlockSpec(memory_space=pl.ANY)


def run_space_forward(index, tables, gain, w_qkv, w_out, chunks):
    tokens = index.shape[0] * index.shape[2]
    features = w_out.shape[0]
    shapes = [
        ((chunks, tokens // chunks, features), BF16),
        ((1, tokens), F32),
        pltpu.VMEM((features, tokens), BF16),
        ((HEADS, 1, tokens), F32),
        pltpu.VMEM((features, tokens), BF16),
        pltpu.VMEM((features, tokens), BF16),
        pltpu.VMEM((3 * features, tokens), BF16),
        pltpu.VMEM((HEADS, tokens, tokens), BF16),
    ]
    arguments = (index,) + tables + (gain, w_qkv, w_out)
    middle, inverse, attended, totals, x, normed, packed, exps = call(
        space_forward,
        shapes,
        arguments,
        10,
        scratch=[
            ((LEVELS, features), F32),
            ((tokens, features), BF16),
            ((LEVELS, tokens), BF16),
        ],
        in_specs=[VMEM] * len(arguments),
        out_specs=[VMEM] * 8,
    )
    return middle, x, normed, inverse, packed, attended, exps, totals


def time_grad(grad_ref, w_out_ref, grad_row_ref, grad_attended_ref, grads_ref):
    round_parts, stab_parts, stabs, features = grad_ref.shape
    rounds = stab_parts * round_parts
    grad = grad_ref[...].astype(F32).reshape(rounds * stabs, features)
    lanes = grads_ref.shape[2]
    for part in range(features // lanes):
        half = slice(part * lanes, (part + 1) * lanes)
        grads_ref[part] = grad[:, half]
        for stab in range(stabs):
            cols = slice(stab * rounds, (stab + 1) * rounds)
            at = pl.ds(stab, rounds, stride=stabs)
            grad_row_ref[cols, half] = grads_ref[part, at, :].astype(BF16)
    grad_attended_ref[...] = dot(w_out_ref[...], grad_row_ref[...], 1, 1).astype(BF16)


def run_time_grad(grad, w_out):
    round_parts, stab_parts, stabs, features = grad.shape
    tokens = stab_parts * round_parts * stabs
    return call(
        time_grad,
        [((tokens, features), BF16), ((features, tokens), BF16)],
        (grad, w_out),
        3,
        scratch=[((features // 128, tokens, 128), F32)],
    )


def time_block(
    middle_ref, grad_ref, grad_attended_ref, gain_ref, w_qkv_ref,
    grad_middle_ref, normed_ref, grad_packed_ref, attended_ref,
    x_ref, inverse_ref, packed_ref, rows_ref,
):
    stab_parts, round_parts, stabs, features = middle_ref.shape
    rounds = stab_parts * round_parts
    tokens = rounds * stabs
    depth = features // HEADS
    scale = depth**-0.5

    middle = jnp.swapaxes(middle_ref[...].astype(F32), 0, 1).reshape(tokens, features)
    lanes = rows_ref.shape[2]
    halves = [slice(part * lanes, (part + 1) * lanes) for part in range(features // lanes)]
    for part, half in enumerate(halves):
        rows_ref[part] = middle[:, half]
    for stab in range(stabs):
        cols = slice(stab * rounds, (stab + 1) * rounds)
        at = pl.ds(stab, rounds, stride=stabs)
        for part, half in enumerate(halves):
            x_ref[half, cols] = rows_ref[part, at, :].T
    x = x_ref[...]
    gain = as_column(gain_ref[...])
    normed, inverse = norm_columns(x, gain)
    normed_ref[...] = normed
    inverse_ref[...] = inverse
    packed = dot(w_qkv_ref[...], normed, 0, 0)
    to_base_two = math.log2(math.e) * scale
    packed_ref[:features, :] = (packed[:features] * to_base_two).astype(BF16)
    packed_ref[features:, :] = packed[features:].astype(BF16)

    def one_stab(stab, carry):
        cols = pl.ds(pl.multiple_of(stab * rounds, rounds), rounds)
        for head in range(HEADS):
            at = head * depth
            query = packed_ref[at : at + depth, cols]
            keys = packed_ref[features + at : features + at + depth, cols]
            values = packed_ref[2 * features + at : 2 * features + at + depth, cols]
            grad = grad_attended_ref[at : at + depth, cols]
            scores = dot(keys, query, 0, 0)
            shifted = jnp.exp2(scores - jnp.max(scores, axis=0, keepdims=True))
            probabilities = shifted * (1.0 / jnp.sum(shifted, axis=0, keepdims=True))
            weights = probabilities.astype(BF16)
            attended_ref[at : at + depth, cols] = dot(values, weights, 1, 0).astype(BF16)
            grad_weights = dot(values, grad, 0, 0)
            inner = jnp.sum(probabilities * grad_weights, axis=0, keepdims=True)
            grad_scores = (probabilities * (grad_weights - inner)).astype(BF16)
            grad_packed_ref[at : at + depth, cols] = (dot(keys, grad_scores, 1, 0) * scale).astype(
                BF16
            )
            grad_packed_ref[features + at : features + at + depth, cols] = (
                dot(query, grad_scores, 1, 1) * math.log(2.0)
            ).astype(BF16)
            grad_packed_ref[2 * features + at : 2 * features + at + depth, cols] = dot(
                grad, weights, 1, 1
            ).astype(BF16)
        return carry

    lax.fori_loop(0, stabs, one_stab, 0, unroll=TIME_UNROLL)

    grad_normed = dot(w_qkv_ref[...], grad_packed_ref[...], 1, 0)
    grad_stream = norm_columns_backward(x_ref[...], gain, inverse_ref[...], grad_normed)
    for stab in range(stabs):
        cols = slice(stab * rounds, (stab + 1) * rounds)
        at = pl.ds(stab, rounds, stride=stabs)
        for part, half in enumerate(halves):
            rows_ref[part, at, :] = grad_stream[half, cols].T
    for part, half in enumerate(halves):
        grad_middle = rows_ref[part].reshape(round_parts, stab_parts, stabs, lanes)
        grad_middle = grad_middle + grad_ref[:, :, :, half].astype(F32)
        grad_middle_ref[:, :, :, half] = jnp.swapaxes(grad_middle, 0, 1).astype(BF16)


TIME_UNROLL = 2


def run_time_block(middle, grad, grad_attended, gain, w_qkv):
    stab_parts, round_parts, stabs, features = middle.shape
    tokens = stab_parts * round_parts * stabs
    shapes = [
        (middle.shape, BF16),
        ((features, tokens), BF16),
        ((3 * features, tokens), BF16),
        ((features, tokens), BF16),
    ]
    return call(
        time_block,
        shapes,
        (middle, grad, grad_attended, gain, w_qkv),
        10,
        scratch=[
            ((features, tokens), F32),
            ((1, tokens), F32),
            ((3 * features, tokens), BF16),
            ((features // 128, tokens, 128), F32),
        ],
    )


def time_rest(
    middle_ref, normed_ref, grad_packed_ref, attended_ref, grad_row_ref, w_out_ref,
    hidden_ref, pieces_ref,
    rows_ref,
):
    stab_parts, round_parts, stabs, features = middle_ref.shape
    rounds = stab_parts * round_parts
    tokens = rounds * stabs
    lanes = rows_ref.shape[2]
    halves = [slice(part * lanes, (part + 1) * lanes) for part in range(features // lanes)]
    attended = attended_ref[...]
    branch = dot(attended, w_out_ref[...], 0, 0)
    middle = jnp.swapaxes(middle_ref[...].astype(F32), 0, 1).reshape(tokens, features)
    for part, half in enumerate(halves):
        rows_ref[part] = middle[:, half]
    for stab in range(stabs):
        cols = slice(stab * rounds, (stab + 1) * rounds)
        at = pl.ds(stab, rounds, stride=stabs)
        for part, half in enumerate(halves):
            rows_ref[part, at, :] = rows_ref[part, at, :] + branch[cols, half]
    for part, half in enumerate(halves):
        hidden = rows_ref[part].reshape(round_parts, stab_parts, stabs, lanes)
        hidden_ref[:, :stab_parts, :, half] = hidden.astype(BF16)
    groups = hidden_ref.shape[1] - stab_parts
    hidden_ref[:, stab_parts:] = jnp.zeros((round_parts, groups, stabs, features), BF16)
    store_blocks(
        pieces_ref,
        0,
        dot(normed_ref[...], grad_packed_ref[...], 1, 1),
        dot(attended, grad_row_ref[...], 1, 0),
    )


def run_time_rest(middle, normed, grad_packed, attended, grad_rows, w_out):
    features, tokens = normed.shape
    stab_parts, round_parts, stabs, _ = middle.shape
    parts = stab_parts * round_parts
    return call(
        time_rest,
        [
            ((round_parts, 3 * stab_parts, stabs, features), BF16),
            ((parts, 1, 4 * features // parts, features), BF16),
        ],
        (middle, normed, grad_packed, attended, grad_rows, w_out),
        5,
        scratch=[((features // 128, tokens, 128), F32)],
    )


def space_backward(
    grad_ref, packed_ref, attended_ref, total_ref, w_out_ref, normed_ref, exps_ref, time_ref,
    grad_packed_ref, pieces_ref,
    grad_attended_ref, grad_scores_ref,
):
    features, tokens = attended_ref.shape
    depth = features // HEADS
    new = grad_ref[...].reshape(tokens, features)
    grad_attended_ref[...] = dot(w_out_ref[...], new, 1, 1).astype(BF16)
    blocks = [slice(start, start + SPACE_BLOCK) for start in range(0, tokens, SPACE_BLOCK)]

    def finish(head, grad):
        at = head * depth
        keys = packed_ref[features + at : features + at + depth, :]
        query = packed_ref[at : at + depth, :]
        scores = grad_scores_ref[head % 2]
        grad_packed_ref[at : at + depth, :] = (dot(keys, scores, 1, 0) * depth**-0.5).astype(BF16)
        grad_packed_ref[features + at : features + at + depth, :] = (
            dot(query, scores, 1, 1) * math.log(2.0)
        ).astype(BF16)
        grad_packed_ref[2 * features + at : 2 * features + at + depth, :] = dot(
            grad, exps_ref[head], 1, 1
        ).astype(BF16)

    before = None
    for head in range(HEADS):
        at = head * depth
        values = packed_ref[2 * features + at : 2 * features + at + depth, :]
        grad = grad_attended_ref[at : at + depth, :].astype(F32) * total_ref[head]
        inner = jnp.sum(
            grad * attended_ref[at : at + depth, :].astype(F32), axis=0, keepdims=True
        )
        grad = grad.astype(BF16)
        wide_grad = jnp.concatenate([grad, split_rows(inner)])
        wide_values = jnp.concatenate([values.T, jnp.full((tokens, 16), -1.0, BF16)], axis=1)
        for cols in blocks:
            for low in range(0, tokens, KEY_TILE):
                rows = slice(low, low + KEY_TILE)
                centred = dot(wide_values[rows], wide_grad[:, cols], 1, 0)
                grad_scores_ref[head % 2, rows, cols] = (
                    exps_ref[head, rows, cols].astype(F32) * centred
                ).astype(BF16)
        if before is not None:
            finish(*before)
        before = head, grad
    finish(*before)
    pieces_ref[:, 0:1] = time_ref[...]
    store_blocks(
        pieces_ref,
        1,
        dot(normed_ref[...], grad_packed_ref[...], 1, 1),
        dot(attended_ref[...], new, 1, 0),
    )


def run_space_backward(grad, normed, packed, attended, exps, totals, w_out, time_pieces):
    features, tokens = attended.shape
    parts, _, rows, _ = time_pieces.shape
    normed, packed, attended, exps = in_vmem(normed, packed, attended, exps)
    shapes = [pltpu.VMEM((3 * features, tokens), BF16), ((parts, 2, rows, features), BF16)]
    return call(
        space_backward,
        shapes,
        (grad, packed, attended, totals, w_out, normed, exps, time_pieces),
        14,
        scratch=[((features, tokens), BF16), ((2, tokens, tokens), BF16)],
        in_specs=[VMEM] * 8,
        out_specs=[VMEM] * 2,
    )


def space_stream(
    grad_ref, x_ref, inverse_ref, grad_packed_ref, gain_ref, w_qkv_ref, out_ref
):
    features, tokens = x_ref.shape
    grad_normed = dot(w_qkv_ref[...], grad_packed_ref[...], 1, 0)
    grad_stream = norm_columns_backward(
        x_ref[...].astype(F32), as_column(gain_ref[...]), inverse_ref[...], grad_normed
    )
    parts, groups, rows, _ = out_ref.shape
    grad_new = grad_ref[...].reshape(tokens, features).astype(F32)
    result = (grad_new + grad_stream.T).astype(BF16)
    here = tokens // (parts * rows)
    out_ref[:, :here] = result.reshape(parts, here, rows, features)
    out_ref[:, here:] = jnp.zeros((parts, groups - here, rows, features), BF16)


def run_space_stream(grad, x, inverse, grad_packed, gain, w_qkv, parts):
    features, tokens = x.shape
    rows = grad.shape[1]
    x, grad_packed = in_vmem(x, grad_packed)
    return call(
        space_stream,
        [((parts, tokens // (parts * rows) + 2, rows, features), BF16)],
        (grad, x, inverse, grad_packed, gain, w_qkv),
        4,
    )[0]


def unpack(
    incoming_ref, hidden_ref, space_qkv_ref, space_out_ref, time_qkv_ref, time_out_ref
):
    round_parts, _, stabs, features = incoming_ref.shape
    here = hidden_ref.shape[0]
    for block in range(round_parts):
        cols = slice(block * stabs, (block + 1) * stabs)
        hidden_ref[:, cols, :] = incoming_ref[block, :here]
    count = round_parts // 4
    for j in range(4):
        pieces = incoming_ref[j * count : (j + 1) * count, here:].astype(F32)
        pieces = pieces.reshape(count, here, 2, stabs, features)
        for kind, qkv_ref, out_ref in (
            (0, time_qkv_ref, time_out_ref),
            (1, space_qkv_ref, space_out_ref),
        ):
            block = pieces[:, :, kind].reshape(features, features)
            if j < 3:
                qkv_ref[:, j * features : (j + 1) * features] = block
            else:
                out_ref[...] = block


def exchange(values, axes):
    return lax.all_to_all(values, axes, split_axis=0, concat_axis=0, tiled=True)


def on_device(
    syndrome,
    basis_ids,
    coordinates,
    syndrome_table,
    basis_table,
    coord_table,
    round_table,
    gain_space,
    w_qkv_space,
    w_out_space,
    gain_time,
    w_qkv_time,
    w_out_time,
    grad_hidden,
):
    stab_parts = lax.axis_size("stab")
    round_parts = lax.axis_size("rounds")
    parts = stab_parts * round_parts
    rounds_here, stabs_here, features = grad_hidden.shape
    stabs_time = stabs_here // round_parts

    own_index = call(
        index_kernel,
        [((stab_parts, 5, stabs_here), jnp.int32)],
        (syndrome, basis_ids.reshape(1, stabs_here), coordinates),
        1,
    )[0]
    index = exchange(own_index, "stab")
    grad_chunks = grad_hidden.reshape(rounds_here, round_parts, stabs_time, features)
    grad_chunks, index = lax.optimization_barrier((jnp.swapaxes(grad_chunks, 0, 1), index))
    grad_time = exchange(grad_chunks, "rounds")

    gain_s = gain_space.reshape(1, features)
    gain_t = gain_time.reshape(1, features)
    tables = (syndrome_table, basis_table, coord_table, round_table)
    middle, x, normed, inverse, packed, attended, exps, totals = run_space_forward(
        index, tables, gain_s, w_qkv_space, w_out_space, parts
    )
    middle, grad_time = lax.optimization_barrier((middle, grad_time))
    middle_time = exchange(middle, ("stab", "rounds"))
    middle_time = middle_time.reshape(stab_parts, round_parts, stabs_time, features)
    grad_rows, grad_attended_t = run_time_grad(grad_time, w_out_time)
    grad_middle, normed_t, grad_packed_t, attended_t = run_time_block(
        middle_time, grad_time, grad_attended_t, gain_t, w_qkv_time
    )
    grad_space = exchange(grad_middle.reshape(parts, stabs_time, features), ("stab", "rounds"))
    hidden, time_pieces = run_time_rest(
        middle_time, normed_t, grad_packed_t, attended_t, grad_rows, w_out_time
    )
    grad_packed, pieces = run_space_backward(
        grad_space, normed, packed, attended, exps, totals, w_out_space, time_pieces
    )
    sources = exchange(pieces, ("rounds", "stab"))
    outgoing = run_space_stream(
        grad_space, x, inverse, grad_packed, gain_s, w_qkv_space, stab_parts
    )
    scaling = 1.0 / math.sqrt(parts * rounds_here * stabs_here)
    summed = (jnp.sum(sources.astype(F32), axis=0) * scaling).astype(BF16)
    here = outgoing.shape[1] - summed.shape[0]
    spread = jnp.broadcast_to(summed[None], (stab_parts,) + summed.shape)
    incoming = exchange(lax.dynamic_update_slice(outgoing, spread, (0, here, 0, 0)), "stab")
    grad_embedded = incoming[:, :here].reshape(grad_hidden.shape)
    gathered = incoming[:, here:].reshape(1, 2 * stab_parts, stabs_time, features)
    spread = jnp.broadcast_to(gathered, (round_parts,) + gathered.shape[1:])
    incoming = exchange(lax.dynamic_update_slice(hidden, spread, (0, stab_parts, 0, 0)), "rounds")
    hidden_home, *weights = call(
        unpack,
        [(grad_hidden.shape, BF16)]
        + [((features, 3 * features), F32), ((features, features), F32)] * 2,
        (incoming,),
        3,
    )
    return (hidden_home, grad_embedded) + tuple(weights)


def solution(mesh):
    in_specs = (
        P("rounds", "stab"),
        P("stab"),
        P(None, "stab"),
        P(),
        P(),
        P(),
        P("rounds", None),
        P(),
        P(),
        P(),
        P(),
        P(),
        P(),
        P("rounds", "stab", None),
    )
    out_specs = (P("rounds", "stab", None), P("rounds", "stab", None), P(), P(), P(), P())
    return jax.shard_map(
        on_device, mesh=mesh, in_specs=in_specs, out_specs=out_specs, check_vma=False
    )
```

```python
import math

import jax
import jax.numpy as jnp
from jax import lax
from jax.experimental import pallas as pl
from jax.experimental.pallas import tpu as pltpu
from jax.sharding import PartitionSpec as P

HEADS = 4
EPSILON = 1e-06
F32 = jnp.float32
BF16 = jnp.bfloat16

LEVELS = 128
ROW_AT, COLUMN_AT, BASIS_AT, SYNDROME_AT, ROUND_AT = 0, 48, 96, 104, 112


def dot(left, right, left_dim, right_dim):
    return lax.dot_general(
        left, right, (((left_dim,), (right_dim,)), ((), ())), preferred_element_type=F32
    )


def call(kernel, shapes, arguments, microseconds, scratch=(), megabytes=60, **grid):
    return pl.pallas_call(
        kernel,
        out_shape=[
            jax.ShapeDtypeStruct(*item) if isinstance(item, tuple) else item for item in shapes
        ],
        scratch_shapes=[pltpu.VMEM(*item) if isinstance(item, tuple) else item for item in scratch],
        compiler_params=pltpu.CompilerParams(vmem_limit_bytes=megabytes * 2**20),
        cost_estimate=pl.CostEstimate(
            flops=microseconds * 500_000_000,
            bytes_accessed=microseconds * 2_000_000,
            transcendentals=0,
        ),
        name=kernel.__name__,
        **grid,
    )(*arguments)


def in_hbm(*arrays):
    return [pltpu.with_memory_space_constraint(array, pltpu.HBM) for array in arrays]


def in_range(inverse_totals):
    least, most = jnp.min(inverse_totals), jnp.max(inverse_totals)
    return jnp.logical_and(least > 2.0**-30, most < 2.0**30)


def split_rows(row):
    terms = []
    for _ in range(3):
        terms.append(row.astype(BF16))
        row = row - terms[-1].astype(F32)
    zeros = jnp.zeros((16 - len(terms), row.shape[1]), BF16)
    return jnp.concatenate(terms + [zeros])


def as_column(gain):
    return jnp.broadcast_to(gain, (8, gain.shape[1])).T[:, :1]


def norm_columns(values, gain):
    inverse = lax.rsqrt(jnp.mean(values * values, axis=0, keepdims=True) + EPSILON)
    return (values * inverse * gain).astype(BF16), inverse


def norm_columns_backward(values, gain, inverse, grad_normed):
    gained = grad_normed * gain
    inner = jnp.mean(gained * values, axis=0, keepdims=True)
    return inverse * gained - values * (inverse * inverse * inverse) * inner


def store_blocks(ref, kind, grad_qkv, grad_out):
    features = grad_out.shape[0]
    blocks = [grad_qkv[:, j * features : (j + 1) * features] for j in range(3)] + [grad_out]
    count = ref.shape[0] // len(blocks)
    for j, block in enumerate(blocks):
        ref[j * count : (j + 1) * count, kind] = block.astype(BF16).reshape(
            count, ref.shape[2], features
        )


def index_kernel(syndrome_ref, basis_ref, coordinates_ref, index_ref):
    width = index_ref.shape[2]
    for block in range(index_ref.shape[0]):
        index_ref[block, 0:1, :] = syndrome_ref[block : block + 1, :] + SYNDROME_AT
        index_ref[block, 1:2, :] = basis_ref[...] + BASIS_AT
        index_ref[block, 2:3, :] = coordinates_ref[0:1, :] + ROW_AT
        index_ref[block, 3:4, :] = coordinates_ref[1:2, :] + COLUMN_AT
        index_ref[block, 4:5, :] = jnp.full((1, width), ROUND_AT + block, jnp.int32)


def space_forward(
    index_ref, syndrome_table_ref, basis_table_ref, coord_table_ref, round_table_ref,
    gain_ref, w_qkv_ref, w_out_ref,
    middle_ref, inverse_ref, attended_ref, total_ref, x_out, normed_out, packed_out, exps_out,
    table_ref, row_ref, onehot_ref, x_ref, normed_ref, packed_ref, exps_ref, sems,
):
    features, tokens = x_ref.shape
    depth = features // HEADS
    copies = [
        pltpu.make_async_copy(x_ref, x_out, sems.at[HEADS]),
        pltpu.make_async_copy(normed_ref, normed_out, sems.at[HEADS + 1]),
        pltpu.make_async_copy(packed_ref, packed_out, sems.at[HEADS + 2]),
    ]
    head_copies = [
        pltpu.make_async_copy(exps_ref.at[head], exps_out.at[head], sems.at[head])
        for head in range(HEADS)
    ]

    coords = coord_table_ref.shape[1]
    table_ref[...] = jnp.zeros(table_ref.shape, F32)
    table_ref[ROW_AT : ROW_AT + coords, :] = coord_table_ref[0].astype(F32)
    table_ref[COLUMN_AT : COLUMN_AT + coords, :] = coord_table_ref[1].astype(F32)
    table_ref[BASIS_AT : BASIS_AT + 2, :] = basis_table_ref[...].astype(F32)
    table_ref[SYNDROME_AT : SYNDROME_AT + 2, :] = syndrome_table_ref[...].astype(F32)
    rounds = round_table_ref.shape[0]
    table_ref[ROUND_AT : ROUND_AT + rounds, :] = round_table_ref[...].astype(F32)
    width = index_ref.shape[2]
    levels = lax.broadcasted_iota(jnp.int32, (LEVELS, width), 0)
    for block in range(index_ref.shape[0]):
        hit = levels == index_ref[block, 0:1, :]
        for kind in range(1, index_ref.shape[1]):
            hit = hit | (levels == index_ref[block, kind : kind + 1, :])
        onehot_ref[:, block * width : (block + 1) * width] = hit.astype(F32).astype(BF16)
    table = table_ref[...].astype(BF16)
    x = dot(table, onehot_ref[...], 0, 0).astype(BF16)
    x_ref[...] = x
    copies[0].start()
    normed, inverse = norm_columns(x.astype(F32), as_column(gain_ref[...]))
    normed_ref[...] = normed
    copies[1].start()
    inverse_ref[...] = inverse
    packed = dot(w_qkv_ref[...], normed, 0, 0)
    packed_ref[:features, :] = (packed[:features] * (math.log2(math.e) * depth**-0.5)).astype(BF16)
    packed_ref[features:, :] = packed[features:].astype(BF16)
    copies[2].start()
    row_ref[...] = dot(onehot_ref[...], table, 0, 0).astype(BF16)

    def operands(head):
        at = head * depth
        query = packed_ref[at : at + depth, :]
        keys = packed_ref[features + at : features + at + depth, :].T
        values = packed_ref[2 * features + at : 2 * features + at + depth, :]
        return query, keys, jnp.concatenate([values, jnp.ones((16, tokens), BF16)])

    def attend(head, values, cols):
        product = dot(values, exps_ref[head, :, cols], 1, 0)
        inverse_total = 1.0 / product[depth : depth + 1]
        total_ref[head, :, cols] = inverse_total
        attended_ref[head * depth : (head + 1) * depth, cols] = (
            product[:depth] * inverse_total
        ).astype(BF16)

    blocks = [slice(start, start + SPACE_BLOCK) for start in range(0, tokens, SPACE_BLOCK)]
    before = None
    for head in range(HEADS):
        query, keys, values = operands(head)
        for cols in blocks:
            for low in range(0, tokens, KEY_TILE):
                rows = slice(low, low + KEY_TILE)
                exps_ref[head, rows, cols] = jnp.exp2(
                    dot(keys[rows], query[:, cols], 1, 0)
                ).astype(BF16)
            if before is not None:
                attend(*before)
            before = head, values, cols
        head_copies[head].start()
    attend(*before)

    @pl.when(jnp.logical_not(in_range(total_ref[...])))
    def _():
        for copy in head_copies:
            copy.wait()
        for head in range(HEADS):
            query, keys, values = operands(head)
            for cols in blocks:
                scores = dot(keys, query[:, cols], 1, 0)
                peak = jnp.max(scores, axis=0, keepdims=True)
                exps_ref[head, :, cols] = jnp.exp2(scores - peak).astype(BF16)
                attend(head, values, cols)
            head_copies[head].start()

    branch = dot(attended_ref[...], w_out_ref[...], 0, 0)
    middle = (row_ref[...].astype(F32) + branch).astype(BF16)
    middle_ref[...] = middle.reshape(middle_ref.shape)
    for copy in head_copies + copies:
        copy.wait()


SPACE_BLOCK = 256
KEY_TILE = 128
LOADS = 4
VMEM = pl.BlockSpec(memory_space=pltpu.VMEM)
ANY = pl.BlockSpec(memory_space=pl.ANY)


def run_space_forward(index, tables, gain, w_qkv, w_out, chunks):
    tokens = index.shape[0] * index.shape[2]
    features = w_out.shape[0]
    shapes = [
        ((chunks, tokens // chunks, features), BF16),
        ((1, tokens), F32),
        ((features, tokens), BF16),
        ((HEADS, 1, tokens), F32),
        pltpu.HBM((features, tokens), BF16),
        pltpu.HBM((features, tokens), BF16),
        pltpu.HBM((3 * features, tokens), BF16),
        pltpu.HBM((HEADS, tokens, tokens), BF16),
    ]
    arguments = (index,) + tables + (gain, w_qkv, w_out)
    middle, inverse, attended, totals, x, normed, packed, exps = call(
        space_forward,
        shapes,
        arguments,
        10,
        scratch=[
            ((LEVELS, features), F32),
            ((tokens, features), BF16),
            ((LEVELS, tokens), BF16),
            ((features, tokens), BF16),
            ((features, tokens), BF16),
            ((3 * features, tokens), BF16),
            ((HEADS, tokens, tokens), BF16),
            pltpu.SemaphoreType.DMA((HEADS + 3,)),
        ],
        in_specs=[VMEM] * len(arguments),
        out_specs=[VMEM] * 4 + [ANY] * 4,
    )
    return middle, x, normed, inverse, packed, attended, exps, totals


def time_grad(grad_ref, w_out_ref, grad_row_ref, grad_attended_ref, grads_ref):
    round_parts, stab_parts, stabs, features = grad_ref.shape
    rounds = stab_parts * round_parts
    grad = grad_ref[...].astype(F32).reshape(rounds * stabs, features)
    lanes = grads_ref.shape[2]
    for part in range(features // lanes):
        half = slice(part * lanes, (part + 1) * lanes)
        grads_ref[part] = grad[:, half]
        for stab in range(stabs):
            cols = slice(stab * rounds, (stab + 1) * rounds)
            at = pl.ds(stab, rounds, stride=stabs)
            grad_row_ref[cols, half] = grads_ref[part, at, :].astype(BF16)
    grad_attended_ref[...] = dot(w_out_ref[...], grad_row_ref[...], 1, 1).astype(BF16)


def run_time_grad(grad, w_out):
    round_parts, stab_parts, stabs, features = grad.shape
    tokens = stab_parts * round_parts * stabs
    return call(
        time_grad,
        [((tokens, features), BF16), ((features, tokens), BF16)],
        (grad, w_out),
        3,
        scratch=[((features // 128, tokens, 128), F32)],
    )


def time_block(
    middle_ref, grad_in, grad_attended_in, gain_ref, w_qkv_ref,
    grad_middle_ref, normed_out, grad_packed_out, attended_out,
    grad_ref, grad_attended_ref, normed_ref, grad_packed_ref, attended_ref, x_ref, packed_ref,
    rows_ref, sems,
):
    stab_parts, round_parts, stabs, features = middle_ref.shape
    rounds = stab_parts * round_parts
    tokens = rounds * stabs
    depth = features // HEADS
    scale = depth**-0.5

    load_grad = pltpu.make_async_copy(grad_in, grad_ref, sems.at[3])
    load_attended = pltpu.make_async_copy(grad_attended_in, grad_attended_ref, sems.at[4])
    load_grad.start()
    load_attended.start()
    middle = jnp.swapaxes(middle_ref[...].astype(F32), 0, 1).reshape(tokens, features)
    lanes = rows_ref.shape[2]
    halves = [slice(part * lanes, (part + 1) * lanes) for part in range(features // lanes)]
    for part, half in enumerate(halves):
        rows_ref[part] = middle[:, half]
    for stab in range(stabs):
        cols = slice(stab * rounds, (stab + 1) * rounds)
        at = pl.ds(stab, rounds, stride=stabs)
        for part, half in enumerate(halves):
            x_ref[half, cols] = rows_ref[part, at, :].T
    x = x_ref[...]
    gain = as_column(gain_ref[...])
    normed, inverse = norm_columns(x, gain)
    normed_ref[...] = normed
    store_normed = pltpu.make_async_copy(normed_ref, normed_out, sems.at[0])
    store_normed.start()
    packed = dot(w_qkv_ref[...], normed, 0, 0)
    to_base_two = math.log2(math.e) * scale
    packed_ref[:features, :] = (packed[:features] * to_base_two).astype(BF16)
    packed_ref[features:, :] = packed[features:].astype(BF16)

    ones = jnp.ones((16, rounds), BF16)
    load_attended.wait()
    load_grad.wait()

    def some_stabs(step, carry):
        items = []
        for stab in range(TIME_GROUP):
            start = pl.multiple_of((step * TIME_GROUP + stab) * rounds, rounds)
            cols = pl.ds(start, rounds)
            items += [(head * depth, cols) for head in range(HEADS)]
        query = [packed_ref[at : at + depth, cols] for at, cols in items]
        keys = [packed_ref[features + at : features + at + depth, cols] for at, cols in items]
        values = [
            packed_ref[2 * features + at : 2 * features + at + depth, cols] for at, cols in items
        ]
        scores = [dot(k, q, 0, 0) for k, q in zip(keys, query)]
        exps = [
            jnp.exp2(each - jnp.max(each, axis=0, keepdims=True)).astype(BF16) for each in scores
        ]
        products = [dot(jnp.concatenate([v, ones]), e, 1, 0) for v, e in zip(values, exps)]
        grads, inners = [], []
        for (at, cols), product in zip(items, products):
            inverse_total = 1.0 / product[depth : depth + 1]
            attended = product[:depth] * inverse_total
            attended_ref[at : at + depth, cols] = attended.astype(BF16)
            grad = grad_attended_ref[at : at + depth, cols].astype(F32) * inverse_total
            inners.append(jnp.sum(grad * attended, axis=0, keepdims=True))
            grads.append(grad.astype(BF16))
        centred = [dot(v, g, 0, 0) - inner for v, g, inner in zip(values, grads, inners)]
        grad_scores = [(e.astype(F32) * c).astype(BF16) for e, c in zip(exps, centred)]
        for (at, cols), g, e in zip(items, grads, exps):
            grad_packed_ref[2 * features + at : 2 * features + at + depth, cols] = dot(
                g, e, 1, 1
            ).astype(BF16)
        for (at, cols), k, each in zip(items, keys, grad_scores):
            grad_packed_ref[at : at + depth, cols] = (dot(k, each, 1, 0) * scale).astype(BF16)
        for (at, cols), q, each in zip(items, query, grad_scores):
            grad_packed_ref[features + at : features + at + depth, cols] = (
                dot(q, each, 1, 1) * math.log(2.0)
            ).astype(BF16)
        return carry

    lax.fori_loop(0, stabs // TIME_GROUP, some_stabs, 0, unroll=TIME_UNROLL)
    store_attended = pltpu.make_async_copy(attended_ref, attended_out, sems.at[1])
    store_packed = pltpu.make_async_copy(grad_packed_ref, grad_packed_out, sems.at[2])
    store_attended.start()
    store_packed.start()

    grad_normed = dot(w_qkv_ref[...], grad_packed_ref[...], 1, 0)
    grad_stream = norm_columns_backward(x_ref[...], gain, inverse, grad_normed)
    for stab in range(stabs):
        cols = slice(stab * rounds, (stab + 1) * rounds)
        at = pl.ds(stab, rounds, stride=stabs)
        for part, half in enumerate(halves):
            rows_ref[part, at, :] = grad_stream[half, cols].T
    for part, half in enumerate(halves):
        grad_middle = rows_ref[part].reshape(round_parts, stab_parts, stabs, lanes)
        grad_middle = grad_middle + grad_ref[:, :, :, half].astype(F32)
        grad_middle_ref[:, :, :, half] = jnp.swapaxes(grad_middle, 0, 1).astype(BF16)
    store_normed.wait()
    store_attended.wait()
    store_packed.wait()


TIME_UNROLL = True
TIME_GROUP = 2


def run_time_block(middle, grad, grad_attended, gain, w_qkv):
    stab_parts, round_parts, stabs, features = middle.shape
    tokens = stab_parts * round_parts * stabs
    grad, grad_attended = in_hbm(grad, grad_attended)
    shapes = [
        (middle.shape, BF16),
        pltpu.HBM((features, tokens), BF16),
        pltpu.HBM((3 * features, tokens), BF16),
        pltpu.HBM((features, tokens), BF16),
    ]
    return call(
        time_block,
        shapes,
        (middle, grad, grad_attended, gain, w_qkv),
        10,
        scratch=[
            (grad.shape, BF16),
            (grad_attended.shape, BF16),
            ((features, tokens), BF16),
            ((3 * features, tokens), BF16),
            ((features, tokens), BF16),
            ((features, tokens), F32),
            ((3 * features, tokens), BF16),
            ((features // 128, tokens, 128), F32),
            pltpu.SemaphoreType.DMA((5,)),
        ],
        megabytes=24,
        in_specs=[VMEM, ANY, ANY, VMEM, VMEM],
        out_specs=[VMEM] + [ANY] * 3,
    )


def time_rest(
    middle_ref, normed_ref, grad_packed_ref, attended_ref, grad_row_ref, w_out_ref,
    hidden_ref, pieces_ref,
    rows_ref,
):
    stab_parts, round_parts, stabs, features = middle_ref.shape
    rounds = stab_parts * round_parts
    tokens = rounds * stabs
    lanes = rows_ref.shape[2]
    halves = [slice(part * lanes, (part + 1) * lanes) for part in range(features // lanes)]
    attended = attended_ref[...]
    branch = dot(attended, w_out_ref[...], 0, 0)
    middle = jnp.swapaxes(middle_ref[...].astype(F32), 0, 1).reshape(tokens, features)
    for part, half in enumerate(halves):
        rows_ref[part] = middle[:, half]
    for stab in range(stabs):
        cols = slice(stab * rounds, (stab + 1) * rounds)
        at = pl.ds(stab, rounds, stride=stabs)
        for part, half in enumerate(halves):
            rows_ref[part, at, :] = rows_ref[part, at, :] + branch[cols, half]
    for part, half in enumerate(halves):
        hidden = rows_ref[part].reshape(round_parts, stab_parts, stabs, lanes)
        hidden_ref[:, :stab_parts, :, half] = hidden.astype(BF16)
    groups = hidden_ref.shape[1] - stab_parts
    hidden_ref[:, stab_parts:] = jnp.zeros((round_parts, groups, stabs, features), BF16)
    store_blocks(
        pieces_ref,
        0,
        dot(normed_ref[...], grad_packed_ref[...], 1, 1),
        dot(attended, grad_row_ref[...], 1, 0),
    )


def run_time_rest(middle, normed, grad_packed, attended, grad_rows, w_out):
    features, tokens = normed.shape
    stab_parts, round_parts, stabs, _ = middle.shape
    parts = stab_parts * round_parts
    return call(
        time_rest,
        [
            ((round_parts, 3 * stab_parts, stabs, features), BF16),
            ((parts, 1, 4 * features // parts, features), BF16),
        ],
        (middle, normed, grad_packed, attended, grad_rows, w_out),
        5,
        scratch=[((features // 128, tokens, 128), F32)],
    )


def space_backward(
    grad_ref, total_ref, w_out_ref, packed_in, attended_in, normed_in, exps_in, time_in,
    grad_packed_out, pieces_out,
    grad_attended_ref, grad_packed_ref, pieces_ref, packed_ref, attended_ref, normed_ref,
    exps_ref, grad_scores_ref, sems, load_sems,
):
    features, tokens = attended_ref.shape
    depth = features // HEADS
    part = tokens // LOADS
    loads = [
        [
            pltpu.make_async_copy(
                exps_in.at[head, pl.ds(low * part, part)],
                exps_ref.at[head, pl.ds(low * part, part)],
                load_sems.at[head, low],
            )
            for low in range(LOADS)
        ]
        for head in range(HEADS)
    ]
    load_packed = pltpu.make_async_copy(packed_in, packed_ref, sems.at[0])
    load_attended = pltpu.make_async_copy(attended_in, attended_ref, sems.at[1])
    load_normed = pltpu.make_async_copy(normed_in, normed_ref, sems.at[HEADS])
    copy_time = pltpu.make_async_copy(time_in, pieces_ref.at[:, 0:1], sems.at[HEADS + 1])
    store_packed = pltpu.make_async_copy(grad_packed_ref, grad_packed_out, sems.at[HEADS + 2])
    store_pieces = pltpu.make_async_copy(pieces_ref, pieces_out, sems.at[HEADS + 3])
    load_packed.start()
    load_attended.start()
    for load in loads[0]:
        load.start()

    new = grad_ref[...].reshape(tokens, features)
    grad_attended_ref[...] = dot(w_out_ref[...], new, 1, 1).astype(BF16)
    load_packed.wait()
    load_attended.wait()
    for load in loads[0]:
        load.wait()
    for load in loads[1] + loads[2] + loads[3]:
        load.start()
    load_normed.start()
    copy_time.start()
    blocks = [slice(start, start + SPACE_BLOCK) for start in range(0, tokens, SPACE_BLOCK)]

    def finish(head, grad):
        at = head * depth
        keys = packed_ref[features + at : features + at + depth, :]
        query = packed_ref[at : at + depth, :]
        scores = grad_scores_ref[head % 2]
        grad_packed_ref[at : at + depth, :] = (dot(keys, scores, 1, 0) * depth**-0.5).astype(BF16)
        grad_packed_ref[features + at : features + at + depth, :] = (
            dot(scores, query.T, 1, 0).T * math.log(2.0)
        ).astype(BF16)
        grad_packed_ref[2 * features + at : 2 * features + at + depth, :] = dot(
            exps_ref[head], grad.T, 1, 0
        ).T.astype(BF16)

    before = None
    for head in range(HEADS):
        at = head * depth
        values = packed_ref[2 * features + at : 2 * features + at + depth, :]
        grad = grad_attended_ref[at : at + depth, :].astype(F32) * total_ref[head]
        inner = jnp.sum(
            grad * attended_ref[at : at + depth, :].astype(F32), axis=0, keepdims=True
        )
        grad = grad.astype(BF16)
        wide_grad = jnp.concatenate([grad, split_rows(inner)])
        wide_values = jnp.concatenate([values.T, jnp.full((tokens, 16), -1.0, BF16)], axis=1)
        if head > 0:
            for load in loads[head]:
                load.wait()
        for cols in blocks:
            for low in range(0, tokens, KEY_TILE):
                rows = slice(low, low + KEY_TILE)
                centred = dot(wide_values[rows], wide_grad[:, cols], 1, 0)
                grad_scores_ref[head % 2, rows, cols] = (
                    exps_ref[head, rows, cols].astype(F32) * centred
                ).astype(BF16)
        finish(head, grad)
    store_packed.start()
    load_normed.wait()
    store_blocks(
        pieces_ref,
        1,
        dot(normed_ref[...], grad_packed_ref[...], 1, 1),
        dot(attended_ref[...], new, 1, 0),
    )
    copy_time.wait()
    store_pieces.start()
    store_packed.wait()
    store_pieces.wait()


def run_space_backward(grad, normed, packed, attended, exps, totals, w_out, time_pieces):
    features, tokens = attended.shape
    parts, _, rows, _ = time_pieces.shape
    packed, attended, normed, exps, time_pieces = in_hbm(
        packed, attended, normed, exps, time_pieces
    )
    shapes = [pltpu.HBM((3 * features, tokens), BF16), ((parts, 2, rows, features), BF16)]
    return call(
        space_backward,
        shapes,
        (grad, totals, w_out, packed, attended, normed, exps, time_pieces),
        14,
        scratch=[
            ((features, tokens), BF16),
            ((3 * features, tokens), BF16),
            ((parts, 2, rows, features), BF16),
            ((3 * features, tokens), BF16),
            ((features, tokens), BF16),
            ((features, tokens), BF16),
            ((HEADS, tokens, tokens), BF16),
            ((2, tokens, tokens), BF16),
            pltpu.SemaphoreType.DMA((HEADS + 4,)),
            pltpu.SemaphoreType.DMA((HEADS, LOADS)),
        ],
        megabytes=32,
        in_specs=[VMEM] * 3 + [ANY] * 5,
        out_specs=[ANY] * 2,
    )


def space_stream(
    grad_ref, x_ref, inverse_ref, grad_packed_ref, gain_ref, w_qkv_ref, out_ref
):
    features, tokens = x_ref.shape
    grad_normed = dot(w_qkv_ref[...], grad_packed_ref[...], 1, 0)
    grad_stream = norm_columns_backward(
        x_ref[...].astype(F32), as_column(gain_ref[...]), inverse_ref[...], grad_normed
    )
    parts, groups, rows, _ = out_ref.shape
    grad_new = grad_ref[...].reshape(tokens, features).astype(F32)
    result = (grad_new + grad_stream.T).astype(BF16)
    here = tokens // (parts * rows)
    out_ref[:, :here] = result.reshape(parts, here, rows, features)
    out_ref[:, here:] = jnp.zeros((parts, groups - here, rows, features), BF16)


def run_space_stream(grad, x, inverse, grad_packed, gain, w_qkv, parts):
    features, tokens = x.shape
    rows = grad.shape[1]
    return call(
        space_stream,
        [((parts, tokens // (parts * rows) + 2, rows, features), BF16)],
        (grad, x, inverse, grad_packed, gain, w_qkv),
        4,
    )[0]


def unpack(
    incoming_ref, hidden_ref, space_qkv_ref, space_out_ref, time_qkv_ref, time_out_ref
):
    round_parts, _, stabs, features = incoming_ref.shape
    here = hidden_ref.shape[0]
    for block in range(round_parts):
        cols = slice(block * stabs, (block + 1) * stabs)
        hidden_ref[:, cols, :] = incoming_ref[block, :here]
    count = round_parts // 4
    for j in range(4):
        pieces = incoming_ref[j * count : (j + 1) * count, here:].astype(F32)
        pieces = pieces.reshape(count, here, 2, stabs, features)
        for kind, qkv_ref, out_ref in (
            (0, time_qkv_ref, time_out_ref),
            (1, space_qkv_ref, space_out_ref),
        ):
            block = pieces[:, :, kind].reshape(features, features)
            if j < 3:
                qkv_ref[:, j * features : (j + 1) * features] = block
            else:
                out_ref[...] = block


def exchange(values, axes):
    return lax.all_to_all(values, axes, split_axis=0, concat_axis=0, tiled=True)


def on_device(
    syndrome,
    basis_ids,
    coordinates,
    syndrome_table,
    basis_table,
    coord_table,
    round_table,
    gain_space,
    w_qkv_space,
    w_out_space,
    gain_time,
    w_qkv_time,
    w_out_time,
    grad_hidden,
):
    stab_parts = lax.axis_size("stab")
    round_parts = lax.axis_size("rounds")
    parts = stab_parts * round_parts
    rounds_here, stabs_here, features = grad_hidden.shape
    stabs_time = stabs_here // round_parts

    own_index = call(
        index_kernel,
        [((stab_parts, 5, stabs_here), jnp.int32)],
        (syndrome, basis_ids.reshape(1, stabs_here), coordinates),
        1,
    )[0]
    index = exchange(own_index, "stab")
    grad_chunks = grad_hidden.reshape(rounds_here, round_parts, stabs_time, features)
    grad_chunks, index = lax.optimization_barrier((jnp.swapaxes(grad_chunks, 0, 1), index))
    grad_time = exchange(grad_chunks, "rounds")

    gain_s = gain_space.reshape(1, features)
    gain_t = gain_time.reshape(1, features)
    tables = (syndrome_table, basis_table, coord_table, round_table)
    middle, x, normed, inverse, packed, attended, exps, totals = run_space_forward(
        index, tables, gain_s, w_qkv_space, w_out_space, parts
    )
    middle, grad_time = lax.optimization_barrier((middle, grad_time))
    middle_time = exchange(middle, ("stab", "rounds"))
    middle_time = middle_time.reshape(stab_parts, round_parts, stabs_time, features)
    grad_rows, grad_attended_t = run_time_grad(grad_time, w_out_time)
    grad_middle, normed_t, grad_packed_t, attended_t = run_time_block(
        middle_time, grad_time, grad_attended_t, gain_t, w_qkv_time
    )
    grad_space = exchange(grad_middle.reshape(parts, stabs_time, features), ("stab", "rounds"))
    hidden, time_pieces = run_time_rest(
        middle_time, normed_t, grad_packed_t, attended_t, grad_rows, w_out_time
    )
    grad_packed, pieces = run_space_backward(
        grad_space, normed, packed, attended, exps, totals, w_out_space, time_pieces
    )
    sources = exchange(pieces, ("rounds", "stab"))
    outgoing = run_space_stream(
        grad_space, x, inverse, grad_packed, gain_s, w_qkv_space, stab_parts
    )
    scaling = 1.0 / math.sqrt(parts * rounds_here * stabs_here)
    summed = (jnp.sum(sources.astype(F32), axis=0) * scaling).astype(BF16)
    here = outgoing.shape[1] - summed.shape[0]
    spread = jnp.broadcast_to(summed[None], (stab_parts,) + summed.shape)
    incoming = exchange(lax.dynamic_update_slice(outgoing, spread, (0, here, 0, 0)), "stab")
    grad_embedded = incoming[:, :here].reshape(grad_hidden.shape)
    gathered = incoming[:, here:].reshape(1, 2 * stab_parts, stabs_time, features)
    spread = jnp.broadcast_to(gathered, (round_parts,) + gathered.shape[1:])
    incoming = exchange(lax.dynamic_update_slice(hidden, spread, (0, stab_parts, 0, 0)), "rounds")
    hidden_home, *weights = call(
        unpack,
        [(grad_hidden.shape, BF16)]
        + [((features, 3 * features), F32), ((features, features), F32)] * 2,
        (incoming,),
        3,
        megabytes=20,
    )
    return (hidden_home, grad_embedded) + tuple(weights)


def solution(mesh):
    in_specs = (
        P("rounds", "stab"),
        P("stab"),
        P(None, "stab"),
        P(),
        P(),
        P(),
        P("rounds", None),
        P(),
        P(),
        P(),
        P(),
        P(),
        P(),
        P("rounds", "stab", None),
    )
    out_specs = (P("rounds", "stab", None), P("rounds", "stab", None), P(), P(), P(), P())
    return jax.shard_map(
        on_device, mesh=mesh, in_specs=in_specs, out_specs=out_specs, check_vma=False
    )
```

```python
import math

import jax
import jax.numpy as jnp
from jax import lax
from jax.experimental import pallas as pl
from jax.experimental.pallas import tpu as pltpu
from jax.sharding import PartitionSpec as P

HEADS = 4
EPSILON = 1e-06
F32 = jnp.float32
BF16 = jnp.bfloat16

LEVELS = 128
ROW_AT, COLUMN_AT, BASIS_AT, SYNDROME_AT, ROUND_AT = 0, 48, 96, 104, 112


def dot(left, right, left_dim, right_dim):
    return lax.dot_general(
        left, right, (((left_dim,), (right_dim,)), ((), ())), preferred_element_type=F32
    )


def call(kernel, shapes, arguments, microseconds, scratch=(), megabytes=60, **grid):
    return pl.pallas_call(
        kernel,
        out_shape=[
            jax.ShapeDtypeStruct(*item) if isinstance(item, tuple) else item for item in shapes
        ],
        scratch_shapes=[pltpu.VMEM(*item) if isinstance(item, tuple) else item for item in scratch],
        compiler_params=pltpu.CompilerParams(vmem_limit_bytes=megabytes * 2**20),
        cost_estimate=pl.CostEstimate(
            flops=microseconds * 500_000_000,
            bytes_accessed=microseconds * 2_000_000,
            transcendentals=0,
        ),
        name=kernel.__name__,
        **grid,
    )(*arguments)


def in_hbm(*arrays):
    return [pltpu.with_memory_space_constraint(array, pltpu.HBM) for array in arrays]


def in_range(inverse_totals):
    least, most = jnp.min(inverse_totals), jnp.max(inverse_totals)
    return jnp.logical_and(least > 2.0**-30, most < 2.0**30)


def split_rows(row):
    terms = []
    for _ in range(3):
        terms.append(row.astype(BF16))
        row = row - terms[-1].astype(F32)
    zeros = jnp.zeros((16 - len(terms), row.shape[1]), BF16)
    return jnp.concatenate(terms + [zeros])


def as_column(gain):
    return jnp.broadcast_to(gain, (8, gain.shape[1])).T[:, :1]


def norm_columns(values, gain):
    inverse = lax.rsqrt(jnp.mean(values * values, axis=0, keepdims=True) + EPSILON)
    return (values * inverse * gain).astype(BF16), inverse


def norm_columns_backward(values, gain, inverse, grad_normed):
    gained = grad_normed * gain
    inner = jnp.mean(gained * values, axis=0, keepdims=True)
    return inverse * gained - values * (inverse * inverse * inverse) * inner


def store_blocks(ref, kind, grad_qkv, grad_out):
    features = grad_out.shape[0]
    blocks = [grad_qkv[:, j * features : (j + 1) * features] for j in range(3)] + [grad_out]
    count = ref.shape[0] // len(blocks)
    for j, block in enumerate(blocks):
        ref[j * count : (j + 1) * count, kind] = block.astype(BF16).reshape(
            count, ref.shape[2], features
        )


def index_kernel(syndrome_ref, basis_ref, coordinates_ref, index_ref):
    width = index_ref.shape[2]
    for block in range(index_ref.shape[0]):
        index_ref[block, 0:1, :] = syndrome_ref[block : block + 1, :] + SYNDROME_AT
        index_ref[block, 1:2, :] = basis_ref[...] + BASIS_AT
        index_ref[block, 2:3, :] = coordinates_ref[0:1, :] + ROW_AT
        index_ref[block, 3:4, :] = coordinates_ref[1:2, :] + COLUMN_AT
        index_ref[block, 4:5, :] = jnp.full((1, width), ROUND_AT + block, jnp.int32)


def space_forward(
    index_ref, syndrome_table_ref, basis_table_ref, coord_table_ref, round_table_ref,
    gain_ref, w_qkv_ref, w_out_ref,
    middle_ref, inverse_ref, attended_ref, total_ref, x_out, normed_out, packed_out, exps_out,
    table_ref, row_ref, onehot_ref, x_ref, normed_ref, packed_ref, exps_ref, sems,
):
    features, tokens = x_ref.shape
    depth = features // HEADS
    copies = [
        pltpu.make_async_copy(x_ref, x_out, sems.at[HEADS]),
        pltpu.make_async_copy(normed_ref, normed_out, sems.at[HEADS + 1]),
        pltpu.make_async_copy(packed_ref, packed_out, sems.at[HEADS + 2]),
    ]
    head_copies = [
        pltpu.make_async_copy(exps_ref.at[head], exps_out.at[head], sems.at[head])
        for head in range(HEADS)
    ]

    coords = coord_table_ref.shape[1]
    table_ref[...] = jnp.zeros(table_ref.shape, F32)
    table_ref[ROW_AT : ROW_AT + coords, :] = coord_table_ref[0].astype(F32)
    table_ref[COLUMN_AT : COLUMN_AT + coords, :] = coord_table_ref[1].astype(F32)
    table_ref[BASIS_AT : BASIS_AT + 2, :] = basis_table_ref[...].astype(F32)
    table_ref[SYNDROME_AT : SYNDROME_AT + 2, :] = syndrome_table_ref[...].astype(F32)
    rounds = round_table_ref.shape[0]
    table_ref[ROUND_AT : ROUND_AT + rounds, :] = round_table_ref[...].astype(F32)
    width = index_ref.shape[2]
    levels = lax.broadcasted_iota(jnp.int32, (LEVELS, width), 0)
    for block in range(index_ref.shape[0]):
        hit = levels == index_ref[block, 0:1, :]
        for kind in range(1, index_ref.shape[1]):
            hit = hit | (levels == index_ref[block, kind : kind + 1, :])
        onehot_ref[:, block * width : (block + 1) * width] = hit.astype(F32).astype(BF16)
    table = table_ref[...].astype(BF16)
    x = dot(table, onehot_ref[...], 0, 0).astype(BF16)
    x_ref[...] = x
    copies[0].start()
    normed, inverse = norm_columns(x.astype(F32), as_column(gain_ref[...]))
    normed_ref[...] = normed
    copies[1].start()
    inverse_ref[...] = inverse
    packed = dot(w_qkv_ref[...], normed, 0, 0)
    packed_ref[:features, :] = (packed[:features] * (math.log2(math.e) * depth**-0.5)).astype(BF16)
    packed_ref[features:, :] = packed[features:].astype(BF16)
    copies[2].start()
    row_ref[...] = dot(onehot_ref[...], table, 0, 0).astype(BF16)

    def operands(head):
        at = head * depth
        query = packed_ref[at : at + depth, :]
        keys = packed_ref[features + at : features + at + depth, :].T
        values = packed_ref[2 * features + at : 2 * features + at + depth, :]
        return query, keys, jnp.concatenate([values, jnp.ones((16, tokens), BF16)])

    def attend(head, values, cols):
        product = dot(values, exps_ref[head, :, cols], 1, 0)
        inverse_total = 1.0 / product[depth : depth + 1]
        total_ref[head, :, cols] = inverse_total
        attended_ref[head * depth : (head + 1) * depth, cols] = (
            product[:depth] * inverse_total
        ).astype(BF16)

    blocks = [slice(start, start + SPACE_BLOCK) for start in range(0, tokens, SPACE_BLOCK)]
    before = None
    for head in range(HEADS):
        query, keys, values = operands(head)
        for cols in blocks:
            for low in range(0, tokens, KEY_TILE):
                rows = slice(low, low + KEY_TILE)
                exps_ref[head, rows, cols] = jnp.exp2(
                    dot(keys[rows], query[:, cols], 1, 0)
                ).astype(BF16)
            if before is not None:
                attend(*before)
            before = head, values, cols
        head_copies[head].start()
    attend(*before)

    @pl.when(jnp.logical_not(in_range(total_ref[...])))
    def _():
        for copy in head_copies:
            copy.wait()
        for head in range(HEADS):
            query, keys, values = operands(head)
            for cols in blocks:
                scores = dot(keys, query[:, cols], 1, 0)
                peak = jnp.max(scores, axis=0, keepdims=True)
                exps_ref[head, :, cols] = jnp.exp2(scores - peak).astype(BF16)
                attend(head, values, cols)
            head_copies[head].start()

    branch = dot(attended_ref[...], w_out_ref[...], 0, 0)
    middle = (row_ref[...].astype(F32) + branch).astype(BF16)
    middle_ref[...] = middle.reshape(middle_ref.shape)
    for copy in head_copies + copies:
        copy.wait()


SPACE_BLOCK = 256
KEY_TILE = 128
LOADS = 4
VMEM = pl.BlockSpec(memory_space=pltpu.VMEM)
ANY = pl.BlockSpec(memory_space=pl.ANY)


def run_space_forward(index, tables, gain, w_qkv, w_out, chunks):
    tokens = index.shape[0] * index.shape[2]
    features = w_out.shape[0]
    shapes = [
        ((chunks, tokens // chunks, features), BF16),
        ((1, tokens), F32),
        ((features, tokens), BF16),
        ((HEADS, 1, tokens), F32),
        pltpu.HBM((features, tokens), BF16),
        pltpu.HBM((features, tokens), BF16),
        pltpu.HBM((3 * features, tokens), BF16),
        pltpu.HBM((HEADS, tokens, tokens), BF16),
    ]
    arguments = (index,) + tables + (gain, w_qkv, w_out)
    middle, inverse, attended, totals, x, normed, packed, exps = call(
        space_forward,
        shapes,
        arguments,
        10,
        scratch=[
            ((LEVELS, features), F32),
            ((tokens, features), BF16),
            ((LEVELS, tokens), BF16),
            ((features, tokens), BF16),
            ((features, tokens), BF16),
            ((3 * features, tokens), BF16),
            ((HEADS, tokens, tokens), BF16),
            pltpu.SemaphoreType.DMA((HEADS + 3,)),
        ],
        in_specs=[VMEM] * len(arguments),
        out_specs=[VMEM] * 4 + [ANY] * 4,
    )
    return middle, x, normed, inverse, packed, attended, exps, totals


def time_grad(grad_ref, w_out_ref, grad_row_ref, grad_attended_ref, grads_ref):
    round_parts, stab_parts, stabs, features = grad_ref.shape
    rounds = stab_parts * round_parts
    grad = grad_ref[...].astype(F32).reshape(rounds * stabs, features)
    lanes = grads_ref.shape[2]
    for part in range(features // lanes):
        half = slice(part * lanes, (part + 1) * lanes)
        grads_ref[part] = grad[:, half]
        for stab in range(stabs):
            cols = slice(stab * rounds, (stab + 1) * rounds)
            at = pl.ds(stab, rounds, stride=stabs)
            grad_row_ref[cols, half] = grads_ref[part, at, :].astype(BF16)
    grad_attended_ref[...] = dot(w_out_ref[...], grad_row_ref[...], 1, 1).astype(BF16)


def run_time_grad(grad, w_out):
    round_parts, stab_parts, stabs, features = grad.shape
    tokens = stab_parts * round_parts * stabs
    return call(
        time_grad,
        [((tokens, features), BF16), ((features, tokens), BF16)],
        (grad, w_out),
        3,
        scratch=[((features // 128, tokens, 128), F32)],
    )


def time_block(
    middle_ref, grad_in, grad_attended_in, gain_ref, w_qkv_ref,
    grad_middle_ref, normed_out, grad_packed_out, attended_out,
    grad_ref, grad_attended_ref, normed_ref, grad_packed_ref, attended_ref, x_ref, packed_ref,
    rows_ref, sems,
):
    stab_parts, round_parts, stabs, features = middle_ref.shape
    rounds = stab_parts * round_parts
    tokens = rounds * stabs
    depth = features // HEADS
    scale = depth**-0.5

    load_grad = pltpu.make_async_copy(grad_in, grad_ref, sems.at[3])
    load_attended = pltpu.make_async_copy(grad_attended_in, grad_attended_ref, sems.at[4])
    load_grad.start()
    load_attended.start()
    middle = jnp.swapaxes(middle_ref[...].astype(F32), 0, 1).reshape(tokens, features)
    lanes = rows_ref.shape[2]
    halves = [slice(part * lanes, (part + 1) * lanes) for part in range(features // lanes)]
    for part, half in enumerate(halves):
        rows_ref[part] = middle[:, half]
    for stab in range(stabs):
        cols = slice(stab * rounds, (stab + 1) * rounds)
        at = pl.ds(stab, rounds, stride=stabs)
        for part, half in enumerate(halves):
            x_ref[half, cols] = rows_ref[part, at, :].T
    x = x_ref[...]
    gain = as_column(gain_ref[...])
    normed, inverse = norm_columns(x, gain)
    normed_ref[...] = normed
    store_normed = pltpu.make_async_copy(normed_ref, normed_out, sems.at[0])
    store_normed.start()
    packed = dot(w_qkv_ref[...], normed, 0, 0)
    to_base_two = math.log2(math.e) * scale
    packed_ref[:features, :] = (packed[:features] * to_base_two).astype(BF16)
    packed_ref[features:, :] = packed[features:].astype(BF16)

    ones = jnp.ones((16, rounds), BF16)
    load_attended.wait()
    load_grad.wait()

    def some_stabs(step, carry):
        items = []
        for stab in range(TIME_GROUP):
            start = pl.multiple_of((step * TIME_GROUP + stab) * rounds, rounds)
            cols = pl.ds(start, rounds)
            items += [(head * depth, cols) for head in range(HEADS)]
        query = [packed_ref[at : at + depth, cols] for at, cols in items]
        keys = [packed_ref[features + at : features + at + depth, cols] for at, cols in items]
        values = [
            packed_ref[2 * features + at : 2 * features + at + depth, cols] for at, cols in items
        ]
        scores = [dot(k, q, 0, 0) for k, q in zip(keys, query)]
        exps = [
            jnp.exp2(each - jnp.max(each, axis=0, keepdims=True)).astype(BF16) for each in scores
        ]
        products = [dot(jnp.concatenate([v, ones]), e, 1, 0) for v, e in zip(values, exps)]
        grads, inners = [], []
        for (at, cols), product in zip(items, products):
            inverse_total = 1.0 / product[depth : depth + 1]
            attended = product[:depth] * inverse_total
            attended_ref[at : at + depth, cols] = attended.astype(BF16)
            grad = grad_attended_ref[at : at + depth, cols].astype(F32) * inverse_total
            inners.append(jnp.sum(grad * attended, axis=0, keepdims=True))
            grads.append(grad.astype(BF16))
        centred = [dot(v, g, 0, 0) - inner for v, g, inner in zip(values, grads, inners)]
        grad_scores = [(e.astype(F32) * c).astype(BF16) for e, c in zip(exps, centred)]
        for (at, cols), g, e in zip(items, grads, exps):
            grad_packed_ref[2 * features + at : 2 * features + at + depth, cols] = dot(
                g, e, 1, 1
            ).astype(BF16)
        for (at, cols), k, each in zip(items, keys, grad_scores):
            grad_packed_ref[at : at + depth, cols] = (dot(k, each, 1, 0) * scale).astype(BF16)
        for (at, cols), q, each in zip(items, query, grad_scores):
            grad_packed_ref[features + at : features + at + depth, cols] = (
                dot(q, each, 1, 1) * math.log(2.0)
            ).astype(BF16)
        return carry

    lax.fori_loop(0, stabs // TIME_GROUP, some_stabs, 0, unroll=TIME_UNROLL)
    store_attended = pltpu.make_async_copy(attended_ref, attended_out, sems.at[1])
    store_packed = pltpu.make_async_copy(grad_packed_ref, grad_packed_out, sems.at[2])
    store_attended.start()
    store_packed.start()

    grad_normed = dot(w_qkv_ref[...], grad_packed_ref[...], 1, 0)
    grad_stream = norm_columns_backward(x_ref[...], gain, inverse, grad_normed)
    for stab in range(stabs):
        cols = slice(stab * rounds, (stab + 1) * rounds)
        at = pl.ds(stab, rounds, stride=stabs)
        for part, half in enumerate(halves):
            rows_ref[part, at, :] = grad_stream[half, cols].T
    for part, half in enumerate(halves):
        grad_middle = rows_ref[part].reshape(round_parts, stab_parts, stabs, lanes)
        grad_middle = grad_middle + grad_ref[:, :, :, half].astype(F32)
        grad_middle_ref[:, :, :, half] = jnp.swapaxes(grad_middle, 0, 1).astype(BF16)
    store_normed.wait()
    store_attended.wait()
    store_packed.wait()


TIME_UNROLL = True
TIME_GROUP = 2


def run_time_block(middle, grad, grad_attended, gain, w_qkv):
    stab_parts, round_parts, stabs, features = middle.shape
    tokens = stab_parts * round_parts * stabs
    grad, grad_attended = in_hbm(grad, grad_attended)
    shapes = [
        (middle.shape, BF16),
        pltpu.HBM((features, tokens), BF16),
        pltpu.HBM((3 * features, tokens), BF16),
        pltpu.HBM((features, tokens), BF16),
    ]
    return call(
        time_block,
        shapes,
        (middle, grad, grad_attended, gain, w_qkv),
        10,
        scratch=[
            (grad.shape, BF16),
            (grad_attended.shape, BF16),
            ((features, tokens), BF16),
            ((3 * features, tokens), BF16),
            ((features, tokens), BF16),
            ((features, tokens), F32),
            ((3 * features, tokens), BF16),
            ((features // 128, tokens, 128), F32),
            pltpu.SemaphoreType.DMA((5,)),
        ],
        megabytes=24,
        in_specs=[VMEM, ANY, ANY, VMEM, VMEM],
        out_specs=[VMEM] + [ANY] * 3,
    )


def time_rest(
    middle_ref, normed_ref, grad_packed_ref, attended_ref, grad_row_ref, w_out_ref,
    hidden_ref, pieces_ref,
    rows_ref,
):
    stab_parts, round_parts, stabs, features = middle_ref.shape
    rounds = stab_parts * round_parts
    tokens = rounds * stabs
    lanes = rows_ref.shape[2]
    halves = [slice(part * lanes, (part + 1) * lanes) for part in range(features // lanes)]
    attended = attended_ref[...]
    branch = dot(attended, w_out_ref[...], 0, 0)
    middle = jnp.swapaxes(middle_ref[...].astype(F32), 0, 1).reshape(tokens, features)
    for part, half in enumerate(halves):
        rows_ref[part] = middle[:, half]
    for stab in range(stabs):
        cols = slice(stab * rounds, (stab + 1) * rounds)
        at = pl.ds(stab, rounds, stride=stabs)
        for part, half in enumerate(halves):
            rows_ref[part, at, :] = rows_ref[part, at, :] + branch[cols, half]
    for part, half in enumerate(halves):
        hidden = rows_ref[part].reshape(round_parts, stab_parts, stabs, lanes)
        hidden_ref[:, :, :, half] = hidden.astype(BF16)
    store_blocks(
        pieces_ref,
        0,
        dot(normed_ref[...], grad_packed_ref[...], 1, 1),
        dot(attended, grad_row_ref[...], 1, 0),
    )


def run_time_rest(middle, normed, grad_packed, attended, grad_rows, w_out):
    features, tokens = normed.shape
    stab_parts, round_parts, stabs, _ = middle.shape
    parts = stab_parts * round_parts
    return call(
        time_rest,
        [
            ((round_parts, stab_parts, stabs, features), BF16),
            ((parts, 1, 4 * features // parts, features), BF16),
        ],
        (middle, normed, grad_packed, attended, grad_rows, w_out),
        5,
        scratch=[((features // 128, tokens, 128), F32)],
    )


def space_backward(
    grad_ref, total_ref, w_out_ref, packed_in, attended_in, normed_in, exps_in, time_in,
    grad_packed_out, pieces_out,
    grad_attended_ref, grad_packed_ref, pieces_ref, packed_ref, attended_ref, normed_ref,
    exps_ref, grad_scores_ref, sems, load_sems,
):
    features, tokens = attended_ref.shape
    depth = features // HEADS
    part = tokens // LOADS
    loads = [
        [
            pltpu.make_async_copy(
                exps_in.at[head, pl.ds(low * part, part)],
                exps_ref.at[head, pl.ds(low * part, part)],
                load_sems.at[head, low],
            )
            for low in range(LOADS)
        ]
        for head in range(HEADS)
    ]
    load_packed = pltpu.make_async_copy(packed_in, packed_ref, sems.at[0])
    load_attended = pltpu.make_async_copy(attended_in, attended_ref, sems.at[1])
    load_normed = pltpu.make_async_copy(normed_in, normed_ref, sems.at[HEADS])
    copy_time = pltpu.make_async_copy(time_in, pieces_ref.at[:, 0:1], sems.at[HEADS + 1])
    store_packed = pltpu.make_async_copy(grad_packed_ref, grad_packed_out, sems.at[HEADS + 2])
    store_pieces = pltpu.make_async_copy(pieces_ref, pieces_out, sems.at[HEADS + 3])
    load_packed.start()
    load_attended.start()
    for load in loads[0]:
        load.start()

    new = grad_ref[...].reshape(tokens, features)
    grad_attended_ref[...] = dot(w_out_ref[...], new, 1, 1).astype(BF16)
    load_packed.wait()
    load_attended.wait()
    for load in loads[0]:
        load.wait()
    for load in loads[1] + loads[2] + loads[3]:
        load.start()
    load_normed.start()
    copy_time.start()
    blocks = [slice(start, start + SPACE_BLOCK) for start in range(0, tokens, SPACE_BLOCK)]

    def finish(head, grad):
        at = head * depth
        keys = packed_ref[features + at : features + at + depth, :]
        query = packed_ref[at : at + depth, :]
        scores = grad_scores_ref[head % 2]
        grad_packed_ref[at : at + depth, :] = (dot(keys, scores, 1, 0) * depth**-0.5).astype(BF16)
        grad_packed_ref[features + at : features + at + depth, :] = (
            dot(scores, query.T, 1, 0).T * math.log(2.0)
        ).astype(BF16)
        grad_packed_ref[2 * features + at : 2 * features + at + depth, :] = dot(
            exps_ref[head], grad.T, 1, 0
        ).T.astype(BF16)

    before = None
    for head in range(HEADS):
        at = head * depth
        values = packed_ref[2 * features + at : 2 * features + at + depth, :]
        grad = grad_attended_ref[at : at + depth, :].astype(F32) * total_ref[head]
        inner = jnp.sum(
            grad * attended_ref[at : at + depth, :].astype(F32), axis=0, keepdims=True
        )
        grad = grad.astype(BF16)
        wide_grad = jnp.concatenate([grad, split_rows(inner)])
        wide_values = jnp.concatenate([values.T, jnp.full((tokens, 16), -1.0, BF16)], axis=1)
        if head > 0:
            for load in loads[head]:
                load.wait()
        for cols in blocks:
            for low in range(0, tokens, KEY_TILE):
                rows = slice(low, low + KEY_TILE)
                centred = dot(wide_values[rows], wide_grad[:, cols], 1, 0)
                grad_scores_ref[head % 2, rows, cols] = (
                    exps_ref[head, rows, cols].astype(F32) * centred
                ).astype(BF16)
        finish(head, grad)
    store_packed.start()
    load_normed.wait()
    store_blocks(
        pieces_ref,
        1,
        dot(normed_ref[...], grad_packed_ref[...], 1, 1),
        dot(attended_ref[...], new, 1, 0),
    )
    copy_time.wait()
    store_pieces.start()
    store_packed.wait()
    store_pieces.wait()


def run_space_backward(grad, normed, packed, attended, exps, totals, w_out, time_pieces):
    features, tokens = attended.shape
    parts, _, rows, _ = time_pieces.shape
    packed, attended, normed, exps, time_pieces = in_hbm(
        packed, attended, normed, exps, time_pieces
    )
    shapes = [pltpu.HBM((3 * features, tokens), BF16), ((parts, 2, rows, features), BF16)]
    return call(
        space_backward,
        shapes,
        (grad, totals, w_out, packed, attended, normed, exps, time_pieces),
        14,
        scratch=[
            ((features, tokens), BF16),
            ((3 * features, tokens), BF16),
            ((parts, 2, rows, features), BF16),
            ((3 * features, tokens), BF16),
            ((features, tokens), BF16),
            ((features, tokens), BF16),
            ((HEADS, tokens, tokens), BF16),
            ((2, tokens, tokens), BF16),
            pltpu.SemaphoreType.DMA((HEADS + 4,)),
            pltpu.SemaphoreType.DMA((HEADS, LOADS)),
        ],
        megabytes=32,
        in_specs=[VMEM] * 3 + [ANY] * 5,
        out_specs=[ANY] * 2,
    )


def space_stream(
    me_ref, grad_ref, x_ref, inverse_ref, grad_packed_ref, gain_ref, w_qkv_ref, *rest
):
    out_refs, rows_ref = rest[:-1], rest[-1]
    features, tokens = x_ref.shape
    grad_normed = dot(w_qkv_ref[...], grad_packed_ref[...], 1, 0)
    grad_stream = norm_columns_backward(
        x_ref[...].astype(F32), as_column(gain_ref[...]), inverse_ref[...], grad_normed
    )
    grad_new = grad_ref[...].reshape(tokens, features).astype(F32)
    rows_ref[...] = (grad_new + grad_stream.T).astype(BF16)
    rows = tokens // len(out_refs)
    for step, out_ref in enumerate(out_refs):
        at = pl.multiple_of((me_ref[0] ^ step) * rows, rows)
        out_ref[...] = rows_ref[pl.ds(at, rows), :]


SMEM = pl.BlockSpec(memory_space=pltpu.SMEM)


def run_space_stream(me, grad, x, inverse, grad_packed, gain, w_qkv, parts):
    features, tokens = x.shape
    return call(
        space_stream,
        [((tokens // parts, features), BF16)] * parts,
        (me, grad, x, inverse, grad_packed, gain, w_qkv),
        4,
        scratch=[((tokens, features), BF16)],
        in_specs=[SMEM] + [VMEM] * 6,
        out_specs=[VMEM] * parts,
    )


def place_blocks(me_ref, *refs):
    in_refs, out_ref = refs[:-1], refs[-1]
    for step, in_ref in enumerate(in_refs):
        out_ref[me_ref[0] ^ step] = in_ref[...]


def unpack(pieces_ref, space_qkv_ref, space_out_ref, time_qkv_ref, time_out_ref):
    features = space_out_ref.shape[0]
    count = pieces_ref.shape[0] // 4
    for j in range(4):
        pieces = pieces_ref[j * count : (j + 1) * count].astype(F32)
        for kind, qkv_ref, out_ref in (
            (0, time_qkv_ref, time_out_ref),
            (1, space_qkv_ref, space_out_ref),
        ):
            block = pieces[:, kind].reshape(features, features)
            if j < 3:
                qkv_ref[:, j * features : (j + 1) * features] = block
            else:
                out_ref[...] = block


def exchange(values, axes):
    return lax.all_to_all(values, axes, split_axis=0, concat_axis=0, tiled=True)


def to_pair(block, step, parts):
    return lax.ppermute(block, "stab", [(i, i ^ step) for i in range(parts)])


def on_device(
    syndrome,
    basis_ids,
    coordinates,
    syndrome_table,
    basis_table,
    coord_table,
    round_table,
    gain_space,
    w_qkv_space,
    w_out_space,
    gain_time,
    w_qkv_time,
    w_out_time,
    grad_hidden,
):
    stab_parts = lax.axis_size("stab")
    round_parts = lax.axis_size("rounds")
    parts = stab_parts * round_parts
    rounds_here, stabs_here, features = grad_hidden.shape
    stabs_time = stabs_here // round_parts

    own_index = call(
        index_kernel,
        [((stab_parts, 5, stabs_here), jnp.int32)],
        (syndrome, basis_ids.reshape(1, stabs_here), coordinates),
        1,
    )[0]
    index = exchange(own_index, "stab")
    grad_chunks = grad_hidden.reshape(rounds_here, round_parts, stabs_time, features)
    grad_chunks, index = lax.optimization_barrier((jnp.swapaxes(grad_chunks, 0, 1), index))
    grad_time = exchange(grad_chunks, "rounds")

    gain_s = gain_space.reshape(1, features)
    gain_t = gain_time.reshape(1, features)
    tables = (syndrome_table, basis_table, coord_table, round_table)
    middle, x, normed, inverse, packed, attended, exps, totals = run_space_forward(
        index, tables, gain_s, w_qkv_space, w_out_space, parts
    )
    middle, grad_time = lax.optimization_barrier((middle, grad_time))
    middle_time = exchange(middle, ("stab", "rounds"))
    middle_time = middle_time.reshape(stab_parts, round_parts, stabs_time, features)
    grad_rows, grad_attended_t = run_time_grad(grad_time, w_out_time)
    grad_middle, normed_t, grad_packed_t, attended_t = run_time_block(
        middle_time, grad_time, grad_attended_t, gain_t, w_qkv_time
    )
    grad_space = exchange(grad_middle.reshape(parts, stabs_time, features), ("stab", "rounds"))
    hidden, time_pieces = run_time_rest(
        middle_time, normed_t, grad_packed_t, attended_t, grad_rows, w_out_time
    )
    hidden, grad_space = lax.optimization_barrier((hidden, grad_space))
    hidden_home = exchange(hidden, "rounds")
    grad_packed, pieces = run_space_backward(
        grad_space, normed, packed, attended, exps, totals, w_out_space, time_pieces
    )
    pieces, grad_packed, hidden_home = lax.optimization_barrier((pieces, grad_packed, hidden_home))
    sources = exchange(pieces, ("rounds", "stab"))
    me = lax.axis_index("stab").astype(jnp.int32).reshape(1)
    blocks = list(
        run_space_stream(
            me, grad_space, x, inverse, grad_packed, gain_s, w_qkv_space, stab_parts
        )
    )
    blocks[1:] = [to_pair(blocks[step], step, stab_parts) for step in range(1, stab_parts)]
    sources, *blocks = lax.optimization_barrier((sources, *blocks))
    scaling = 1.0 / math.sqrt(parts * rounds_here * stabs_here)
    summed = (jnp.sum(sources.astype(F32), axis=0) * scaling).astype(BF16)
    gathered = exchange(
        jnp.broadcast_to(summed[None], (parts,) + summed.shape), ("rounds", "stab")
    )
    grad_embedded = call(
        place_blocks,
        [(grad_hidden.shape, BF16)],
        (me, *blocks),
        2,
        in_specs=[SMEM] + [VMEM] * stab_parts,
        out_specs=[VMEM],
    )[0]
    hidden_home = jnp.swapaxes(hidden_home, 0, 1).reshape(grad_hidden.shape)
    weights = call(
        unpack,
        [((features, 3 * features), F32), ((features, features), F32)] * 2,
        (gathered,),
        2,
        megabytes=20,
    )
    return (hidden_home, grad_embedded) + tuple(weights)


def solution(mesh):
    in_specs = (
        P("rounds", "stab"),
        P("stab"),
        P(None, "stab"),
        P(),
        P(),
        P(),
        P("rounds", None),
        P(),
        P(),
        P(),
        P(),
        P(),
        P(),
        P("rounds", "stab", None),
    )
    out_specs = (P("rounds", "stab", None), P("rounds", "stab", None), P(), P(), P(), P())
    return jax.shard_map(
        on_device, mesh=mesh, in_specs=in_specs, out_specs=out_specs, check_vma=False
    )
```

```python
import math

import jax
import jax.numpy as jnp
from jax import lax
from jax.experimental import pallas as pl
from jax.experimental.pallas import tpu as pltpu
from jax.sharding import PartitionSpec as P

HEADS = 4
EPSILON = 1e-06
F32 = jnp.float32
BF16 = jnp.bfloat16

LEVELS = 128
ROW_AT, COLUMN_AT, BASIS_AT, SYNDROME_AT, ROUND_AT = 0, 48, 96, 104, 112


def dot(left, right, left_dim, right_dim):
    return lax.dot_general(
        left, right, (((left_dim,), (right_dim,)), ((), ())), preferred_element_type=F32
    )


def call(kernel, shapes, arguments, microseconds, scratch=(), megabytes=60, **grid):
    return pl.pallas_call(
        kernel,
        out_shape=[
            jax.ShapeDtypeStruct(*item) if isinstance(item, tuple) else item for item in shapes
        ],
        scratch_shapes=[pltpu.VMEM(*item) if isinstance(item, tuple) else item for item in scratch],
        compiler_params=pltpu.CompilerParams(vmem_limit_bytes=megabytes * 2**20),
        cost_estimate=pl.CostEstimate(
            flops=microseconds * 500_000_000,
            bytes_accessed=microseconds * 2_000_000,
            transcendentals=0,
        ),
        name=kernel.__name__,
        **grid,
    )(*arguments)


def in_hbm(*arrays):
    return [pltpu.with_memory_space_constraint(array, pltpu.HBM) for array in arrays]


def in_range(inverse_totals):
    least, most = jnp.min(inverse_totals), jnp.max(inverse_totals)
    return jnp.logical_and(least > 2.0**-30, most < 2.0**30)


def split_rows(row):
    terms = []
    for _ in range(3):
        terms.append(row.astype(BF16))
        row = row - terms[-1].astype(F32)
    zeros = jnp.zeros((16 - len(terms), row.shape[1]), BF16)
    return jnp.concatenate(terms + [zeros])


def as_column(gain):
    return jnp.broadcast_to(gain, (8, gain.shape[1])).T[:, :1]


def norm_columns(values, gain):
    inverse = lax.rsqrt(jnp.mean(values * values, axis=0, keepdims=True) + EPSILON)
    return (values * inverse * gain).astype(BF16), inverse


def norm_columns_backward(values, gain, inverse, grad_normed):
    gained = grad_normed * gain
    inner = jnp.mean(gained * values, axis=0, keepdims=True)
    return inverse * gained - values * (inverse * inverse * inverse) * inner


def store_blocks(ref, kind, grad_qkv, grad_out):
    features = grad_out.shape[0]
    blocks = [grad_qkv[:, j * features : (j + 1) * features] for j in range(3)] + [grad_out]
    count = ref.shape[0] // len(blocks)
    for j, block in enumerate(blocks):
        ref[j * count : (j + 1) * count, kind] = block.astype(BF16).reshape(
            count, ref.shape[2], features
        )


def index_kernel(syndrome_ref, basis_ref, coordinates_ref, index_ref):
    width = index_ref.shape[2]
    for block in range(index_ref.shape[0]):
        index_ref[block, 0:1, :] = syndrome_ref[block : block + 1, :] + SYNDROME_AT
        index_ref[block, 1:2, :] = basis_ref[...] + BASIS_AT
        index_ref[block, 2:3, :] = coordinates_ref[0:1, :] + ROW_AT
        index_ref[block, 3:4, :] = coordinates_ref[1:2, :] + COLUMN_AT
        index_ref[block, 4:5, :] = jnp.full((1, width), ROUND_AT + block, jnp.int32)


def space_forward(
    index_ref, syndrome_table_ref, basis_table_ref, coord_table_ref, round_table_ref,
    gain_ref, w_qkv_ref, w_out_ref,
    middle_ref, inverse_ref, attended_ref, total_ref, x_out, normed_out, packed_out, exps_out,
    table_ref, row_ref, onehot_ref, x_ref, normed_ref, packed_ref, exps_ref, sems,
):
    features, tokens = x_ref.shape
    depth = features // HEADS
    copies = [
        pltpu.make_async_copy(x_ref, x_out, sems.at[HEADS]),
        pltpu.make_async_copy(normed_ref, normed_out, sems.at[HEADS + 1]),
        pltpu.make_async_copy(packed_ref, packed_out, sems.at[HEADS + 2]),
    ]
    head_copies = [
        pltpu.make_async_copy(exps_ref.at[head], exps_out.at[head], sems.at[head])
        for head in range(HEADS)
    ]

    coords = coord_table_ref.shape[1]
    table_ref[...] = jnp.zeros(table_ref.shape, F32)
    table_ref[ROW_AT : ROW_AT + coords, :] = coord_table_ref[0].astype(F32)
    table_ref[COLUMN_AT : COLUMN_AT + coords, :] = coord_table_ref[1].astype(F32)
    table_ref[BASIS_AT : BASIS_AT + 2, :] = basis_table_ref[...].astype(F32)
    table_ref[SYNDROME_AT : SYNDROME_AT + 2, :] = syndrome_table_ref[...].astype(F32)
    rounds = round_table_ref.shape[0]
    table_ref[ROUND_AT : ROUND_AT + rounds, :] = round_table_ref[...].astype(F32)
    width = index_ref.shape[2]
    levels = lax.broadcasted_iota(jnp.int32, (LEVELS, width), 0)
    for block in range(index_ref.shape[0]):
        hit = levels == index_ref[block, 0:1, :]
        for kind in range(1, index_ref.shape[1]):
            hit = hit | (levels == index_ref[block, kind : kind + 1, :])
        onehot_ref[:, block * width : (block + 1) * width] = hit.astype(F32).astype(BF16)
    table = table_ref[...].astype(BF16)
    x = dot(table, onehot_ref[...], 0, 0).astype(BF16)
    x_ref[...] = x
    copies[0].start()
    normed, inverse = norm_columns(x.astype(F32), as_column(gain_ref[...]))
    normed_ref[...] = normed
    copies[1].start()
    inverse_ref[...] = inverse
    packed = dot(w_qkv_ref[...], normed, 0, 0)
    packed_ref[:features, :] = (packed[:features] * (math.log2(math.e) * depth**-0.5)).astype(BF16)
    packed_ref[features:, :] = packed[features:].astype(BF16)
    copies[2].start()
    row_ref[...] = dot(onehot_ref[...], table, 0, 0).astype(BF16)

    def operands(head):
        at = head * depth
        query = packed_ref[at : at + depth, :]
        keys = packed_ref[features + at : features + at + depth, :].T
        values = packed_ref[2 * features + at : 2 * features + at + depth, :]
        return query, keys, jnp.concatenate([values, jnp.ones((16, tokens), BF16)])

    def attend(head, values, cols):
        product = dot(values, exps_ref[head, :, cols], 1, 0)
        inverse_total = 1.0 / product[depth : depth + 1]
        total_ref[head, :, cols] = inverse_total
        attended_ref[head * depth : (head + 1) * depth, cols] = (
            product[:depth] * inverse_total
        ).astype(BF16)

    blocks = [slice(start, start + SPACE_BLOCK) for start in range(0, tokens, SPACE_BLOCK)]
    before = None
    for head in range(HEADS):
        query, keys, values = operands(head)
        for cols in blocks:
            for low in range(0, tokens, KEY_TILE):
                rows = slice(low, low + KEY_TILE)
                exps_ref[head, rows, cols] = jnp.exp2(
                    dot(keys[rows], query[:, cols], 1, 0)
                ).astype(BF16)
            if before is not None:
                attend(*before)
            before = head, values, cols
        head_copies[head].start()
    attend(*before)

    @pl.when(jnp.logical_not(in_range(total_ref[...])))
    def _():
        for copy in head_copies:
            copy.wait()
        for head in range(HEADS):
            query, keys, values = operands(head)
            for cols in blocks:
                scores = dot(keys, query[:, cols], 1, 0)
                peak = jnp.max(scores, axis=0, keepdims=True)
                exps_ref[head, :, cols] = jnp.exp2(scores - peak).astype(BF16)
                attend(head, values, cols)
            head_copies[head].start()

    branch = dot(attended_ref[...], w_out_ref[...], 0, 0)
    middle = (row_ref[...].astype(F32) + branch).astype(BF16)
    middle_ref[...] = middle.reshape(middle_ref.shape)
    for copy in head_copies + copies:
        copy.wait()


SPACE_BLOCK = 256
KEY_TILE = 128
LOADS = 4
VMEM = pl.BlockSpec(memory_space=pltpu.VMEM)
ANY = pl.BlockSpec(memory_space=pl.ANY)


def run_space_forward(index, tables, gain, w_qkv, w_out, chunks):
    tokens = index.shape[0] * index.shape[2]
    features = w_out.shape[0]
    shapes = [
        ((chunks, tokens // chunks, features), BF16),
        ((1, tokens), F32),
        ((features, tokens), BF16),
        ((HEADS, 1, tokens), F32),
        pltpu.HBM((features, tokens), BF16),
        pltpu.HBM((features, tokens), BF16),
        pltpu.HBM((3 * features, tokens), BF16),
        pltpu.HBM((HEADS, tokens, tokens), BF16),
    ]
    arguments = (index,) + tables + (gain, w_qkv, w_out)
    middle, inverse, attended, totals, x, normed, packed, exps = call(
        space_forward,
        shapes,
        arguments,
        10,
        scratch=[
            ((LEVELS, features), F32),
            ((tokens, features), BF16),
            ((LEVELS, tokens), BF16),
            ((features, tokens), BF16),
            ((features, tokens), BF16),
            ((3 * features, tokens), BF16),
            ((HEADS, tokens, tokens), BF16),
            pltpu.SemaphoreType.DMA((HEADS + 3,)),
        ],
        in_specs=[VMEM] * len(arguments),
        out_specs=[VMEM] * 4 + [ANY] * 4,
    )
    return middle, x, normed, inverse, packed, attended, exps, totals


def time_grad(grad_ref, w_out_ref, grad_row_ref, grad_attended_ref, grads_ref):
    round_parts, stab_parts, stabs, features = grad_ref.shape
    rounds = stab_parts * round_parts
    grad = grad_ref[...].astype(F32).reshape(rounds * stabs, features)
    lanes = grads_ref.shape[2]
    for part in range(features // lanes):
        half = slice(part * lanes, (part + 1) * lanes)
        grads_ref[part] = grad[:, half]
        for stab in range(stabs):
            cols = slice(stab * rounds, (stab + 1) * rounds)
            at = pl.ds(stab, rounds, stride=stabs)
            grad_row_ref[cols, half] = grads_ref[part, at, :].astype(BF16)
    grad_attended_ref[...] = dot(w_out_ref[...], grad_row_ref[...], 1, 1).astype(BF16)


def run_time_grad(grad, w_out):
    round_parts, stab_parts, stabs, features = grad.shape
    tokens = stab_parts * round_parts * stabs
    return call(
        time_grad,
        [((tokens, features), BF16), ((features, tokens), BF16)],
        (grad, w_out),
        3,
        scratch=[((features // 128, tokens, 128), F32)],
    )


def time_block(
    middle_ref, grad_in, grad_attended_in, gain_ref, w_qkv_ref,
    grad_middle_ref, normed_out, grad_packed_out, attended_out,
    grad_ref, grad_attended_ref, normed_ref, grad_packed_ref, attended_ref, x_ref, packed_ref,
    rows_ref, sems,
):
    stab_parts, round_parts, stabs, features = middle_ref.shape
    rounds = stab_parts * round_parts
    tokens = rounds * stabs
    depth = features // HEADS
    scale = depth**-0.5

    load_grad = pltpu.make_async_copy(grad_in, grad_ref, sems.at[3])
    load_attended = pltpu.make_async_copy(grad_attended_in, grad_attended_ref, sems.at[4])
    load_grad.start()
    load_attended.start()
    middle = jnp.swapaxes(middle_ref[...].astype(F32), 0, 1).reshape(tokens, features)
    lanes = rows_ref.shape[2]
    halves = [slice(part * lanes, (part + 1) * lanes) for part in range(features // lanes)]
    for part, half in enumerate(halves):
        rows_ref[part] = middle[:, half]
    for stab in range(stabs):
        cols = slice(stab * rounds, (stab + 1) * rounds)
        at = pl.ds(stab, rounds, stride=stabs)
        for part, half in enumerate(halves):
            x_ref[half, cols] = rows_ref[part, at, :].T
    x = x_ref[...]
    gain = as_column(gain_ref[...])
    normed, inverse = norm_columns(x, gain)
    normed_ref[...] = normed
    store_normed = pltpu.make_async_copy(normed_ref, normed_out, sems.at[0])
    store_normed.start()
    packed = dot(w_qkv_ref[...], normed, 0, 0)
    to_base_two = math.log2(math.e) * scale
    packed_ref[:features, :] = (packed[:features] * to_base_two).astype(BF16)
    packed_ref[features:, :] = packed[features:].astype(BF16)

    ones = jnp.ones((16, rounds), BF16)
    load_attended.wait()
    load_grad.wait()

    def some_stabs(step, carry):
        items = []
        for stab in range(TIME_GROUP):
            start = pl.multiple_of((step * TIME_GROUP + stab) * rounds, rounds)
            cols = pl.ds(start, rounds)
            items += [(head * depth, cols) for head in range(HEADS)]
        query = [packed_ref[at : at + depth, cols] for at, cols in items]
        keys = [packed_ref[features + at : features + at + depth, cols] for at, cols in items]
        values = [
            packed_ref[2 * features + at : 2 * features + at + depth, cols] for at, cols in items
        ]
        scores = [dot(k, q, 0, 0) for k, q in zip(keys, query)]
        exps = [
            jnp.exp2(each - jnp.max(each, axis=0, keepdims=True)).astype(BF16) for each in scores
        ]
        products = [dot(jnp.concatenate([v, ones]), e, 1, 0) for v, e in zip(values, exps)]
        grads, inners = [], []
        for (at, cols), product in zip(items, products):
            inverse_total = 1.0 / product[depth : depth + 1]
            attended = product[:depth] * inverse_total
            attended_ref[at : at + depth, cols] = attended.astype(BF16)
            grad = grad_attended_ref[at : at + depth, cols].astype(F32) * inverse_total
            inners.append(jnp.sum(grad * attended, axis=0, keepdims=True))
            grads.append(grad.astype(BF16))
        centred = [dot(v, g, 0, 0) - inner for v, g, inner in zip(values, grads, inners)]
        grad_scores = [(e.astype(F32) * c).astype(BF16) for e, c in zip(exps, centred)]
        for (at, cols), g, e in zip(items, grads, exps):
            grad_packed_ref[2 * features + at : 2 * features + at + depth, cols] = dot(
                g, e, 1, 1
            ).astype(BF16)
        for (at, cols), k, each in zip(items, keys, grad_scores):
            grad_packed_ref[at : at + depth, cols] = (dot(k, each, 1, 0) * scale).astype(BF16)
        for (at, cols), q, each in zip(items, query, grad_scores):
            grad_packed_ref[features + at : features + at + depth, cols] = (
                dot(q, each, 1, 1) * math.log(2.0)
            ).astype(BF16)
        return carry

    lax.fori_loop(0, stabs // TIME_GROUP, some_stabs, 0, unroll=TIME_UNROLL)
    store_attended = pltpu.make_async_copy(attended_ref, attended_out, sems.at[1])
    store_packed = pltpu.make_async_copy(grad_packed_ref, grad_packed_out, sems.at[2])
    store_attended.start()
    store_packed.start()

    grad_normed = dot(w_qkv_ref[...], grad_packed_ref[...], 1, 0)
    grad_stream = norm_columns_backward(x_ref[...], gain, inverse, grad_normed)
    for stab in range(stabs):
        cols = slice(stab * rounds, (stab + 1) * rounds)
        at = pl.ds(stab, rounds, stride=stabs)
        for part, half in enumerate(halves):
            rows_ref[part, at, :] = grad_stream[half, cols].T
    for part, half in enumerate(halves):
        grad_middle = rows_ref[part].reshape(round_parts, stab_parts, stabs, lanes)
        grad_middle = grad_middle + grad_ref[:, :, :, half].astype(F32)
        grad_middle_ref[:, :, :, half] = jnp.swapaxes(grad_middle, 0, 1).astype(BF16)
    store_normed.wait()
    store_attended.wait()
    store_packed.wait()


TIME_UNROLL = True
TIME_GROUP = 2


def run_time_block(middle, grad, grad_attended, gain, w_qkv):
    stab_parts, round_parts, stabs, features = middle.shape
    tokens = stab_parts * round_parts * stabs
    grad, grad_attended = in_hbm(grad, grad_attended)
    shapes = [
        (middle.shape, BF16),
        pltpu.HBM((features, tokens), BF16),
        pltpu.HBM((3 * features, tokens), BF16),
        pltpu.HBM((features, tokens), BF16),
    ]
    return call(
        time_block,
        shapes,
        (middle, grad, grad_attended, gain, w_qkv),
        10,
        scratch=[
            (grad.shape, BF16),
            (grad_attended.shape, BF16),
            ((features, tokens), BF16),
            ((3 * features, tokens), BF16),
            ((features, tokens), BF16),
            ((features, tokens), F32),
            ((3 * features, tokens), BF16),
            ((features // 128, tokens, 128), F32),
            pltpu.SemaphoreType.DMA((5,)),
        ],
        megabytes=24,
        in_specs=[VMEM, ANY, ANY, VMEM, VMEM],
        out_specs=[VMEM] + [ANY] * 3,
    )


def time_rest(
    middle_ref, normed_ref, grad_packed_ref, attended_ref, grad_row_ref, w_out_ref,
    hidden_ref, pieces_ref,
    rows_ref,
):
    stab_parts, round_parts, stabs, features = middle_ref.shape
    rounds = stab_parts * round_parts
    tokens = rounds * stabs
    lanes = rows_ref.shape[2]
    halves = [slice(part * lanes, (part + 1) * lanes) for part in range(features // lanes)]
    attended = attended_ref[...]
    branch = dot(attended, w_out_ref[...], 0, 0)
    middle = jnp.swapaxes(middle_ref[...].astype(F32), 0, 1).reshape(tokens, features)
    for part, half in enumerate(halves):
        rows_ref[part] = middle[:, half]
    for stab in range(stabs):
        cols = slice(stab * rounds, (stab + 1) * rounds)
        at = pl.ds(stab, rounds, stride=stabs)
        for part, half in enumerate(halves):
            rows_ref[part, at, :] = rows_ref[part, at, :] + branch[cols, half]
    for part, half in enumerate(halves):
        hidden = rows_ref[part].reshape(round_parts, stab_parts, stabs, lanes)
        hidden_ref[:, :, :, half] = hidden.astype(BF16)
    store_blocks(
        pieces_ref,
        0,
        dot(normed_ref[...], grad_packed_ref[...], 1, 1),
        dot(attended, grad_row_ref[...], 1, 0),
    )


def run_time_rest(middle, normed, grad_packed, attended, grad_rows, w_out):
    features, tokens = normed.shape
    stab_parts, round_parts, stabs, _ = middle.shape
    parts = stab_parts * round_parts
    return call(
        time_rest,
        [
            ((round_parts, stab_parts, stabs, features), BF16),
            ((parts, 1, 4 * features // parts, features), BF16),
        ],
        (middle, normed, grad_packed, attended, grad_rows, w_out),
        5,
        scratch=[((features // 128, tokens, 128), F32)],
    )


def space_backward(
    grad_ref, total_ref, w_out_ref, packed_in, attended_in, normed_in, exps_in, time_in,
    grad_packed_out, pieces_out,
    grad_attended_ref, grad_packed_ref, pieces_ref, packed_ref, attended_ref, normed_ref,
    exps_ref, grad_scores_ref, sems, load_sems,
):
    features, tokens = attended_ref.shape
    depth = features // HEADS
    part = tokens // LOADS
    loads = [
        [
            pltpu.make_async_copy(
                exps_in.at[head, pl.ds(low * part, part)],
                exps_ref.at[head, pl.ds(low * part, part)],
                load_sems.at[head, low],
            )
            for low in range(LOADS)
        ]
        for head in range(HEADS)
    ]
    load_packed = pltpu.make_async_copy(packed_in, packed_ref, sems.at[0])
    load_attended = pltpu.make_async_copy(attended_in, attended_ref, sems.at[1])
    load_normed = pltpu.make_async_copy(normed_in, normed_ref, sems.at[HEADS])
    copy_time = pltpu.make_async_copy(time_in, pieces_ref.at[:, 0:1], sems.at[HEADS + 1])
    store_packed = pltpu.make_async_copy(grad_packed_ref, grad_packed_out, sems.at[HEADS + 2])
    store_pieces = pltpu.make_async_copy(pieces_ref, pieces_out, sems.at[HEADS + 3])
    load_packed.start()
    load_attended.start()
    for load in loads[0]:
        load.start()

    new = grad_ref[...].reshape(tokens, features)
    grad_attended_ref[...] = dot(w_out_ref[...], new, 1, 1).astype(BF16)
    load_packed.wait()
    load_attended.wait()
    for load in loads[0]:
        load.wait()
    for load in loads[1] + loads[2] + loads[3]:
        load.start()
    load_normed.start()
    copy_time.start()
    blocks = [slice(start, start + SPACE_BLOCK) for start in range(0, tokens, SPACE_BLOCK)]

    def finish(head, grad):
        at = head * depth
        keys = packed_ref[features + at : features + at + depth, :]
        query = packed_ref[at : at + depth, :]
        scores = grad_scores_ref[head % 2]
        grad_packed_ref[at : at + depth, :] = (dot(keys, scores, 1, 0) * depth**-0.5).astype(BF16)
        grad_packed_ref[features + at : features + at + depth, :] = (
            dot(scores, query.T, 1, 0).T * math.log(2.0)
        ).astype(BF16)
        grad_packed_ref[2 * features + at : 2 * features + at + depth, :] = dot(
            exps_ref[head], grad.T, 1, 0
        ).T.astype(BF16)

    before = None
    for head in range(HEADS):
        at = head * depth
        values = packed_ref[2 * features + at : 2 * features + at + depth, :]
        grad = grad_attended_ref[at : at + depth, :].astype(F32) * total_ref[head]
        inner = jnp.sum(
            grad * attended_ref[at : at + depth, :].astype(F32), axis=0, keepdims=True
        )
        grad = grad.astype(BF16)
        wide_grad = jnp.concatenate([grad, split_rows(inner)])
        wide_values = jnp.concatenate([values.T, jnp.full((tokens, 16), -1.0, BF16)], axis=1)
        if head > 0:
            for load in loads[head]:
                load.wait()
        for cols in blocks:
            for low in range(0, tokens, KEY_TILE):
                rows = slice(low, low + KEY_TILE)
                centred = dot(wide_values[rows], wide_grad[:, cols], 1, 0)
                grad_scores_ref[head % 2, rows, cols] = (
                    exps_ref[head, rows, cols].astype(F32) * centred
                ).astype(BF16)
        finish(head, grad)
    store_packed.start()
    load_normed.wait()
    store_blocks(
        pieces_ref,
        1,
        dot(normed_ref[...], grad_packed_ref[...], 1, 1),
        dot(attended_ref[...], new, 1, 0),
    )
    copy_time.wait()
    store_pieces.start()
    store_packed.wait()
    store_pieces.wait()


def run_space_backward(grad, normed, packed, attended, exps, totals, w_out, time_pieces):
    features, tokens = attended.shape
    parts, _, rows, _ = time_pieces.shape
    packed, attended, normed, exps, time_pieces = in_hbm(
        packed, attended, normed, exps, time_pieces
    )
    shapes = [pltpu.HBM((3 * features, tokens), BF16), ((parts, 2, rows, features), BF16)]
    return call(
        space_backward,
        shapes,
        (grad, totals, w_out, packed, attended, normed, exps, time_pieces),
        14,
        scratch=[
            ((features, tokens), BF16),
            ((3 * features, tokens), BF16),
            ((parts, 2, rows, features), BF16),
            ((3 * features, tokens), BF16),
            ((features, tokens), BF16),
            ((features, tokens), BF16),
            ((HEADS, tokens, tokens), BF16),
            ((2, tokens, tokens), BF16),
            pltpu.SemaphoreType.DMA((HEADS + 4,)),
            pltpu.SemaphoreType.DMA((HEADS, LOADS)),
        ],
        megabytes=32,
        in_specs=[VMEM] * 3 + [ANY] * 5,
        out_specs=[ANY] * 2,
    )


def space_stream(
    me_ref, grad_ref, x_ref, inverse_ref, grad_packed_ref, gain_ref, w_qkv_ref, *rest
):
    out_refs, rows_ref = rest[:-1], rest[-1]
    features, tokens = x_ref.shape
    grad_normed = dot(w_qkv_ref[...], grad_packed_ref[...], 1, 0)
    grad_stream = norm_columns_backward(
        x_ref[...].astype(F32), as_column(gain_ref[...]), inverse_ref[...], grad_normed
    )
    grad_new = grad_ref[...].reshape(tokens, features).astype(F32)
    rows_ref[...] = (grad_new + grad_stream.T).astype(BF16)
    rows = tokens // len(out_refs)
    for step, out_ref in enumerate(out_refs):
        at = pl.multiple_of((me_ref[0] ^ step) * rows, rows)
        out_ref[...] = rows_ref[pl.ds(at, rows), :]


SMEM = pl.BlockSpec(memory_space=pltpu.SMEM)


def run_space_stream(me, grad, x, inverse, grad_packed, gain, w_qkv, parts):
    features, tokens = x.shape
    return call(
        space_stream,
        [((tokens // parts, features), BF16)] * parts,
        (me, grad, x, inverse, grad_packed, gain, w_qkv),
        4,
        scratch=[((tokens, features), BF16)],
        in_specs=[SMEM] + [VMEM] * 6,
        out_specs=[VMEM] * parts,
    )


def place_blocks(me_ref, *refs):
    in_refs, out_ref = refs[:-1], refs[-1]
    for step, in_ref in enumerate(in_refs):
        out_ref[me_ref[0] ^ step] = in_ref[...]


def unpack(pieces_ref, space_qkv_ref, space_out_ref, time_qkv_ref, time_out_ref):
    features = space_out_ref.shape[0]
    count = pieces_ref.shape[0] // 4
    for j in range(4):
        pieces = pieces_ref[j * count : (j + 1) * count].astype(F32)
        for kind, qkv_ref, out_ref in (
            (0, time_qkv_ref, time_out_ref),
            (1, space_qkv_ref, space_out_ref),
        ):
            block = pieces[:, kind].reshape(features, features)
            if j < 3:
                qkv_ref[:, j * features : (j + 1) * features] = block
            else:
                out_ref[...] = block


def exchange(values, axes):
    return lax.all_to_all(values, axes, split_axis=0, concat_axis=0, tiled=True)


def to_pair(block, step, parts):
    return lax.ppermute(block, "stab", [(i, i ^ step) for i in range(parts)])


def on_device(
    syndrome,
    basis_ids,
    coordinates,
    syndrome_table,
    basis_table,
    coord_table,
    round_table,
    gain_space,
    w_qkv_space,
    w_out_space,
    gain_time,
    w_qkv_time,
    w_out_time,
    grad_hidden,
):
    stab_parts = lax.axis_size("stab")
    round_parts = lax.axis_size("rounds")
    parts = stab_parts * round_parts
    rounds_here, stabs_here, features = grad_hidden.shape
    stabs_time = stabs_here // round_parts

    own_index = call(
        index_kernel,
        [((stab_parts, 5, stabs_here), jnp.int32)],
        (syndrome, basis_ids.reshape(1, stabs_here), coordinates),
        1,
    )[0]
    index = exchange(own_index, "stab")
    grad_chunks = grad_hidden.reshape(rounds_here, round_parts, stabs_time, features)
    grad_chunks, index = lax.optimization_barrier((jnp.swapaxes(grad_chunks, 0, 1), index))
    grad_time = exchange(grad_chunks, "rounds")

    gain_s = gain_space.reshape(1, features)
    gain_t = gain_time.reshape(1, features)
    tables = (syndrome_table, basis_table, coord_table, round_table)
    middle, x, normed, inverse, packed, attended, exps, totals = run_space_forward(
        index, tables, gain_s, w_qkv_space, w_out_space, parts
    )
    middle, grad_time = lax.optimization_barrier((middle, grad_time))
    middle_time = exchange(middle, ("stab", "rounds"))
    middle_time = middle_time.reshape(stab_parts, round_parts, stabs_time, features)
    grad_rows, grad_attended_t = run_time_grad(grad_time, w_out_time)
    grad_middle, normed_t, grad_packed_t, attended_t = run_time_block(
        middle_time, grad_time, grad_attended_t, gain_t, w_qkv_time
    )
    grad_space = exchange(grad_middle.reshape(parts, stabs_time, features), ("stab", "rounds"))
    hidden, time_pieces = run_time_rest(
        middle_time, normed_t, grad_packed_t, attended_t, grad_rows, w_out_time
    )
    hidden, grad_space = lax.optimization_barrier((hidden, grad_space))
    hidden_home = exchange(hidden, "rounds")
    grad_packed, pieces = run_space_backward(
        grad_space, normed, packed, attended, exps, totals, w_out_space, time_pieces
    )
    pieces, grad_packed, hidden_home = lax.optimization_barrier((pieces, grad_packed, hidden_home))
    sources = exchange(pieces, ("rounds", "stab"))
    me = lax.axis_index("stab").astype(jnp.int32).reshape(1)
    blocks = list(
        run_space_stream(
            me, grad_space, x, inverse, grad_packed, gain_s, w_qkv_space, stab_parts
        )
    )
    for step in range(1, stab_parts, 2):
        blocks[step] = to_pair(blocks[step], step, stab_parts)
    sources, *blocks = lax.optimization_barrier((sources, *blocks))
    blocks = list(blocks)
    for step in range(2, stab_parts, 2):
        blocks[step] = to_pair(blocks[step], step, stab_parts)
    scaling = 1.0 / math.sqrt(parts * rounds_here * stabs_here)
    summed = (jnp.sum(sources.astype(F32), axis=0) * scaling).astype(BF16)
    gathered = exchange(
        jnp.broadcast_to(summed[None], (parts,) + summed.shape), ("rounds", "stab")
    )
    hidden_home = jnp.swapaxes(hidden_home, 0, 1).reshape(grad_hidden.shape)
    weights = call(
        unpack,
        [((features, 3 * features), F32), ((features, features), F32)] * 2,
        (gathered,),
        2,
        megabytes=20,
    )
    *weights, hidden_home, blocks = lax.optimization_barrier((*weights, hidden_home, blocks))
    grad_embedded = call(
        place_blocks,
        [(grad_hidden.shape, BF16)],
        (me, *blocks),
        2,
        in_specs=[SMEM] + [VMEM] * stab_parts,
        out_specs=[VMEM],
    )[0]
    return (hidden_home, grad_embedded) + tuple(weights)


def solution(mesh):
    in_specs = (
        P("rounds", "stab"),
        P("stab"),
        P(None, "stab"),
        P(),
        P(),
        P(),
        P("rounds", None),
        P(),
        P(),
        P(),
        P(),
        P(),
        P(),
        P("rounds", "stab", None),
    )
    out_specs = (P("rounds", "stab", None), P("rounds", "stab", None), P(), P(), P(), P())
    return jax.shard_map(
        on_device, mesh=mesh, in_specs=in_specs, out_specs=out_specs, check_vma=False
    )
```

```python
import math

import jax
import jax.numpy as jnp
from jax import lax
from jax.experimental import pallas as pl
from jax.experimental.pallas import tpu as pltpu
from jax.sharding import PartitionSpec as P

HEADS = 4
EPSILON = 1e-06
F32 = jnp.float32
BF16 = jnp.bfloat16

LEVELS = 128
ROW_AT, COLUMN_AT, BASIS_AT, SYNDROME_AT, ROUND_AT = 0, 48, 96, 104, 112


def dot(left, right, left_dim, right_dim):
    return lax.dot_general(
        left, right, (((left_dim,), (right_dim,)), ((), ())), preferred_element_type=F32
    )


def call(kernel, shapes, arguments, microseconds, scratch=(), megabytes=60, **grid):
    return pl.pallas_call(
        kernel,
        out_shape=[
            jax.ShapeDtypeStruct(*item) if isinstance(item, tuple) else item for item in shapes
        ],
        scratch_shapes=[pltpu.VMEM(*item) if isinstance(item, tuple) else item for item in scratch],
        compiler_params=pltpu.CompilerParams(vmem_limit_bytes=megabytes * 2**20),
        cost_estimate=pl.CostEstimate(
            flops=microseconds * 500_000_000,
            bytes_accessed=microseconds * 2_000_000,
            transcendentals=0,
        ),
        name=kernel.__name__,
        **grid,
    )(*arguments)


def in_hbm(*arrays):
    return [pltpu.with_memory_space_constraint(array, pltpu.HBM) for array in arrays]


def in_range(inverse_totals):
    least, most = jnp.min(inverse_totals), jnp.max(inverse_totals)
    return jnp.logical_and(least > 2.0**-30, most < 2.0**30)


def split_rows(row):
    terms = []
    for _ in range(3):
        terms.append(row.astype(BF16))
        row = row - terms[-1].astype(F32)
    zeros = jnp.zeros((16 - len(terms), row.shape[1]), BF16)
    return jnp.concatenate(terms + [zeros])


def as_column(gain):
    return jnp.broadcast_to(gain, (8, gain.shape[1])).T[:, :1]


def norm_columns(values, gain):
    inverse = lax.rsqrt(jnp.mean(values * values, axis=0, keepdims=True) + EPSILON)
    return (values * inverse * gain).astype(BF16), inverse


def norm_columns_backward(values, gain, inverse, grad_normed):
    gained = grad_normed * gain
    inner = jnp.mean(gained * values, axis=0, keepdims=True)
    return inverse * gained - values * (inverse * inverse * inverse) * inner


def store_blocks(ref, kind, grad_qkv, grad_out):
    features = grad_out.shape[0]
    blocks = [grad_qkv[:, j * features : (j + 1) * features] for j in range(3)] + [grad_out]
    count = ref.shape[0] // len(blocks)
    for j, block in enumerate(blocks):
        ref[j * count : (j + 1) * count, kind] = block.astype(BF16).reshape(
            count, ref.shape[2], features
        )


def index_kernel(syndrome_ref, basis_ref, coordinates_ref, index_ref):
    width = index_ref.shape[2]
    for block in range(index_ref.shape[0]):
        index_ref[block, 0:1, :] = syndrome_ref[block : block + 1, :] + SYNDROME_AT
        index_ref[block, 1:2, :] = basis_ref[...] + BASIS_AT
        index_ref[block, 2:3, :] = coordinates_ref[0:1, :] + ROW_AT
        index_ref[block, 3:4, :] = coordinates_ref[1:2, :] + COLUMN_AT
        index_ref[block, 4:5, :] = jnp.full((1, width), ROUND_AT + block, jnp.int32)


def space_forward(
    index_ref, syndrome_table_ref, basis_table_ref, coord_table_ref, round_table_ref,
    gain_ref, w_qkv_ref, w_out_ref,
    middle_ref, inverse_ref, attended_ref, total_ref, x_out, normed_out, packed_out, exps_out,
    table_ref, row_ref, onehot_ref, x_ref, normed_ref, packed_ref, exps_ref, sems,
):
    features, tokens = x_ref.shape
    depth = features // HEADS
    copies = [
        pltpu.make_async_copy(x_ref, x_out, sems.at[HEADS]),
        pltpu.make_async_copy(normed_ref, normed_out, sems.at[HEADS + 1]),
        pltpu.make_async_copy(packed_ref, packed_out, sems.at[HEADS + 2]),
    ]
    head_copies = [
        pltpu.make_async_copy(exps_ref.at[head], exps_out.at[head], sems.at[head])
        for head in range(HEADS)
    ]

    coords = coord_table_ref.shape[1]
    table_ref[...] = jnp.zeros(table_ref.shape, F32)
    table_ref[ROW_AT : ROW_AT + coords, :] = coord_table_ref[0].astype(F32)
    table_ref[COLUMN_AT : COLUMN_AT + coords, :] = coord_table_ref[1].astype(F32)
    table_ref[BASIS_AT : BASIS_AT + 2, :] = basis_table_ref[...].astype(F32)
    table_ref[SYNDROME_AT : SYNDROME_AT + 2, :] = syndrome_table_ref[...].astype(F32)
    rounds = round_table_ref.shape[0]
    table_ref[ROUND_AT : ROUND_AT + rounds, :] = round_table_ref[...].astype(F32)
    width = index_ref.shape[2]
    levels = lax.broadcasted_iota(jnp.int32, (LEVELS, width), 0)
    for block in range(index_ref.shape[0]):
        hit = levels == index_ref[block, 0:1, :]
        for kind in range(1, index_ref.shape[1]):
            hit = hit | (levels == index_ref[block, kind : kind + 1, :])
        onehot_ref[:, block * width : (block + 1) * width] = hit.astype(F32).astype(BF16)
    table = table_ref[...].astype(BF16)
    x = dot(table, onehot_ref[...], 0, 0).astype(BF16)
    x_ref[...] = x
    copies[0].start()
    normed, inverse = norm_columns(x.astype(F32), as_column(gain_ref[...]))
    normed_ref[...] = normed
    copies[1].start()
    inverse_ref[...] = inverse
    packed = dot(w_qkv_ref[...], normed, 0, 0)
    packed_ref[:features, :] = (packed[:features] * (math.log2(math.e) * depth**-0.5)).astype(BF16)
    packed_ref[features:, :] = packed[features:].astype(BF16)
    copies[2].start()
    row_ref[...] = dot(onehot_ref[...], table, 0, 0).astype(BF16)

    def operands(head):
        at = head * depth
        query = packed_ref[at : at + depth, :]
        keys = packed_ref[features + at : features + at + depth, :].T
        values = packed_ref[2 * features + at : 2 * features + at + depth, :]
        return query, keys, jnp.concatenate([values, jnp.ones((16, tokens), BF16)])

    def attend(head, values, cols):
        product = dot(values, exps_ref[head, :, cols], 1, 0)
        inverse_total = 1.0 / product[depth : depth + 1]
        total_ref[head, :, cols] = inverse_total
        attended_ref[head * depth : (head + 1) * depth, cols] = (
            product[:depth] * inverse_total
        ).astype(BF16)

    blocks = [slice(start, start + SPACE_BLOCK) for start in range(0, tokens, SPACE_BLOCK)]
    before = None
    for head in range(HEADS):
        query, keys, values = operands(head)
        for cols in blocks:
            for low in range(0, tokens, KEY_TILE):
                rows = slice(low, low + KEY_TILE)
                exps_ref[head, rows, cols] = jnp.exp2(
                    dot(keys[rows], query[:, cols], 1, 0)
                ).astype(BF16)
            if before is not None:
                attend(*before)
            before = head, values, cols
        head_copies[head].start()
    attend(*before)

    @pl.when(jnp.logical_not(in_range(total_ref[...])))
    def _():
        for copy in head_copies:
            copy.wait()
        for head in range(HEADS):
            query, keys, values = operands(head)
            for cols in blocks:
                scores = dot(keys, query[:, cols], 1, 0)
                peak = jnp.max(scores, axis=0, keepdims=True)
                exps_ref[head, :, cols] = jnp.exp2(scores - peak).astype(BF16)
                attend(head, values, cols)
            head_copies[head].start()

    branch = dot(attended_ref[...], w_out_ref[...], 0, 0)
    middle = (row_ref[...].astype(F32) + branch).astype(BF16)
    middle_ref[...] = middle.reshape(middle_ref.shape)
    for copy in head_copies + copies:
        copy.wait()


SPACE_BLOCK = 256
KEY_TILE = 128
LOADS = 4
VMEM = pl.BlockSpec(memory_space=pltpu.VMEM)
ANY = pl.BlockSpec(memory_space=pl.ANY)


def run_space_forward(index, tables, gain, w_qkv, w_out, chunks):
    tokens = index.shape[0] * index.shape[2]
    features = w_out.shape[0]
    shapes = [
        ((chunks, tokens // chunks, features), BF16),
        ((1, tokens), F32),
        ((features, tokens), BF16),
        ((HEADS, 1, tokens), F32),
        pltpu.HBM((features, tokens), BF16),
        pltpu.HBM((features, tokens), BF16),
        pltpu.HBM((3 * features, tokens), BF16),
        pltpu.HBM((HEADS, tokens, tokens), BF16),
    ]
    arguments = (index,) + tables + (gain, w_qkv, w_out)
    middle, inverse, attended, totals, x, normed, packed, exps = call(
        space_forward,
        shapes,
        arguments,
        10,
        scratch=[
            ((LEVELS, features), F32),
            ((tokens, features), BF16),
            ((LEVELS, tokens), BF16),
            ((features, tokens), BF16),
            ((features, tokens), BF16),
            ((3 * features, tokens), BF16),
            ((HEADS, tokens, tokens), BF16),
            pltpu.SemaphoreType.DMA((HEADS + 3,)),
        ],
        in_specs=[VMEM] * len(arguments),
        out_specs=[VMEM] * 4 + [ANY] * 4,
    )
    return middle, x, normed, inverse, packed, attended, exps, totals


def time_grad(grad_ref, w_out_ref, grad_row_ref, grad_attended_ref, grads_ref):
    round_parts, stab_parts, stabs, features = grad_ref.shape
    rounds = stab_parts * round_parts
    grad = grad_ref[...].astype(F32).reshape(rounds * stabs, features)
    lanes = grads_ref.shape[2]
    for part in range(features // lanes):
        half = slice(part * lanes, (part + 1) * lanes)
        grads_ref[part] = grad[:, half]
        for stab in range(stabs):
            cols = slice(stab * rounds, (stab + 1) * rounds)
            at = pl.ds(stab, rounds, stride=stabs)
            grad_row_ref[cols, half] = grads_ref[part, at, :].astype(BF16)
    grad_attended_ref[...] = dot(w_out_ref[...], grad_row_ref[...], 1, 1).astype(BF16)


def run_time_grad(grad, w_out):
    round_parts, stab_parts, stabs, features = grad.shape
    tokens = stab_parts * round_parts * stabs
    return call(
        time_grad,
        [((tokens, features), BF16), ((features, tokens), BF16)],
        (grad, w_out),
        3,
        scratch=[((features // 128, tokens, 128), F32)],
    )


def time_block(
    middle_ref, grad_in, grad_attended_in, gain_ref, w_qkv_ref,
    grad_middle_ref, normed_out, grad_packed_out, attended_out,
    grad_ref, grad_attended_ref, normed_ref, grad_packed_ref, attended_ref, x_ref, packed_ref,
    rows_ref, sems,
):
    stab_parts, round_parts, stabs, features = middle_ref.shape
    rounds = stab_parts * round_parts
    tokens = rounds * stabs
    depth = features // HEADS
    scale = depth**-0.5

    load_grad = pltpu.make_async_copy(grad_in, grad_ref, sems.at[3])
    load_attended = pltpu.make_async_copy(grad_attended_in, grad_attended_ref, sems.at[4])
    load_grad.start()
    load_attended.start()
    middle = jnp.swapaxes(middle_ref[...].astype(F32), 0, 1).reshape(tokens, features)
    lanes = rows_ref.shape[2]
    halves = [slice(part * lanes, (part + 1) * lanes) for part in range(features // lanes)]
    for part, half in enumerate(halves):
        rows_ref[part] = middle[:, half]
    for stab in range(stabs):
        cols = slice(stab * rounds, (stab + 1) * rounds)
        at = pl.ds(stab, rounds, stride=stabs)
        for part, half in enumerate(halves):
            x_ref[half, cols] = rows_ref[part, at, :].T
    x = x_ref[...]
    gain = as_column(gain_ref[...])
    normed, inverse = norm_columns(x, gain)
    normed_ref[...] = normed
    store_normed = pltpu.make_async_copy(normed_ref, normed_out, sems.at[0])
    store_normed.start()
    packed = dot(w_qkv_ref[...], normed, 0, 0)
    to_base_two = math.log2(math.e) * scale
    packed_ref[:features, :] = (packed[:features] * to_base_two).astype(BF16)
    packed_ref[features:, :] = packed[features:].astype(BF16)

    ones = jnp.ones((16, rounds), BF16)
    load_attended.wait()
    load_grad.wait()

    def some_stabs(step, carry):
        items = []
        for stab in range(TIME_GROUP):
            start = pl.multiple_of((step * TIME_GROUP + stab) * rounds, rounds)
            cols = pl.ds(start, rounds)
            items += [(head * depth, cols) for head in range(HEADS)]
        query = [packed_ref[at : at + depth, cols] for at, cols in items]
        keys = [packed_ref[features + at : features + at + depth, cols] for at, cols in items]
        values = [
            packed_ref[2 * features + at : 2 * features + at + depth, cols] for at, cols in items
        ]
        scores = [dot(k, q, 0, 0) for k, q in zip(keys, query)]
        exps = [
            jnp.exp2(each - jnp.max(each, axis=0, keepdims=True)).astype(BF16) for each in scores
        ]
        products = [dot(jnp.concatenate([v, ones]), e, 1, 0) for v, e in zip(values, exps)]
        grads, inners = [], []
        for (at, cols), product in zip(items, products):
            inverse_total = 1.0 / product[depth : depth + 1]
            attended = product[:depth] * inverse_total
            attended_ref[at : at + depth, cols] = attended.astype(BF16)
            grad = grad_attended_ref[at : at + depth, cols].astype(F32) * inverse_total
            inners.append(jnp.sum(grad * attended, axis=0, keepdims=True))
            grads.append(grad.astype(BF16))
        centred = [dot(v, g, 0, 0) - inner for v, g, inner in zip(values, grads, inners)]
        grad_scores = [(e.astype(F32) * c).astype(BF16) for e, c in zip(exps, centred)]
        for (at, cols), g, e in zip(items, grads, exps):
            grad_packed_ref[2 * features + at : 2 * features + at + depth, cols] = dot(
                g, e, 1, 1
            ).astype(BF16)
        for (at, cols), k, each in zip(items, keys, grad_scores):
            grad_packed_ref[at : at + depth, cols] = (dot(k, each, 1, 0) * scale).astype(BF16)
        for (at, cols), q, each in zip(items, query, grad_scores):
            grad_packed_ref[features + at : features + at + depth, cols] = (
                dot(q, each, 1, 1) * math.log(2.0)
            ).astype(BF16)
        return carry

    lax.fori_loop(0, stabs // TIME_GROUP, some_stabs, 0, unroll=TIME_UNROLL)
    store_attended = pltpu.make_async_copy(attended_ref, attended_out, sems.at[1])
    store_packed = pltpu.make_async_copy(grad_packed_ref, grad_packed_out, sems.at[2])
    store_attended.start()
    store_packed.start()

    grad_normed = dot(w_qkv_ref[...], grad_packed_ref[...], 1, 0)
    grad_stream = norm_columns_backward(x_ref[...], gain, inverse, grad_normed)
    for stab in range(stabs):
        cols = slice(stab * rounds, (stab + 1) * rounds)
        at = pl.ds(stab, rounds, stride=stabs)
        for part, half in enumerate(halves):
            rows_ref[part, at, :] = grad_stream[half, cols].T
    for part, half in enumerate(halves):
        grad_middle = rows_ref[part].reshape(round_parts, stab_parts, stabs, lanes)
        grad_middle = grad_middle + grad_ref[:, :, :, half].astype(F32)
        grad_middle_ref[:, :, :, half] = jnp.swapaxes(grad_middle, 0, 1).astype(BF16)
    store_normed.wait()
    store_attended.wait()
    store_packed.wait()


TIME_UNROLL = True
TIME_GROUP = 2


def run_time_block(middle, grad, grad_attended, gain, w_qkv):
    stab_parts, round_parts, stabs, features = middle.shape
    tokens = stab_parts * round_parts * stabs
    grad, grad_attended = in_hbm(grad, grad_attended)
    shapes = [
        (middle.shape, BF16),
        pltpu.HBM((features, tokens), BF16),
        pltpu.HBM((3 * features, tokens), BF16),
        pltpu.HBM((features, tokens), BF16),
    ]
    return call(
        time_block,
        shapes,
        (middle, grad, grad_attended, gain, w_qkv),
        10,
        scratch=[
            (grad.shape, BF16),
            (grad_attended.shape, BF16),
            ((features, tokens), BF16),
            ((3 * features, tokens), BF16),
            ((features, tokens), BF16),
            ((features, tokens), F32),
            ((3 * features, tokens), BF16),
            ((features // 128, tokens, 128), F32),
            pltpu.SemaphoreType.DMA((5,)),
        ],
        megabytes=24,
        in_specs=[VMEM, ANY, ANY, VMEM, VMEM],
        out_specs=[VMEM] + [ANY] * 3,
    )


def time_rest(
    middle_ref, normed_ref, grad_packed_ref, attended_ref, grad_row_ref, w_out_ref,
    hidden_ref, pieces_ref,
    rows_ref,
):
    stab_parts, round_parts, stabs, features = middle_ref.shape
    rounds = stab_parts * round_parts
    tokens = rounds * stabs
    lanes = rows_ref.shape[2]
    halves = [slice(part * lanes, (part + 1) * lanes) for part in range(features // lanes)]
    attended = attended_ref[...]
    branch = dot(attended, w_out_ref[...], 0, 0)
    middle = jnp.swapaxes(middle_ref[...].astype(F32), 0, 1).reshape(tokens, features)
    for part, half in enumerate(halves):
        rows_ref[part] = middle[:, half]
    for stab in range(stabs):
        cols = slice(stab * rounds, (stab + 1) * rounds)
        at = pl.ds(stab, rounds, stride=stabs)
        for part, half in enumerate(halves):
            rows_ref[part, at, :] = rows_ref[part, at, :] + branch[cols, half]
    for part, half in enumerate(halves):
        hidden = rows_ref[part].reshape(round_parts, stab_parts, stabs, lanes)
        hidden_ref[:, :, :, half] = hidden.astype(BF16)
    store_blocks(
        pieces_ref,
        0,
        dot(normed_ref[...], grad_packed_ref[...], 1, 1),
        dot(attended, grad_row_ref[...], 1, 0),
    )


def run_time_rest(middle, normed, grad_packed, attended, grad_rows, w_out):
    features, tokens = normed.shape
    stab_parts, round_parts, stabs, _ = middle.shape
    parts = stab_parts * round_parts
    return call(
        time_rest,
        [
            ((round_parts, stab_parts, stabs, features), BF16),
            ((parts, 1, 4 * features // parts, features), BF16),
        ],
        (middle, normed, grad_packed, attended, grad_rows, w_out),
        5,
        scratch=[((features // 128, tokens, 128), F32)],
    )


def space_backward(
    grad_ref, total_ref, w_out_ref, packed_in, attended_in, normed_in, exps_in, time_in,
    grad_packed_out, pieces_out,
    grad_attended_ref, grad_packed_ref, pieces_ref, packed_ref, attended_ref, normed_ref,
    exps_ref, grad_scores_ref, sems, load_sems,
):
    features, tokens = attended_ref.shape
    depth = features // HEADS
    part = tokens // LOADS
    loads = [
        [
            pltpu.make_async_copy(
                exps_in.at[head, pl.ds(low * part, part)],
                exps_ref.at[head, pl.ds(low * part, part)],
                load_sems.at[head, low],
            )
            for low in range(LOADS)
        ]
        for head in range(HEADS)
    ]
    load_packed = pltpu.make_async_copy(packed_in, packed_ref, sems.at[0])
    load_attended = pltpu.make_async_copy(attended_in, attended_ref, sems.at[1])
    load_normed = pltpu.make_async_copy(normed_in, normed_ref, sems.at[HEADS])
    copy_time = pltpu.make_async_copy(time_in, pieces_ref.at[:, 0:1], sems.at[HEADS + 1])
    store_packed = pltpu.make_async_copy(grad_packed_ref, grad_packed_out, sems.at[HEADS + 2])
    store_pieces = pltpu.make_async_copy(pieces_ref, pieces_out, sems.at[HEADS + 3])
    load_packed.start()
    load_attended.start()
    for load in loads[0]:
        load.start()

    new = grad_ref[...].reshape(tokens, features)
    grad_attended_ref[...] = dot(w_out_ref[...], new, 1, 1).astype(BF16)
    load_packed.wait()
    load_attended.wait()
    for load in loads[0]:
        load.wait()
    for load in loads[1] + loads[2] + loads[3]:
        load.start()
    load_normed.start()
    copy_time.start()
    blocks = [slice(start, start + SPACE_BLOCK) for start in range(0, tokens, SPACE_BLOCK)]

    def finish(head, grad):
        at = head * depth
        keys = packed_ref[features + at : features + at + depth, :]
        query = packed_ref[at : at + depth, :]
        scores = grad_scores_ref[head % 2]
        grad_packed_ref[at : at + depth, :] = (dot(keys, scores, 1, 0) * depth**-0.5).astype(BF16)
        grad_packed_ref[features + at : features + at + depth, :] = (
            dot(scores, query.T, 1, 0).T * math.log(2.0)
        ).astype(BF16)
        grad_packed_ref[2 * features + at : 2 * features + at + depth, :] = dot(
            exps_ref[head], grad.T, 1, 0
        ).T.astype(BF16)

    before = None
    for head in range(HEADS):
        at = head * depth
        values = packed_ref[2 * features + at : 2 * features + at + depth, :]
        grad = grad_attended_ref[at : at + depth, :].astype(F32) * total_ref[head]
        inner = jnp.sum(
            grad * attended_ref[at : at + depth, :].astype(F32), axis=0, keepdims=True
        )
        grad = grad.astype(BF16)
        wide_grad = jnp.concatenate([grad, split_rows(inner)])
        wide_values = jnp.concatenate([values.T, jnp.full((tokens, 16), -1.0, BF16)], axis=1)
        if head > 0:
            for load in loads[head]:
                load.wait()
        for cols in blocks:
            for low in range(0, tokens, KEY_TILE):
                rows = slice(low, low + KEY_TILE)
                centred = dot(wide_values[rows], wide_grad[:, cols], 1, 0)
                grad_scores_ref[head % 2, rows, cols] = (
                    exps_ref[head, rows, cols].astype(F32) * centred
                ).astype(BF16)
        finish(head, grad)
    store_packed.start()
    load_normed.wait()
    store_blocks(
        pieces_ref,
        1,
        dot(normed_ref[...], grad_packed_ref[...], 1, 1),
        dot(attended_ref[...], new, 1, 0),
    )
    copy_time.wait()
    store_pieces.start()
    store_packed.wait()
    store_pieces.wait()


def run_space_backward(grad, normed, packed, attended, exps, totals, w_out, time_pieces):
    features, tokens = attended.shape
    parts, _, rows, _ = time_pieces.shape
    packed, attended, normed, exps, time_pieces = in_hbm(
        packed, attended, normed, exps, time_pieces
    )
    shapes = [pltpu.HBM((3 * features, tokens), BF16), ((parts, 2, rows, features), BF16)]
    return call(
        space_backward,
        shapes,
        (grad, totals, w_out, packed, attended, normed, exps, time_pieces),
        14,
        scratch=[
            ((features, tokens), BF16),
            ((3 * features, tokens), BF16),
            ((parts, 2, rows, features), BF16),
            ((3 * features, tokens), BF16),
            ((features, tokens), BF16),
            ((features, tokens), BF16),
            ((HEADS, tokens, tokens), BF16),
            ((2, tokens, tokens), BF16),
            pltpu.SemaphoreType.DMA((HEADS + 4,)),
            pltpu.SemaphoreType.DMA((HEADS, LOADS)),
        ],
        megabytes=32,
        in_specs=[VMEM] * 3 + [ANY] * 5,
        out_specs=[ANY] * 2,
    )


def space_stream(
    me_ref, grad_ref, x_ref, inverse_ref, grad_packed_ref, gain_ref, w_qkv_ref, *rest
):
    out_refs, rows_ref = rest[:-1], rest[-1]
    features, tokens = x_ref.shape
    grad_normed = dot(w_qkv_ref[...], grad_packed_ref[...], 1, 0)
    grad_stream = norm_columns_backward(
        x_ref[...].astype(F32), as_column(gain_ref[...]), inverse_ref[...], grad_normed
    )
    grad_new = grad_ref[...].reshape(tokens, features).astype(F32)
    rows_ref[...] = (grad_new + grad_stream.T).astype(BF16)
    rows = tokens // len(out_refs)
    for step, out_ref in enumerate(out_refs):
        at = pl.multiple_of((me_ref[0] ^ step) * rows, rows)
        out_ref[...] = rows_ref[pl.ds(at, rows), :]


SMEM = pl.BlockSpec(memory_space=pltpu.SMEM)


def run_space_stream(me, grad, x, inverse, grad_packed, gain, w_qkv, parts):
    features, tokens = x.shape
    return call(
        space_stream,
        [((tokens // parts, features), BF16)] * parts,
        (me, grad, x, inverse, grad_packed, gain, w_qkv),
        4,
        scratch=[((tokens, features), BF16)],
        in_specs=[SMEM] + [VMEM] * 6,
        out_specs=[VMEM] * parts,
    )


def place_blocks(me_ref, *refs):
    in_refs, out_ref = refs[:-1], refs[-1]
    for step, in_ref in enumerate(in_refs):
        out_ref[me_ref[0] ^ step] = in_ref[...]


def unpack(pieces_ref, space_qkv_ref, space_out_ref, time_qkv_ref, time_out_ref):
    features = space_out_ref.shape[0]
    count = pieces_ref.shape[0] // 4
    for j in range(4):
        pieces = pieces_ref[j * count : (j + 1) * count].astype(F32)
        for kind, qkv_ref, out_ref in (
            (0, time_qkv_ref, time_out_ref),
            (1, space_qkv_ref, space_out_ref),
        ):
            block = pieces[:, kind].reshape(features, features)
            if j < 3:
                qkv_ref[:, j * features : (j + 1) * features] = block
            else:
                out_ref[...] = block


def exchange(values, axes):
    return lax.all_to_all(values, axes, split_axis=0, concat_axis=0, tiled=True)


def to_pair(block, step, parts):
    return lax.ppermute(block, "stab", [(i, i ^ step) for i in range(parts)])


def on_device(
    syndrome,
    basis_ids,
    coordinates,
    syndrome_table,
    basis_table,
    coord_table,
    round_table,
    gain_space,
    w_qkv_space,
    w_out_space,
    gain_time,
    w_qkv_time,
    w_out_time,
    grad_hidden,
):
    stab_parts = lax.axis_size("stab")
    round_parts = lax.axis_size("rounds")
    parts = stab_parts * round_parts
    rounds_here, stabs_here, features = grad_hidden.shape
    stabs_time = stabs_here // round_parts

    own_index = call(
        index_kernel,
        [((stab_parts, 5, stabs_here), jnp.int32)],
        (syndrome, basis_ids.reshape(1, stabs_here), coordinates),
        1,
    )[0]
    index = exchange(own_index, "stab")
    grad_chunks = grad_hidden.reshape(rounds_here, round_parts, stabs_time, features)
    grad_chunks, index = lax.optimization_barrier((jnp.swapaxes(grad_chunks, 0, 1), index))
    grad_time = exchange(grad_chunks, "rounds")

    gain_s = gain_space.reshape(1, features)
    gain_t = gain_time.reshape(1, features)
    tables = (syndrome_table, basis_table, coord_table, round_table)
    middle, x, normed, inverse, packed, attended, exps, totals = run_space_forward(
        index, tables, gain_s, w_qkv_space, w_out_space, parts
    )
    middle, grad_time = lax.optimization_barrier((middle, grad_time))
    middle_time = exchange(middle, ("stab", "rounds"))
    middle_time = middle_time.reshape(stab_parts, round_parts, stabs_time, features)
    grad_rows, grad_attended_t = run_time_grad(grad_time, w_out_time)
    grad_middle, normed_t, grad_packed_t, attended_t = run_time_block(
        middle_time, grad_time, grad_attended_t, gain_t, w_qkv_time
    )
    grad_space = exchange(grad_middle.reshape(parts, stabs_time, features), ("stab", "rounds"))
    hidden, time_pieces = run_time_rest(
        middle_time, normed_t, grad_packed_t, attended_t, grad_rows, w_out_time
    )
    hidden, grad_space = lax.optimization_barrier((hidden, grad_space))
    hidden_home = exchange(hidden, "rounds")
    grad_packed, pieces = run_space_backward(
        grad_space, normed, packed, attended, exps, totals, w_out_space, time_pieces
    )
    pieces, grad_packed, hidden_home = lax.optimization_barrier((pieces, grad_packed, hidden_home))
    sources = exchange(pieces, ("rounds", "stab"))
    me = lax.axis_index("stab").astype(jnp.int32).reshape(1)
    blocks = list(
        run_space_stream(
            me, grad_space, x, inverse, grad_packed, gain_s, w_qkv_space, stab_parts
        )
    )
    near = [step for step in range(1, stab_parts) if step % 4 == 2]
    for step in sorted(set(range(1, stab_parts)) - set(near)):
        blocks[step] = to_pair(blocks[step], step, stab_parts)
    sources, *blocks = lax.optimization_barrier((sources, *blocks))
    blocks = list(blocks)
    for step in near:
        blocks[step] = to_pair(blocks[step], step, stab_parts)
    scaling = 1.0 / math.sqrt(parts * rounds_here * stabs_here)
    summed = (jnp.sum(sources.astype(F32), axis=0) * scaling).astype(BF16)
    gathered = exchange(
        jnp.broadcast_to(summed[None], (parts,) + summed.shape), ("rounds", "stab")
    )
    hidden_home = jnp.swapaxes(hidden_home, 0, 1).reshape(grad_hidden.shape)
    weights = call(
        unpack,
        [((features, 3 * features), F32), ((features, features), F32)] * 2,
        (gathered,),
        2,
        megabytes=20,
    )
    grad_embedded = call(
        place_blocks,
        [(grad_hidden.shape, BF16)],
        (me, *blocks),
        2,
        in_specs=[SMEM] + [VMEM] * stab_parts,
        out_specs=[VMEM],
    )[0]
    return (hidden_home, grad_embedded) + tuple(weights)


def solution(mesh):
    in_specs = (
        P("rounds", "stab"),
        P("stab"),
        P(None, "stab"),
        P(),
        P(),
        P(),
        P("rounds", None),
        P(),
        P(),
        P(),
        P(),
        P(),
        P(),
        P("rounds", "stab", None),
    )
    out_specs = (P("rounds", "stab", None), P("rounds", "stab", None), P(), P(), P(), P())
    return jax.shard_map(
        on_device, mesh=mesh, in_specs=in_specs, out_specs=out_specs, check_vma=False
    )
```
